32 devices in a mesh: dp: 8 (over z, y), seq: 4 (over x, core).
Axes of the slice: x: 2, y: 2, z: 4, core: 2. Of those that a mesh axis runs over, the one named last changes fastest.
Arguments:
- hidden_in: bfloat16 [1024, 24, 256], P('seq', 'dp'), may hold values from -6 to 6
- embedding: bfloat16 [1024, 24, 256], P('seq', 'dp'), may hold values from -6 to 6
- lengths: int32 [24], P('dp'), may hold values from 128 to 1024, as said below
- cotangent: bfloat16 [1024, 24, 256], P('seq', 'dp'), may hold values from -6 to 6
- ln1_gain: float32 [256], replicated, may hold values from 0.1 to 1.9
- ln1_bias: float32 [256], replicated, may hold values from -1.75 to 1.75
- qkv_weight: bfloat16 [256, 768], replicated, may hold values from -0.5 to 0.5
- qv_bias: float32 [2, 256], replicated, may hold values from -1.75 to 1.75
- out_weight: bfloat16 [256, 256], replicated, may hold values from -4 to 4
- out_bias: float32 [256], replicated, may hold values from -1.75 to 1.75
- ln2_gain: float32 [256], replicated, may hold values from 0.1 to 1.9
- ln2_bias: float32 [256], replicated, may hold values from -1.75 to 1.75
- up_weight: bfloat16 [256, 1024], replicated, may hold values from -0.375 to 0.375
- up_bias: float32 [1024], replicated, may hold values from -1.75 to 1.75
- down_weight: bfloat16 [1024, 256], replicated, may hold values from -0.1875 to 0.1875
- down_bias: float32 [256], replicated, may hold values from -1.75 to 1.75
Outputs:
- output: bfloat16 [1024, 24, 256], P('seq', 'dp')
- grad_hidden: float32 [1024, 24, 256], P('seq', 'dp')
- grad_embed: float32 [1024, 24, 256], P('seq', 'dp')
- grad_ln1_gain: float32 [256], replicated
- grad_ln1_bias: float32 [256], replicated
- grad_qkv_weight: float32 [256, 768], replicated
- grad_qv_bias: float32 [2, 256], replicated
- grad_out_weight: float32 [256, 256], replicated
- grad_out_bias: float32 [256], replicated
- grad_ln2_gain: float32 [256], replicated
- grad_ln2_bias: float32 [256], replicated
- grad_up_weight: float32 [256, 1024], replicated
- grad_up_bias: float32 [1024], replicated
- grad_down_weight: float32 [1024, 256], replicated
- grad_down_bias: float32 [256], replicated
The draws below stay inside these ranges and needn't reach their ends.
Inputs may be any that keep to these rules, and one draw needn't show every extreme that they name: `lengths`: among each dp index's 3 rows (aligned blocks of 3), one row, drawn from the seed, has length 1024; positions at or past a row's length are padding keys.
All inputs are finite; a program needn't handle non-finite values.
Results may differ from the reference program's by a relative error of at most 0.022.
The reference program's roundings to bfloat16 on the way count: a program that leaves them out, or rounds other values in their place, can miss the bound.
Values may be sent and summed in bfloat16 or wider, within the bound.
A program may use at most 128 MiB of HBM per device.

```python
import math
import jax
import jax.numpy as jnp
from jax import lax

D = 256
HEADS = 4
FF = 1024
LEN = 1024
ROWS = 3
HEAD_DIM = 64
BATCH = 24


def draw_lengths(key, part):
    key = jax.random.fold_in(key, 11)
    first_key, second_key = jax.random.split(key)
    base = jax.random.randint(first_key, (BATCH,), LEN // 8, LEN + 1)
    picked = jax.random.randint(second_key, (BATCH // ROWS,), 0, ROWS)
    chosen = jnp.arange(BATCH) % ROWS == jnp.repeat(picked, ROWS, total_repeat_length=BATCH)
    return jnp.where(chosen, LEN, base).astype(jnp.int32)


def shard_levels(own_key, extent, pieces, low, high):
    factor_of = 1.0
    for position, parts in pieces:
        draws = jax.random.uniform(jax.random.fold_in(jax.random.fold_in(own_key, 6), position), (parts,), jnp.float32, low / len(pieces), high / len(pieces))
        factor_of = factor_of * jnp.repeat(jnp.exp(draws), extent[position] // parts).reshape((-1,) + (1,) * (len(extent) - 1 - position))
    return factor_of


def normal_values(stream_key, shape, deviation, most, cuts=(), kind=jnp.bfloat16):
    drawn = deviation * jax.random.normal(stream_key, shape, jnp.float32)
    if cuts:
        drawn = drawn * shard_levels(stream_key, shape, cuts, -0.22, 0.18)
    return jnp.clip(drawn, -most, most).astype(kind)


def setup_inputs(seed: int = 0) -> dict:
    keys = jax.random.split(jax.random.key(seed), 17)
    hidden_in = normal_values(keys[0], (LEN, BATCH, D), 1.0, 6.0, ((0, 4), (1, 8)))
    embedding = normal_values(keys[1], (LEN, BATCH, D), 1.0, 6.0, ((0, 4), (1, 8)))
    lengths = draw_lengths(jax.random.fold_in(keys[16], 71), 0)
    cotangent = normal_values(keys[3], (LEN, BATCH, D), 1.0, 6.0, ((0, 4), (1, 8)))
    ln1_gain = jnp.clip(1.0 + 0.18 * jax.random.normal(keys[4], (D,), jnp.float32), 0.1, 1.9)
    ln1_bias = normal_values(keys[5], (D,), 0.3, 1.75, (), jnp.float32)
    qkv_weight = normal_values(keys[6], (D, 3 * D), (D // 2) ** -0.5, 0.5)
    qv_bias = normal_values(keys[7], (2, D), 0.3, 1.75, (), jnp.float32)
    out_weight = normal_values(keys[8], (D, D), (max(1, D // 128)) ** -0.5, 4.0)
    out_bias = normal_values(keys[9], (D,), 0.3, 1.75, (), jnp.float32)
    ln2_gain = jnp.clip(1.0 + 0.18 * jax.random.normal(keys[10], (D,), jnp.float32), 0.1, 1.9)
    ln2_bias = normal_values(keys[11], (D,), 0.3, 1.75, (), jnp.float32)
    up_weight = normal_values(keys[12], (D, FF), D ** -0.5, 0.375)
    up_bias = normal_values(keys[13], (FF,), 0.3, 1.75, (), jnp.float32)
    down_weight = normal_values(keys[14], (FF, D), FF ** -0.5, 0.1875)
    down_bias = normal_values(keys[15], (D,), 0.3, 1.75, (), jnp.float32)
    return {"hidden_in": hidden_in, "embedding": embedding, "lengths": lengths, "cotangent": cotangent, "ln1_gain": ln1_gain, "ln1_bias": ln1_bias, "qkv_weight": qkv_weight, "qv_bias": qv_bias, "out_weight": out_weight, "out_bias": out_bias, "ln2_gain": ln2_gain, "ln2_bias": ln2_bias, "up_weight": up_weight, "up_bias": up_bias, "down_weight": down_weight, "down_bias": down_bias}


EPS = 1e-05
MASKED = -1e+30
HIGH = lax.Precision.HIGHEST

@jax.custom_vjp
def low(v):
    return lax.optimization_barrier(v.astype(jnp.bfloat16)).astype(jnp.float32)

@jax.custom_vjp
def low_back(v):
    return v

def low_keep(v):
    return (low(v), None)

def low_pass(kept, grad):
    return (grad,)

def back_keep(v):
    return (v, None)

def back_low(kept, grad):
    return (low(grad),)
low.defvjp(low_keep, low_pass)
low_back.defvjp(back_keep, back_low)

def layer_norm(stream, gain, bias):
    mean_value = lax.optimization_barrier(jnp.mean(stream, axis=-1, keepdims=True))
    centred = stream - mean_value
    variance = lax.optimization_barrier(jnp.mean(centred * centred, axis=-1, keepdims=True))
    return centred * lax.rsqrt(variance + EPS) * gain + bias

def project(inputs, weight):
    return jnp.dot(inputs, weight, precision=HIGH)

def attend_group(group_data):
    query_rows, key_rows, value_rows, group_lengths = group_data
    rows_in = query_rows.shape[0]
    heads_q = query_rows.reshape(rows_in, LEN, HEADS, HEAD_DIM)
    heads_k = key_rows.reshape(rows_in, LEN, HEADS, HEAD_DIM)
    heads_v = value_rows.reshape(rows_in, LEN, HEADS, HEAD_DIM)
    raw = jnp.einsum('gqhd,gkhd->ghqk', heads_q, heads_k, precision=HIGH) * HEAD_DIM ** (-0.5)
    raw = low_back(raw)
    positions = jnp.arange(LEN, dtype=jnp.int32)
    allowed = (positions[None, None, None, :] <= positions[None, None, :, None]) & (positions[None, None, None, :] < group_lengths[:, None, None, None])
    scores = jnp.where(allowed, raw, MASKED)
    attn_probs = low(jax.nn.softmax(scores, axis=-1))
    result = jnp.einsum('ghqk,gkhd->gqhd', attn_probs, heads_v, precision=HIGH)
    return result.reshape(rows_in, LEN, D)

def attention(query_rows, key_rows, value_rows, lengths):
    group = math.gcd(BATCH, max(1, 4096 // LEN))

    def regroup(rows):
        return jnp.transpose(rows, (1, 0, 2)).reshape(BATCH // group, group, LEN, D)
    results = lax.map(jax.checkpoint(attend_group), (regroup(query_rows), regroup(key_rows), regroup(value_rows), lengths.reshape(BATCH // group, group)))
    return jnp.transpose(results.reshape(BATCH, LEN, D), (1, 0, 2))

def block(stream, lengths, params):
    ln1_gain, ln1_bias, qkv_weight, qv_bias, out_weight, out_bias, ln2_gain, ln2_bias, up_weight, up_bias, down_weight, down_bias = params
    normed = low(layer_norm(stream, ln1_gain, ln1_bias))
    qkv_bias = jnp.concatenate([qv_bias[0], jnp.zeros_like(qv_bias[0]), qv_bias[1]])
    qkv_rows = low_back(low(project(normed, qkv_weight) + qkv_bias))
    attended = attention(qkv_rows[:, :, :D], qkv_rows[:, :, D:2 * D], qkv_rows[:, :, 2 * D:], lengths)
    attended = low_back(low(attended))
    middle = stream + low_back(project(attended, out_weight) + out_bias)
    normed2 = low(layer_norm(middle, ln2_gain, ln2_bias))
    pre_act = low_back(project(normed2, up_weight) + up_bias)
    hidden = low(jax.nn.gelu(pre_act))
    return middle + low_back(project(hidden, down_weight) + down_bias)

def reference(hidden_in, embedding, lengths, cotangent, ln1_gain, ln1_bias, qkv_weight, qv_bias, out_weight, out_bias, ln2_gain, ln2_bias, up_weight, up_bias, down_weight, down_bias):
    params = tuple((item.astype(jnp.float32) for item in (ln1_gain, ln1_bias, qkv_weight, qv_bias, out_weight, out_bias, ln2_gain, ln2_bias, up_weight, up_bias, down_weight, down_bias)))

    def forward(start, embed_rows, weights):
        first = block(start + embed_rows, lengths, weights)
        return block(first + embed_rows, lengths, weights)
    output, pullback = jax.vjp(forward, hidden_in.astype(jnp.float32), embedding.astype(jnp.float32), params)
    grad_hidden, grad_embed, grad_params = pullback(cotangent.astype(jnp.float32))
    return (output.astype(jnp.bfloat16), grad_hidden, grad_embed, grad_params[0], grad_params[1], grad_params[2], grad_params[3], grad_params[4], grad_params[5], grad_params[6], grad_params[7], grad_params[8], grad_params[9], grad_params[10], grad_params[11])
```

```python
import functools

import jax
import jax.numpy as jnp
from jax import lax
from jax.experimental import pallas as pl
from jax.experimental.pallas import tpu as pltpu
from jax.sharding import PartitionSpec as P

EPS = 1e-05
MASKED = -1e30
HEADS = 4
BF = jnp.bfloat16
F32 = jnp.float32
MESH = pl.DeviceIdType.MESH


def nn(a, b):
    return lax.dot_general(a, b, (((1,), (0,)), ((), ())), preferred_element_type=F32)


def nt(a, b):
    return lax.dot_general(a, b, (((1,), (1,)), ((), ())), preferred_element_type=F32)


def normalise(x):
    mean = jnp.mean(x, axis=-1, keepdims=True)
    centred = x - mean
    rstd = lax.rsqrt(jnp.mean(centred * centred, axis=-1, keepdims=True) + EPS)
    return centred * rstd, rstd


def norm_back(grad, gain, xhat, rstd):
    gl = grad * gain
    m1 = jnp.mean(gl, axis=-1, keepdims=True)
    m2 = jnp.mean(gl * xhat, axis=-1, keepdims=True)
    return rstd * (gl - m1 - xhat * m2)


def fold(x):
    return jnp.sum(x.reshape(x.shape[0] // 8, 8, x.shape[1]), axis=0)


def gelu_parts(x):
    c0 = 0.7978845608028654
    x2 = x * x
    t = jnp.tanh(c0 * (x + 0.044715 * (x2 * x)))
    half = 0.5 * (1.0 + t)
    slope = half + (0.5 * x) * (1.0 - t * t) * (c0 * (1.0 + (3 * 0.044715) * x2))
    return x * half, slope


HD = 64


def head_rows(x, h):
    own = x[h * HD:(h + 1) * HD]
    zero = jnp.zeros_like(own)
    return jnp.concatenate([own, zero] if h % 2 == 0 else [zero, own], axis=0)


def pair(h):
    return slice((h // 2) * 2 * HD, (h // 2 + 1) * 2 * HD)


def block_kernel(cfg, *refs):
    S, DP, R, L, D, FF, reduce_here = cfg
    W = 3 * D + D + 2 * FF
    UP, DN, OW, QW = 0, FF, 2 * FF, 2 * FF + D
    (hid_ref, emb_ref, cot_ref, len_ref, ln1g_ref, ln1b_ref, wqkv_ref, qvb_ref, wout_ref, bout_ref, ln2g_ref, ln2b_ref,
     wup_ref, bup_ref, wdn_ref, bdn_ref,
     y_ref, g1_ref, ge_ref, gw_ref, gv_ref,
     wT, bcol, stream, gstream, gmid, nall, xh1, rs1, xh2, rs2, n2T, qT_s, qn_s, linv, oT_s, hid_s, slope_s,
     e_scr, pg_out, pg_in, vec, *comm) = refs
    nsend, nrecv, psend, precv, out_sem = comm[:5]
    me = lax.axis_index("seq")
    dp = lax.axis_index("dp")
    mine = pl.ds(pl.multiple_of(me * L, L), L)

    def at(s):
        return (dp, s)

    barrier = pltpu.get_barrier_semaphore()
    for k in range(1, S):
        pl.semaphore_signal(barrier, inc=1, device_id=(dp, lax.rem(me + k, S)), device_id_type=MESH)
    peers = S - 1
    if reduce_here:
        for k in range(1, DP):
            pl.semaphore_signal(barrier, inc=1, device_id=(lax.rem(dp + k, DP), me), device_id_type=MESH)
        peers += DP - 1
    pl.semaphore_wait(barrier, peers)

    ln1g, ln1b = ln1g_ref[...], ln1b_ref[...]
    ln2g, ln2b = ln2g_ref[...], ln2b_ref[...]

    def normed_copy(a, r, src, dst):
        rows = pl.ds(pl.multiple_of(src * L, L), L)
        return pltpu.make_async_remote_copy(
            src_ref=nall.at[a, r, rows], dst_ref=nall.at[a, r, rows], send_sem=nsend.at[a, r, dst],
            recv_sem=nrecv.at[a, r, src], device_id=at(dst), device_id_type=MESH)

    def part_copy(a, r, src, dst):
        return pltpu.make_async_remote_copy(
            src_ref=pg_out.at[a, r, dst], dst_ref=pg_in.at[a, r, src - 1], send_sem=psend.at[a, r, dst],
            recv_sem=precv.at[a, r, src], device_id=at(dst), device_id_type=MESH)

    def first_norm(a, r):
        u = stream[r] + emb_ref[r].astype(F32)
        stream[r] = u
        xhat, rstd = normalise(u)
        xh1[a, r] = xhat
        rs1[a, r] = jnp.broadcast_to(rstd, (L, 128))
        nall[a, r, mine] = (xhat * ln1g + ln1b).astype(BF)

        @pl.loop(me + 1, S)
        def _(dst):
            normed_copy(a, r, me, dst).start()

    @pl.loop(0, R)
    def _(r):
        stream[r] = hid_ref[r].astype(F32)
        first_norm(0, r)

    for k in range(3):
        wT[k] = wqkv_ref[:, k * D:(k + 1) * D].T
    for k in range(2):
        bcol[k] = jnp.broadcast_to(qvb_ref[k:k + 1, :], (128, D)).T
    bq = jnp.concatenate([bcol[0]] * (L // 128), axis=1)
    bv = jnp.concatenate([bcol[1]] * (L // 128), axis=1)

    vec[...] = jnp.zeros_like(vec)

    def forward(a, r, VT, s_scr, m_scr, l_scr, oacc):
        normed = nall[a, r, mine]
        qT = ((nt(wT[0], normed) + bq) * (HD ** -0.5)).astype(BF)
        qn_s[a, r] = qT.T
        qT_s[...] = qT
        m_scr[...] = jnp.full_like(m_scr, MASKED)
        l_scr[...] = jnp.zeros_like(l_scr)
        oacc[...] = jnp.zeros_like(oacc)
        length = len_ref[r]

        @pl.loop(0, me + 1)
        def _(t):
            @pl.when(t < me)
            def _():
                normed_copy(a, r, t, me).wait_recv()

            rows = nall[a, r, pl.ds(pl.multiple_of(t * L, L), L)]
            keys = nn(rows, wqkv_ref[:, D:2 * D]).astype(BF)
            VT[t] = (nt(wT[2], rows) + bv).astype(BF)
            key_pos = t * L + lax.broadcasted_iota(jnp.int32, (L, L), 0)
            query_pos = me * L + lax.broadcasted_iota(jnp.int32, (L, L), 1)
            bias = jnp.where((key_pos <= query_pos) & (key_pos < length), 0.0, MASKED)
            for h in range(HEADS):
                s = nn(keys[:, pair(h)], head_rows(qT_s[...], h)) + bias
                s_scr[t, h] = s
                m_scr[h] = jnp.maximum(m_scr[h], jnp.max(s.reshape(L // 8, 8, L), axis=0))

        for h in range(HEADS):
            m_scr[h] = jnp.broadcast_to(jnp.max(m_scr[h], axis=0, keepdims=True), (8, L))

        @pl.loop(0, me + 1)
        def _(t):
            for h in range(HEADS):
                e = jnp.exp(s_scr[t, h] - m_scr[h, 0:1])
                l_scr[h] += fold(e)
                low = e.astype(BF)
                e_scr[a, r, t, h] = low
                oacc[h * HD:(h + 1) * HD] += nn(VT[t, h * HD:(h + 1) * HD, :], low)

        heads = []
        for h in range(HEADS):
            inv = 1.0 / jnp.sum(l_scr[h], axis=0, keepdims=True)
            linv[a, r, h] = jnp.broadcast_to(inv, (8, L))
            heads.append(oacc[h * HD:(h + 1) * HD] * inv)
        oT = jnp.concatenate(heads, axis=0).astype(BF)
        oT_s[a, r] = oT
        middle = stream[r] + (nn(oT.T, wout_ref[...]) + bout_ref[...])
        xhat, rstd = normalise(middle)
        xh2[a, r] = xhat
        rs2[a, r] = jnp.broadcast_to(rstd, (L, 128))
        normed2 = (xhat * ln2g + ln2b).astype(BF)
        n2T[a, r] = normed2.T
        hidden, slope = gelu_parts(nn(normed2, wup_ref[...]) + bup_ref[...])
        hidden = hidden.astype(BF)
        hid_s[a, r] = hidden
        slope_s[a, r] = slope
        stream[r] = middle + (nn(hidden, wdn_ref[...]) + bdn_ref[...])

    def forward_all(*scr):
        @pl.loop(0, 2 * R)
        def _(n):
            a, r = lax.div(n, R), lax.rem(n, R)
            forward(a, r, *scr)

            @pl.when(a == 0)
            def _():
                first_norm(1, r)

            @pl.when(a == 1)
            def _():
                y_ref[r] = stream[r].astype(BF)
                gstream[r] = cot_ref[r].astype(F32)

    VM = pltpu.VMEM
    pl.run_scoped(forward_all, VM((S, D, L), BF), VM((S, HEADS, L, L), F32), VM((HEADS, 8, L), F32), VM((HEADS, 8, L), F32),
                  VM((D, L), F32))
    pl.run_scoped(functools.partial(backward_kernel, cfg, refs, me, dp, mine, normed_copy, part_copy),
                  VM((D, L), F32), VM((R, D, L), BF), VM((R, L, FF), BF), VM((R, L, D), BF), VM((R, L, 3 * D), BF),
                  VM((D, W), F32))


def backward_kernel(cfg, refs, me, dp, mine, normed_copy, part_copy, gqacc, gbT, gpre, ga_s, gqkv, dW):
    S, DP, R, L, D, FF, reduce_here = cfg
    W = 3 * D + D + 2 * FF
    UP, DN, OW, QW = 0, FF, 2 * FF, 2 * FF + D
    (hid_ref, emb_ref, cot_ref, len_ref, ln1g_ref, ln1b_ref, wqkv_ref, qvb_ref, wout_ref, bout_ref, ln2g_ref, ln2b_ref,
     wup_ref, bup_ref, wdn_ref, bdn_ref,
     y_ref, g1_ref, ge_ref, gw_ref, gv_ref,
     wT, bcol, stream, gstream, gmid, nall, xh1, rs1, xh2, rs2, n2T, qT_s, qn_s, linv, oT_s, hid_s, slope_s,
     e_scr, pg_out, pg_in, vec, *comm) = refs
    nsend, nrecv, psend, precv, out_sem = comm[:5]
    ln1g, ln2g = ln1g_ref[...], ln2g_ref[...]

    def add_vec(start, terms):
        vec[:, start:start + terms.shape[1]] += fold(terms)

    V_LN1G, V_LN1B, V_QB, V_VB, V_OB, V_LN2G, V_LN2B, V_DB, V_UB = [D * k for k in range(9)]

    lane = lax.broadcasted_iota(jnp.int32, (L, 2 * HD), 1)

    def head_lanes(x, h):
        keep = (lane < HD) if h % 2 == 0 else (lane >= HD)
        return jnp.where(keep, x[:, pair(h)], jnp.zeros((), x.dtype))

    def backward_mlp(a, r):
        g = gstream[r]
        gb = g.astype(BF)
        add_vec(V_DB, gb.astype(F32))
        gbT[r] = gb.T
        pre = (nt(gb, wdn_ref[...]) * slope_s[a, r]).astype(BF)
        gpre[r] = pre
        add_vec(V_UB, pre.astype(F32))
        gn2 = nt(pre, wup_ref[...])
        xhat = xh2[a, r]
        add_vec(V_LN2G, gn2 * xhat)
        add_vec(V_LN2B, gn2)
        rstd = jnp.concatenate([rs2[a, r]] * (D // 128), axis=1)
        gm = g + norm_back(gn2, ln2g, xhat, rstd)
        gmid[r] = gm
        ga = gm.astype(BF)
        ga_s[r] = ga
        add_vec(V_OB, ga.astype(F32))

    def backward_attention(a, r):
        gaT = nt(wout_ref[...], ga_s[r]).astype(BF).astype(F32)
        oT = oT_s[a, r].astype(F32)
        scaled, deltas = [], []
        for h in range(HEADS):
            hs = slice(h * HD, (h + 1) * HD)
            inv = linv[a, r, h, 0:1]
            part = gaT[hs] * inv
            scaled.append(part.astype(BF))
            deltas.append(jnp.sum(part * oT[hs], axis=0, keepdims=True))
        gaT_n = jnp.concatenate(scaled, axis=0)
        ga_n = gaT_n.T
        queries = qn_s[a, r]
        gqacc[...] = jnp.zeros_like(gqacc)

        @pl.loop(0, me + 1)
        def _(t):
            rows = nall[a, r, pl.ds(pl.multiple_of(t * L, L), L)]
            values = (nn(rows, wqkv_ref[:, 2 * D:]) + qvb_ref[1:2, :]).astype(BF)
            KT = nt(wT[1], rows).astype(BF)
            gk, gv = [], []
            for h in range(HEADS):
                hs = slice(h * HD, (h + 1) * HD)
                gp = nn(values[:, pair(h)], head_rows(gaT_n, h))
                low = e_scr[a, r, t, h]
                ds = (low.astype(F32) * (gp - deltas[h])).astype(BF)
                gk.append(nn(ds, head_lanes(queries, h)))
                gv.append(nn(low, head_lanes(ga_n, h)))
                gqacc[hs] += nn(KT[hs], ds)
            gkv = jnp.concatenate([gk[0] + gk[1], gk[2] + gk[3], gv[0] + gv[1], gv[2] + gv[3]], axis=1).astype(BF)
            add_vec(V_VB, gkv[:, D:].astype(F32))
            dW[:, QW + D:QW + 3 * D] += nn(rows.T, gkv)

            @pl.when(t < me)
            def _():
                pg_out[a, r, t] = nt(gkv, wqkv_ref[:, D:]).astype(BF)
                part_copy(a, r, me, t).start()

            @pl.when(t == me)
            def _():
                gqkv[r, :, D:] = gkv

        gq = (gqacc[...] * (HD ** -0.5)).T.astype(BF)
        gqkv[r, :, :D] = gq
        add_vec(V_QB, gq.astype(F32))

    def backward_norm(a, r):
        gn = nt(gqkv[r], wqkv_ref[...])
        gmid_r = gmid[r]

        def add(s, total):
            part_copy(a, r, s, me).wait_recv()
            return total + pg_in[a, r, s - 1].astype(F32)

        gn = lax.fori_loop(me + 1, S, add, gn)
        xhat = xh1[a, r]
        add_vec(V_LN1G, gn * xhat)
        add_vec(V_LN1B, gn)
        rstd = jnp.concatenate([rs1[a, r]] * (D // 128), axis=1)
        gstream[r] = gmid_r + norm_back(gn, ln1g, xhat, rstd)

    def weight_terms(a, first):
        def put(start, value):
            if first:
                dW[:, start:start + value.shape[1]] = value
            else:
                dW[:, start:start + value.shape[1]] += value

        put(UP, sum(nn(n2T[a, r], gpre[r]) for r in range(R)))
        put(DN, sum(nn(gbT[r], hid_s[a, r]) for r in range(R)))
        put(OW, sum(nn(oT_s[a, r], ga_s[r]) for r in range(R)))

    def query_terms(a, first):
        value = sum(nn(nall[a, r, mine].T, gqkv[r, :, :D]) for r in range(R))
        if first:
            dW[:, QW:QW + D] = value
        else:
            dW[:, QW:QW + D] += value

    dW[:, QW + D:QW + 3 * D] = jnp.zeros((D, 2 * D), F32)
    for a in (1, 0):
        @pl.loop(0, R)
        def _(r):
            backward_mlp(a, r)

        weight_terms(a, a == 1)

        @pl.loop(0, R)
        def _(r):
            backward_attention(a, r)

        query_terms(a, a == 1)

        @pl.loop(0, R)
        def _(r):
            backward_norm(a, r)
            if a == 1:
                g1_ref[r] = gstream[r]
            else:
                g = gstream[r]
                ge_ref[r] = g + g1_ref[r]
                g1_ref[r] = g

    sums = jnp.sum(vec[...], axis=0, keepdims=True)
    if reduce_here:
        stage, seq_in, mid, dp_in, gath, vs, vs_seq, vs_dp, ss, sr, ds_, dr, gs, gr, fs, fr, vss, vsr, vds, vdr = comm[5:]
        rows = D // S
        groups = min(DP, rows // 16)
        lanes = W // (DP // groups)
        crow = rows // groups
        stage[...] = dW[...].astype(BF)

        def rows_of(s):
            return pl.ds(pl.multiple_of(s * rows, rows), rows)

        for k in range(W // 128):
            vs[k:k + 1, :] = sums[:, k * 128:(k + 1) * 128]

        def seq_copy(k):
            dst = lax.rem(me + k, S)
            return pltpu.make_async_remote_copy(
                src_ref=stage.at[rows_of(dst)], dst_ref=seq_in.at[k - 1], send_sem=ss.at[k - 1], recv_sem=sr.at[k - 1],
                device_id=(dp, dst), device_id_type=MESH)

        def vseq_copy(k):
            dst = lax.rem(me + k, S)
            return pltpu.make_async_remote_copy(
                src_ref=vs, dst_ref=vs_seq.at[me], send_sem=vss.at[k - 1], recv_sem=vsr.at[k - 1],
                device_id=(dp, dst), device_id_type=MESH)

        for k in range(1, S):
            vseq_copy(k).start()
            seq_copy(k).start()
        vs_seq[me] = vs[...]
        for k in range(1, S):
            vseq_copy(k).wait()
        total = vs_seq[0]
        for s in range(1, S):
            total = total + vs_seq[s]
        vs_dp[dp] = total

        def vdp_copy(k):
            dst = lax.rem(dp + k, DP)
            return pltpu.make_async_remote_copy(
                src_ref=vs_dp.at[dp], dst_ref=vs_dp.at[dp], send_sem=vds.at[k - 1], recv_sem=vdr.at[k - 1],
                device_id=(dst, me), device_id_type=MESH)

        for k in range(1, DP):
            vdp_copy(k).start()
        for k in range(1, S):
            seq_copy(k).wait()
        acc = dW[rows_of(me), :]
        for k in range(1, S):
            acc = acc + seq_in[k - 1].astype(F32)
        dW[rows_of(me), :] = acc
        mid[...] = acc.astype(BF)

        def chunk(d):
            rg, lg = lax.div(d, DP // groups), lax.rem(d, DP // groups)
            return pl.ds(pl.multiple_of(rg * crow, crow), crow), pl.ds(pl.multiple_of(lg * lanes, 128), lanes)

        def dp_copy(k):
            dst = lax.rem(dp + k, DP)
            cr, cl = chunk(dst)
            return pltpu.make_async_remote_copy(
                src_ref=mid.at[cr, cl], dst_ref=dp_in.at[k - 1], send_sem=ds_.at[k - 1], recv_sem=dr.at[k - 1],
                device_id=(dst, me), device_id_type=MESH)

        for k in range(1, DP):
            dp_copy(k).start()
        for k in range(1, DP):
            vdp_copy(k).wait()
        total = vs_dp[0]
        for s in range(1, DP):
            total = total + vs_dp[s]
        gv_ref[...] = total
        for k in range(1, DP):
            dp_copy(k).wait()
        rg, lg = lax.div(dp, DP // groups), lax.rem(dp, DP // groups)
        cr = pl.ds(pl.multiple_of(me * rows + rg * crow, crow), crow)
        cl = pl.ds(pl.multiple_of(lg * lanes, 128), lanes)
        acc = dW[cr, cl]
        for k in range(1, DP):
            acc = acc + dp_in[k - 1].astype(F32)
        gath[cr, cl] = acc.astype(BF)

        def back_copy(k):
            dst = lax.rem(dp + k, DP)
            return pltpu.make_async_remote_copy(
                src_ref=gath.at[cr, cl], dst_ref=gath.at[cr, cl], send_sem=gs.at[k - 1], recv_sem=gr.at[k - 1],
                device_id=(dst, me), device_id_type=MESH)

        for k in range(1, DP):
            back_copy(k).start()
        for k in range(1, DP):
            back_copy(k).wait()

        def full_copy(k):
            dst = lax.rem(me + k, S)
            return pltpu.make_async_remote_copy(
                src_ref=gath.at[rows_of(me)], dst_ref=gath.at[rows_of(me)], send_sem=fs.at[k - 1], recv_sem=fr.at[k - 1],
                device_id=(dp, dst), device_id_type=MESH)

        for k in range(1, S):
            full_copy(k).start()
        for k in range(1, S):
            full_copy(k).wait()
        out = pltpu.make_async_copy(gath, gw_ref, out_sem)
        out.start()
        out.wait()
    else:
        out = pltpu.make_async_copy(dW, gw_ref, out_sem)
        out.start()
        out.wait()
        for k in range(W // 128):
            gv_ref[k:k + 1, :] = sums[:, k * 128:(k + 1) * 128]

    for a in range(2):
        for r in range(R):
            @pl.loop(me + 1, S)
            def _(dst):
                normed_copy(a, r, me, dst).wait_send()

            @pl.loop(0, me)
            def _(dst):
                part_copy(a, r, me, dst).wait_send()


def solution(mesh):
    S, DP = mesh.shape["seq"], mesh.shape["dp"]

    def shards(hidden_in, embedding, lengths, cotangent, ln1_gain, ln1_bias, qkv_weight, qv_bias, out_weight, out_bias,
               ln2_gain, ln2_bias, up_weight, up_bias, down_weight, down_bias):
        L, R, D = hidden_in.shape
        FF = up_weight.shape[1]
        W = 4 * D + 2 * FF
        rows = D // S
        groups = min(DP, rows // 16)
        reduce_here = rows % 16 == 0 and DP % groups == 0 and rows % (16 * groups) == 0 and W % (128 * (DP // groups)) == 0
        cfg = (S, DP, R, L, D, FF, reduce_here)
        lanes = W // (DP // groups)
        crow = rows // groups
        VM = pltpu.VMEM
        DMA = pltpu.SemaphoreType.DMA
        scratch = [
            VM((3, D, D), BF), VM((2, D, 128), F32), VM((R, L, D), F32), VM((R, L, D), F32), VM((R, L, D), F32),
            VM((2, R, S * L, D), BF), VM((2, R, L, D), F32), VM((2, R, L, 128), F32), VM((2, R, L, D), F32),
            VM((2, R, L, 128), F32), VM((2, R, D, L), BF), VM((D, L), BF), VM((2, R, L, D), BF),
            VM((2, R, HEADS, 8, L), F32), VM((2, R, D, L), BF), VM((2, R, L, FF), BF), VM((2, R, L, FF), F32),
            VM((2, R, S, HEADS, L, L), BF), VM((2, R, S - 1, L, D), BF), VM((2, R, S - 1, L, D), BF), VM((8, W), F32),
            DMA((2, R, S)), DMA((2, R, S)), DMA((2, R, S)), DMA((2, R, S)), DMA,
        ]
        if reduce_here:
            scratch += [
                VM((D, W), BF), VM((S - 1, rows, W), BF), VM((rows, W), BF), VM((DP - 1, crow, lanes), BF), VM((D, W), BF),
                VM((W // 128, 128), F32), VM((S, W // 128, 128), F32), VM((DP, W // 128, 128), F32),
                DMA((S - 1,)), DMA((S - 1,)), DMA((DP - 1,)), DMA((DP - 1,)), DMA((DP - 1,)), DMA((DP - 1,)),
                DMA((S - 1,)), DMA((S - 1,)), DMA((S - 1,)), DMA((S - 1,)), DMA((DP - 1,)), DMA((DP - 1,)),
            ]
        vm = pl.BlockSpec(memory_space=pltpu.VMEM)
        sm = pl.BlockSpec(memory_space=pltpu.SMEM)
        rows_first = lambda x: jnp.transpose(x, (1, 0, 2))
        line = lambda x: x.reshape(1, -1)
        y, g1, ge, gw, gv = pl.pallas_call(
            functools.partial(block_kernel, cfg),
            out_shape=(
                jax.ShapeDtypeStruct((R, L, D), BF), jax.ShapeDtypeStruct((R, L, D), F32),
                jax.ShapeDtypeStruct((R, L, D), F32), jax.ShapeDtypeStruct((D, W), BF if reduce_here else F32),
                jax.ShapeDtypeStruct((W // 128, 128), F32)),
            in_specs=[vm, vm, vm, sm] + [vm] * 12,
            out_specs=(vm, vm, vm, pl.BlockSpec(memory_space=pl.ANY), vm),
            scratch_shapes=scratch,
            compiler_params=pltpu.CompilerParams(
                collective_id=0, has_side_effects=True, vmem_limit_bytes=VMEM_LIMIT),
        )(rows_first(hidden_in), rows_first(embedding), rows_first(cotangent), lengths, line(ln1_gain), line(ln1_bias),
          qkv_weight, qv_bias, out_weight, line(out_bias), line(ln2_gain), line(ln2_bias), up_weight, line(up_bias),
          down_weight, line(down_bias))
        gv = gv.reshape(-1)
        if not reduce_here:
            gw, gv = lax.psum((gw, gv), ("dp", "seq"))
        gw = gw.astype(F32)
        part = lambda k, n=1: gv[k * D:(k + n) * D]
        return (
            rows_first(y), rows_first(g1), rows_first(ge), part(0), part(1), gw[:, 2 * FF + D:], part(2, 2).reshape(2, D),
            gw[:, 2 * FF:2 * FF + D], part(4), part(5), part(6), gw[:, :FF], part(8, FF // D), gw[:, FF:2 * FF].T, part(7))

    token = P("seq", "dp", None)
    return jax.shard_map(
        shards, mesh=mesh, in_specs=(token, token, P("dp"), token) + (P(),) * 12, out_specs=(token,) * 3 + (P(),) * 12,
        check_vma=False)


VMEM_LIMIT = 62 * 1024 * 1024
```

```python
import functools
import types

import jax
import jax.numpy as jnp
from jax import lax
from jax.experimental import pallas as pl
from jax.experimental.pallas import tpu as pltpu
from jax.sharding import PartitionSpec as P

EPS = 1e-05
MASKED = -1e30
HEADS = 4
HD = 64
BF = jnp.bfloat16
F32 = jnp.float32
MESH = pl.DeviceIdType.MESH
VMEM_LIMIT = 60 * 1024 * 1024


def nn(a, b):
    return lax.dot_general(a, b, (((1,), (0,)), ((), ())), preferred_element_type=F32)


def nt(a, b):
    return lax.dot_general(a, b, (((1,), (1,)), ((), ())), preferred_element_type=F32)


def normalise(x):
    mean = jnp.mean(x, axis=-1, keepdims=True)
    centred = x - mean
    rstd = lax.rsqrt(jnp.mean(centred * centred, axis=-1, keepdims=True) + EPS)
    return centred * rstd, rstd


def norm_back(grad, gain, xhat, rstd):
    gl = grad * gain
    m1 = jnp.mean(gl, axis=-1, keepdims=True)
    m2 = jnp.mean(gl * xhat, axis=-1, keepdims=True)
    return rstd * (gl - m1 - xhat * m2)


def fold(x):
    return jnp.sum(x.reshape(x.shape[0] // 8, 8, x.shape[1]), axis=0)


def gelu_parts(x):
    c0 = 0.7978845608028654
    x2 = x * x
    t = jnp.tanh(c0 * (x + 0.044715 * (x2 * x)))
    half = 0.5 * (1.0 + t)
    slope = half + (0.5 * x) * (1.0 - t * t) * (c0 * (1.0 + (3 * 0.044715) * x2))
    return x * half, slope


def head_rows(x, h):
    own = x[h * HD:(h + 1) * HD]
    zero = jnp.zeros_like(own)
    return jnp.concatenate([own, zero] if h % 2 == 0 else [zero, own], axis=0)


def pair(h):
    return slice((h // 2) * 2 * HD, (h // 2 + 1) * 2 * HD)


def heads_apart(x):
    lane = lax.broadcasted_iota(jnp.int32, x.shape, 1)
    return jnp.concatenate(
        [jnp.where((lane >= h * HD) & (lane < (h + 1) * HD), x, jnp.zeros((), x.dtype)) for h in range(HEADS)], axis=0)


def wide(x, n):
    return jnp.concatenate([x] * (n // 128), axis=1)


class Share:
    def __init__(self, v, start, w, into):
        self.v, self.w = v, w
        self.cols = slice(start, start + w)
        self.start_lane = start
        self.r1, self.r2, self.r3, self.r4, self.send, self.recv = into
        self.Z, self.X = v.DP // 2, v.S // 2
        D = v.D
        self.k, self.x = lax.rem(v.me, 2), lax.div(v.me, 2)
        self.y, self.z = lax.rem(v.dp, 2), lax.div(v.dp, 2)
        self.h1, self.h2, self.h3 = D // 2, D // 4, D // 4 // self.Z
        self.b1 = self.k * self.h1
        self.b2 = self.b1 + self.y * self.h2
        self.b3 = self.b2 + self.z * self.h3
        self.wx = w // self.X

    def rows(self, base, n):
        return pl.ds(pl.multiple_of(base, 16), n)

    def lanes(self, x):
        return pl.ds(pl.multiple_of(self.start_lane + x * self.wx, 128), self.wx)

    def copies(self, i):
        v, Z, X = self.v, self.Z, self.X
        if i == 1 or i == 8:
            dev = (v.dp, v.me + 1 - 2 * self.k)
            if i == 1:
                return [(v.stage.at[self.rows((1 - self.k) * self.h1, self.h1), self.cols], self.r1, dev)]
            ref = v.gath.at[self.rows(self.b1, self.h1), self.cols]
            return [(ref, ref, dev)]
        if i == 2 or i == 7:
            dev = (v.dp + 1 - 2 * self.y, v.me)
            if i == 2:
                return [(v.stage.at[self.rows(self.b1 + (1 - self.y) * self.h2, self.h2), self.cols], self.r2, dev)]
            ref = v.gath.at[self.rows(self.b2, self.h2), self.cols]
            return [(ref, ref, dev)]
        out = []
        if i == 3 or i == 6:
            for j in range(1, Z):
                other = lax.rem(self.z + j, Z)
                dev = (other * 2 + self.y, v.me)
                if i == 3:
                    out.append((v.stage.at[self.rows(self.b2 + other * self.h3, self.h3), self.cols], self.r3.at[j - 1], dev))
                else:
                    ref = v.gath.at[self.rows(self.b3, self.h3), self.cols]
                    out.append((ref, ref, dev))
            return out
        for j in range(1, X):
            other = lax.rem(self.x + j, X)
            dev = (v.dp, other * 2 + self.k)
            if i == 4:
                out.append((v.stage.at[self.rows(self.b3, self.h3), self.lanes(other)], self.r4.at[j - 1], dev))
            else:
                ref = v.gath.at[self.rows(self.b3, self.h3), self.lanes(self.x)]
                out.append((ref, ref, dev))
        return out

    def made(self, i):
        return [pltpu.make_async_remote_copy(src_ref=s, dst_ref=d, send_sem=self.send.at[i - 1, j], recv_sem=self.recv.at[i - 1, j],
                                             device_id=dev, device_id_type=MESH)
                for j, (s, d, dev) in enumerate(self.copies(i))]

    def start(self, i):
        v = self.v
        if i == 1:
            there = self.rows((1 - self.k) * self.h1, self.h1)
            v.stage[there, self.cols] = v.dW[there, self.cols].astype(BF)
        for c in self.made(i):
            c.start()

    def finish(self, i):
        v = self.v
        for c in self.made(i):
            c.wait()
        if i == 1:
            here, n, got = self.rows(self.b1, self.h1), self.h1, [self.r1]
        elif i == 2:
            here, n, got = self.rows(self.b2, self.h2), self.h2, [self.r2]
        elif i == 3:
            here, n, got = self.rows(self.b3, self.h3), self.h3, [self.r3.at[j] for j in range(self.Z - 1)]
        elif i == 4:
            here = self.rows(self.b3, self.h3)
            total = v.dW[here, self.lanes(self.x)]
            for j in range(self.X - 1):
                total = total + self.r4[j].astype(F32)
            v.gath[here, self.lanes(self.x)] = total.astype(BF)
            return
        else:
            return
        total = v.dW[here, self.cols]
        for g in got:
            total = total + g[...].astype(F32)
        v.dW[here, self.cols] = total
        v.stage[here, self.cols] = total.astype(BF)

    def step(self, i):
        if i >= 1:
            self.finish(i)
        if i < 8:
            self.start(i + 1)


class SmallSum:
    def __init__(self, v):
        self.v = v

    def copies(self, i):
        v = self.v
        buf, n, me, send, recv = (v.vs_seq, v.S, v.me, v.vss, v.vsr) if i == 0 else (v.vs_dp, v.DP, v.dp, v.vds, v.vdr)
        out = []
        for k in range(1, n):
            other = lax.rem(me + k, n)
            out.append(pltpu.make_async_remote_copy(
                src_ref=buf.at[me], dst_ref=buf.at[me], send_sem=send.at[k - 1], recv_sem=recv.at[k - 1],
                device_id=(v.dp, other) if i == 0 else (other, v.me), device_id_type=MESH))
        return out

    def start(self, i):
        for c in self.copies(i):
            c.start()

    def finish(self, i):
        for c in self.copies(i):
            c.wait()
        v = self.v
        buf, n = (v.vs_seq, v.S) if i == 0 else (v.vs_dp, v.DP)
        total = buf[0]
        for s in range(1, n):
            total = total + buf[s]
        return total


def block_kernel(cfg, names, *refs):
    S, DP, R, L, D, FF, reduce_here = cfg
    W = 4 * D + 2 * FF
    v = types.SimpleNamespace(**dict(zip(names, refs, strict=True)))
    v.S, v.DP, v.R, v.L, v.D, v.FF, v.W, v.reduce_here = S, DP, R, L, D, FF, W, reduce_here
    v.me, v.dp = me, dp = lax.axis_index("seq"), lax.axis_index("dp")
    v.chip, v.core = chip, core = lax.div(me, 2), lax.rem(me, 2)
    X = S // 2
    v.mine = mine = pl.ds(pl.multiple_of(me * L, L), L)
    sizes = (S // 2, S) if S > 1 else (S,)

    def with_size(body):
        low = 0
        for n in sizes:
            pl.when((me >= low) & (me < n))(functools.partial(body, n))
            low = n

    @pl.loop(me + 1, S)
    def _(t):
        for a in range(2):
            for r in range(R):
                v.nall[a, r, pl.ds(pl.multiple_of(t * L, L), L)] = jnp.zeros((L, D), BF)

    barrier = pltpu.get_barrier_semaphore()
    for k in range(1, S):
        pl.semaphore_signal(barrier, inc=1, device_id=(dp, lax.rem(me + k, S)), device_id_type=MESH)
    peers = S - 1
    if reduce_here:
        for k in range(1, DP):
            pl.semaphore_signal(barrier, inc=1, device_id=(lax.rem(dp + k, DP), me), device_id_type=MESH)
        peers += DP - 1

    ln1g, ln1b = v.ln1g[...], v.ln1b[...]
    ln2g, ln2b = v.ln2g[...], v.ln2b[...]

    def block_of(a, r, t):
        return v.nall.at[a, r, pl.ds(pl.multiple_of(t * L, L), L)]

    def normed_copy(a, r, t, send_sem, dst):
        ref = block_of(a, r, t)
        return pltpu.make_async_remote_copy(
            src_ref=ref, dst_ref=ref, send_sem=send_sem, recv_sem=v.nrecv.at[a, r, t], device_id=(dp, dst), device_id_type=MESH)

    def to_chip(a, r, c):
        return normed_copy(a, r, me, v.nsend.at[a, r, c], 2 * c + core)

    def to_sibling(a, r):
        return normed_copy(a, r, me, v.nsend.at[a, r, X], me + 1 - 2 * core)

    def handed_on(a, r, c):
        return normed_copy(a, r, 2 * c + core, v.fsend.at[a, r, c], me + 1 - 2 * core)

    def each_send(a, r, action):
        @pl.loop(chip + 1, X)
        def _(c):
            action(to_chip(a, r, c))

        @pl.when(core == 0)
        def _():
            action(to_sibling(a, r))

    def first_norm(a, r):
        u = v.stream[r] + v.emb[r].astype(F32)
        v.stream[r] = u
        xhat, rstd = normalise(u)
        v.xh1[a, r] = xhat
        v.rs1[a, r] = jnp.broadcast_to(rstd, (L, 128))
        v.nall[a, r, mine] = (xhat * ln1g + ln1b).astype(BF)

    def announce(a, r):
        each_send(a, r, lambda c: c.start())

    def hand_on(a, r):
        @pl.loop(0, chip)
        def _(c):
            handed_on(a, r, c).wait_recv()
            handed_on(a, r, c).start()

    def gathered(a, r):
        @pl.loop(0, chip)
        def _(c):
            normed_copy(a, r, 2 * c + 1 - core, v.fsend.at[a, r, c], me).wait_recv()

        @pl.when(core == 1)
        def _():
            normed_copy(a, r, me - 1, v.nsend.at[a, r, X], me).wait_recv()

    @pl.loop(0, R)
    def _(r):
        v.stream[r] = v.hid[r].astype(F32)

    first_norm(0, 0)
    pl.semaphore_wait(barrier, peers)
    announce(0, 0)

    for k in range(3):
        v.wT[k] = v.wqkv[:, k * D:(k + 1) * D].T
    for k in range(2):
        v.bcol[k] = jnp.broadcast_to(v.qvb[k:k + 1, :], (128, D)).T
    v.vec[...] = jnp.zeros_like(v.vec)

    @pl.loop(1, R)
    def _(r):
        first_norm(0, r)
        announce(0, r)

    def forward_attention(a, r, bias, s_scr, nb):
        KB = nb * L
        length = v.lengths[r]
        rows = v.nall[a, r, 0:KB, :]
        keys = nn(rows, v.wqkv[:, D:2 * D]).astype(BF)
        VT = (nt(v.wT[2], rows) + wide(v.bcol[1], KB)).astype(BF)
        qT = v.qT[...]
        for t in range(nb):
            key_pos = t * L + lax.broadcasted_iota(jnp.int32, (L, L), 0)
            query_pos = me * L + lax.broadcasted_iota(jnp.int32, (L, L), 1)
            bias[t * L:(t + 1) * L] = jnp.where((key_pos <= query_pos) & (key_pos < length), 0.0, MASKED)
        tops = []
        for h in range(HEADS):
            s = nn(keys[:, pair(h)], head_rows(qT, h)) + bias[0:KB]
            s_scr[0:KB, h * L:(h + 1) * L] = s
            tops.append(jnp.max(jnp.max(s.reshape(KB // 8, 8, L), axis=0), axis=0, keepdims=True))
        for h in range(HEADS):
            hs = slice(h * HD, (h + 1) * HD)
            e = jnp.exp(s_scr[0:KB, h * L:(h + 1) * L] - tops[h])
            inv = 1.0 / jnp.sum(fold(e), axis=0, keepdims=True)
            low = e.astype(BF)
            v.e_scr[a, r, 0:KB, h * L:(h + 1) * L] = low
            v.linv[a, r, h] = jnp.broadcast_to(inv, (8, L))
            v.oT[a, r, hs] = (nn(VT[hs], low) * inv).astype(BF)

    def forward_all(bias, s_scr):
        hand_on(0, 0)

        @pl.loop(0, 2 * R)
        def _(n):
            a, r = lax.div(n, R), lax.rem(n, R)
            normed = v.nall[a, r, mine]
            qT = ((nt(v.wT[0], normed) + wide(v.bcol[0], L)) * (HD ** -0.5)).astype(BF)
            v.qn[a, r] = qT.T
            v.qT[...] = qT
            gathered(a, r)
            with_size(functools.partial(forward_attention, a, r, bias, s_scr))

            @pl.when(n < 2 * R - 1)
            def _():
                hand_on(lax.div(n + 1, R), lax.rem(n + 1, R))

            middle = v.stream[r] + (nn(v.oT[a, r].T, v.wout[...]) + v.bout[...])
            xhat, rstd = normalise(middle)
            v.xh2[a, r] = xhat
            v.rs2[a, r] = jnp.broadcast_to(rstd, (L, 128))
            normed2 = (xhat * ln2g + ln2b).astype(BF)
            v.n2T[a, r] = normed2.T
            hidden, slope = gelu_parts(nn(normed2, v.wup[...]) + v.bup[...])
            hidden = hidden.astype(BF)
            v.hidden[a, r] = hidden
            v.slope[a, r] = slope
            v.stream[r] = middle + (nn(hidden, v.wdn[...]) + v.bdn[...])

            @pl.when(a == 0)
            def _():
                first_norm(1, r)
                announce(1, r)

            @pl.when(a == 1)
            def _():
                v.y[r] = v.stream[r].astype(BF)
                v.gstream[r] = v.cot[r].astype(F32)

    VM = pltpu.VMEM
    pl.run_scoped(forward_all, VM((S * L, L), F32), VM((S * L, HEADS * L), F32))
    pl.run_scoped(functools.partial(backward, v, with_size), VM((R, D, L), BF), VM((R, L, FF), BF), VM((R, L, D), BF),
                  VM((R, L, 3 * D), BF), VM((D, W), F32), VM((S * L, HEADS * L), BF))

    for a in range(2):
        for r in range(R):
            each_send(a, r, lambda c: c.wait_send())

            @pl.loop(0, chip)
            def _(c):
                handed_on(a, r, c).wait_send()


def backward(v, with_size, gbT, gpre, ga_s, gqkv, dW, ds_s):
    S, DP, R, L, D, FF, W = v.S, v.DP, v.R, v.L, v.D, v.FF, v.W
    me, dp, mine = v.me, v.dp, v.mine
    v.dW = dW
    ln1g, ln2g = v.ln1g[...], v.ln2g[...]
    UP, DN, OW, QW = 0, FF, 2 * FF, 2 * FF + D
    V_LN1G, V_LN1B, V_QB, V_VB, V_OB, V_LN2G, V_LN2B, V_DB, V_UB = [D * k for k in range(9)]

    def part_copy(a, r, src, dst):
        return pltpu.make_async_remote_copy(
            src_ref=v.pg_out.at[a, r, dst], dst_ref=v.pg_in.at[a, r, src - 1], send_sem=v.psend.at[a, r, dst],
            recv_sem=v.precv.at[a, r, src], device_id=(dp, dst), device_id_type=MESH)

    def add_vec(start, terms):
        v.vec[:, start:start + terms.shape[1]] += fold(terms)

    def backward_mlp(a, r):
        g = v.gstream[r]
        gb = g.astype(BF)
        add_vec(V_DB, gb.astype(F32))
        gbT[r] = gb.T
        pre = (nt(gb, v.wdn[...]) * v.slope[a, r]).astype(BF)
        gpre[r] = pre
        add_vec(V_UB, pre.astype(F32))
        gn2 = nt(pre, v.wup[...])
        xhat = v.xh2[a, r]
        add_vec(V_LN2G, gn2 * xhat)
        add_vec(V_LN2B, gn2)
        gm = g + norm_back(gn2, ln2g, xhat, wide(v.rs2[a, r], D))
        v.gmid[r] = gm
        ga = gm.astype(BF)
        ga_s[r] = ga
        add_vec(V_OB, ga.astype(F32))

    def attention_core(a, r, nb):
        KB = nb * L
        gaT = nt(v.wout[...], ga_s[r]).astype(BF).astype(F32)
        oT = v.oT[a, r].astype(F32)
        scaled, deltas = [], []
        for h in range(HEADS):
            hs = slice(h * HD, (h + 1) * HD)
            part = gaT[hs] * v.linv[a, r, h, 0:1]
            scaled.append(part.astype(BF))
            deltas.append(jnp.sum(part * oT[hs], axis=0, keepdims=True))
        gaT_n = jnp.concatenate(scaled, axis=0)
        rows = v.nall[a, r, 0:KB, :]
        values = (nn(rows, v.wqkv[:, 2 * D:]) + v.qvb[1:2, :]).astype(BF)
        KT = nt(v.wT[1], rows).astype(BF)
        for h in range(HEADS):
            hl = slice(h * L, (h + 1) * L)
            gp = nn(values[:, pair(h)], head_rows(gaT_n, h))
            ds_s[0:KB, hl] = (v.e_scr[a, r, 0:KB, hl].astype(F32) * (gp - deltas[h])).astype(BF)
        gv = nn(v.e_scr[a, r, 0:KB, :], heads_apart(gaT_n.T))
        gk = nn(ds_s[0:KB, :], heads_apart(v.qn[a, r]))
        gkv = jnp.concatenate([gk, gv], axis=1).astype(BF)
        gqT = jnp.concatenate([nn(KT[h * HD:(h + 1) * HD], ds_s[0:KB, h * L:(h + 1) * L]) for h in range(HEADS)], axis=0)
        pg = nt(gkv, v.wqkv[:, D:]).astype(BF)
        for t in range(nb):
            @pl.when(t < me)
            def _():
                v.pg_out[a, r, t] = pg[t * L:(t + 1) * L]
                part_copy(a, r, me, t).start()

            @pl.when(t == me)
            def _():
                gqkv[r, :, D:] = gkv[t * L:(t + 1) * L]

        add_vec(V_VB, gkv[:, D:].astype(F32))
        dW[:, QW + D:QW + 3 * D] += nn(rows.T, gkv)
        gq = (gqT * (HD ** -0.5)).T.astype(BF)
        gqkv[r, :, :D] = gq
        add_vec(V_QB, gq.astype(F32))

    def backward_norm(a, r):
        gn = nt(gqkv[r], v.wqkv[...])

        def add(s, total):
            part_copy(a, r, s, me).wait_recv()
            return total + v.pg_in[a, r, s - 1].astype(F32)

        gn = lax.fori_loop(me + 1, S, add, gn)
        xhat = v.xh1[a, r]
        add_vec(V_LN1G, gn * xhat)
        add_vec(V_LN1B, gn)
        v.gstream[r] = v.gmid[r] + norm_back(gn, ln1g, xhat, wide(v.rs1[a, r], D))

    def put(first, start, value):
        if first:
            dW[:, start:start + value.shape[1]] = value
        else:
            dW[:, start:start + value.shape[1]] += value

    def weight_terms(a):
        first = a == 1
        put(first, UP, sum(nn(v.n2T[a, r], gpre[r]) for r in range(R)))
        put(first, DN, sum(nn(gbT[r], v.hidden[a, r]) for r in range(R)))
        put(first, OW, sum(nn(v.oT[a, r], ga_s[r]) for r in range(R)))

    def query_terms(a):
        put(a == 1, QW, sum(nn(v.nall[a, r, mine].T, gqkv[r, :, :D]) for r in range(R)))

    shares = []
    if v.reduce_here:
        into = lambda p: tuple(getattr(v, f"{n}_{p}") for n in ("r1", "r2", "r3", "r4", "ss", "sr"))
        shares = [Share(v, 0, 2 * FF + D, into(0)), Share(v, QW, 3 * D, into(1))]

    dW[:, QW + D:QW + 3 * D] = jnp.zeros((D, 2 * D), F32)
    for a in (1, 0):
        @pl.loop(0, R)
        def _(r):
            backward_mlp(a, r)

        weight_terms(a)

        @pl.loop(0, R)
        def _(r):
            with_size(functools.partial(attention_core, a, r))

        query_terms(a)

        @pl.loop(0, R)
        def _(r):
            backward_norm(a, r)
            if a == 1:
                v.g1[r] = v.gstream[r]
            else:
                g = v.gstream[r]
                v.ge[r] = g + v.g1[r]
                v.g1[r] = g

    sums = jnp.sum(v.vec[...], axis=0, keepdims=True)
    if v.reduce_here:
        for k in range(W // 128):
            v.vs_seq[me, k:k + 1, :] = sums[:, k * 128:(k + 1) * 128]
        small = SmallSum(v)
        small.start(0)
        for share in shares:
            share.start(1)
        v.vs_dp[dp] = small.finish(0)
        small.start(1)
        for i in range(1, 9):
            for share in shares:
                share.step(i)
            if i == 1:
                v.gv[...] = small.finish(1)
        out = pltpu.make_async_copy(v.gath, v.gw, v.out_sem)
        out.start()
        out.wait()
    else:
        out = pltpu.make_async_copy(v.gath if v.reduce_here else dW, v.gw, v.out_sem)
        out.start()
        out.wait()
        for k in range(W // 128):
            v.gv[k:k + 1, :] = sums[:, k * 128:(k + 1) * 128]

    for a in range(2):
        for r in range(R):
            @pl.loop(0, me)
            def _(dst):
                part_copy(a, r, me, dst).wait_send()


def finish_kernel(D, FF, names, *refs):
    v = types.SimpleNamespace(**dict(zip(names, refs, strict=True)))
    load = lambda i, src, dst: pltpu.make_async_copy(src, dst, v.sems.at[0, i])
    save = lambda i, src, dst: pltpu.make_async_copy(src, dst, v.sems.at[1, i])
    loads = [load(0, v.gw, v.gw_s), load(1, v.gv, v.gv_s), load(2, v.g1, v.g1_s), load(3, v.ge, v.ge_s), load(4, v.y, v.y_s)]
    for c in loads:
        c.start()
    saves = []

    def keep(src, dst):
        saves.append(save(len(saves), src, dst))
        saves[-1].start()

    loads[0].wait()
    v.wup_s[...] = v.gw_s[:, 0:FF].astype(F32)
    keep(v.wup_s, v.wup)
    v.wdn_s[...] = v.gw_s[:, FF:2 * FF].T.astype(F32)
    keep(v.wdn_s, v.wdn)
    v.wqkv_s[...] = v.gw_s[:, 2 * FF + D:].astype(F32)
    keep(v.wqkv_s, v.wqkv)
    v.wout_s[...] = v.gw_s[:, 2 * FF:2 * FF + D].astype(F32)
    keep(v.wout_s, v.wout)
    for c, src, dst in zip(loads[2:], (v.g1_s, v.ge_s, v.y_s), (v.g1_o, v.ge_o, v.y_o)):
        c.wait()
        keep(src, dst)
    loads[1].wait()
    n = D // 128
    at = 0
    for ref, size in ((v.ln1g, n), (v.ln1b, n), (v.qvb, 2 * n), (v.bout, n), (v.ln2g, n), (v.ln2b, n), (v.bdn, n),
                      (v.bup, FF // 128)):
        for k in range(size):
            row, col = divmod(k, ref.shape[1] // 128)
            ref[row:row + 1, col * 128:(col + 1) * 128] = v.gv_s[at + k:at + k + 1, :]
        at += size
    for c in saves:
        c.wait()


def solution(mesh):
    S, DP = mesh.shape["seq"], mesh.shape["dp"]

    def shards(hidden_in, embedding, lengths, cotangent, ln1_gain, ln1_bias, qkv_weight, qv_bias, out_weight, out_bias,
               ln2_gain, ln2_bias, up_weight, up_bias, down_weight, down_bias):
        L, R, D = hidden_in.shape
        FF = up_weight.shape[1]
        W = 4 * D + 2 * FF
        X, Z = max(S // 2, 1), max(DP // 2, 1)
        parts = (2 * FF + D, 3 * D)
        reduce_here = (S % 2 == 0 and DP % 2 == 0 and Z > 1 and X > 1 and (D // 4) % (16 * Z) == 0
                       and all(w % (128 * X) == 0 for w in parts))
        cfg = (S, DP, R, L, D, FF, reduce_here)
        VM = pltpu.VMEM
        DMA = pltpu.SemaphoreType.DMA
        scratch = dict(
            wT=VM((3, D, D), BF), bcol=VM((2, D, 128), F32), stream=VM((R, L, D), F32), gstream=VM((R, L, D), F32),
            gmid=VM((R, L, D), F32), nall=VM((2, R, S * L, D), BF), xh1=VM((2, R, L, D), F32), rs1=VM((2, R, L, 128), F32),
            xh2=VM((2, R, L, D), F32), rs2=VM((2, R, L, 128), F32), n2T=VM((2, R, D, L), BF), qT=VM((D, L), BF),
            qn=VM((2, R, L, D), BF), linv=VM((2, R, HEADS, 8, L), F32), oT=VM((2, R, D, L), BF),
            hidden=VM((2, R, L, FF), BF), slope=VM((2, R, L, FF), F32), e_scr=VM((2, R, S * L, HEADS * L), BF),
            pg_out=VM((2, R, S - 1, L, D), BF), pg_in=VM((2, R, S - 1, L, D), BF), vec=VM((8, W), F32),
            nsend=DMA((2, R, X + 1)), fsend=DMA((2, R, X)), nrecv=DMA((2, R, S)), psend=DMA((2, R, S)), precv=DMA((2, R, S)),
            out_sem=DMA)
        if reduce_here:
            most = max(Z, X) - 1
            scratch.update(
                stage=VM((D, W), BF), gath=VM((D, W), BF), vs_seq=VM((S, W // 128, 128), F32), vs_dp=VM((DP, W // 128, 128), F32),
                vss=DMA((S - 1,)), vsr=DMA((S - 1,)), vds=DMA((DP - 1,)), vdr=DMA((DP - 1,)))
            for p, w in enumerate(parts):
                scratch.update({
                    f"r1_{p}": VM((D // 2, w), BF), f"r2_{p}": VM((D // 4, w), BF), f"r3_{p}": VM((Z - 1, D // 4 // Z, w), BF),
                    f"r4_{p}": VM((X - 1, D // 4 // Z, w // X), BF), f"ss_{p}": DMA((8, most)), f"sr_{p}": DMA((8, most))})
        vm = pl.BlockSpec(memory_space=pltpu.VMEM)
        sm = pl.BlockSpec(memory_space=pltpu.SMEM)
        hbm = pl.BlockSpec(memory_space=pl.ANY)
        rows_first = lambda x: jnp.transpose(x, (1, 0, 2))
        line = lambda x: x.reshape(1, -1)
        ins = dict(
            hid=rows_first(hidden_in), emb=rows_first(embedding), cot=rows_first(cotangent), lengths=lengths, ln1g=line(ln1_gain),
            ln1b=line(ln1_bias), wqkv=qkv_weight, qvb=qv_bias, wout=out_weight, bout=line(out_bias), ln2g=line(ln2_gain),
            ln2b=line(ln2_bias), wup=up_weight, bup=line(up_bias), wdn=down_weight, bdn=line(down_bias))
        shape = jax.ShapeDtypeStruct
        outs = dict(
            y=shape((R, L, D), BF), g1=shape((R, L, D), F32), ge=shape((R, L, D), F32),
            gw=shape((D, W), BF if reduce_here else F32), gv=shape((W // 128, 128), F32))
        names = (*ins, *outs, *scratch)
        y, g1, ge, gw, gv = pl.pallas_call(
            functools.partial(block_kernel, cfg, names), out_shape=tuple(outs.values()),
            in_specs=[sm if n == "lengths" else vm for n in ins], out_specs=tuple(hbm if n == "gw" else vm for n in outs),
            scratch_shapes=list(scratch.values()),
            compiler_params=pltpu.CompilerParams(collective_id=0, has_side_effects=True, vmem_limit_bytes=VMEM_LIMIT),
        )(*ins.values())
        if not reduce_here:
            gw, gv = lax.psum((gw, gv), ("dp", "seq"))
        full = [shape((R, L, D), BF), shape((R, L, D), F32), shape((R, L, D), F32), shape((1, D), F32), shape((1, D), F32),
                shape((D, 3 * D), F32), shape((2, D), F32), shape((D, D), F32), shape((1, D), F32), shape((1, D), F32),
                shape((1, D), F32), shape((D, FF), F32), shape((1, FF), F32), shape((FF, D), F32), shape((1, D), F32)]
        ends = ["y_o", "g1_o", "ge_o", "ln1g", "ln1b", "wqkv", "qvb", "wout", "bout", "ln2g", "ln2b", "wup", "bup", "wdn", "bdn"]
        large = ("y_o", "g1_o", "ge_o", "wqkv", "wout", "wup", "wdn")
        temps = dict(
            y_s=VM((R, L, D), BF), g1_s=VM((R, L, D), F32), ge_s=VM((R, L, D), F32), gw_s=VM((D, W), gw.dtype),
            gv_s=VM((W // 128, 128), F32), wup_s=VM((D, FF), F32), wdn_s=VM((FF, D), F32), wqkv_s=VM((D, 3 * D), F32),
            wout_s=VM((D, D), F32), sems=DMA((2, 7)))
        res = pl.pallas_call(
            functools.partial(finish_kernel, D, FF, (*outs, *ends, *temps)), out_shape=full, in_specs=[hbm] * 5,
            out_specs=[hbm if n in large else vm for n in ends], scratch_shapes=list(temps.values()),
            compiler_params=pltpu.CompilerParams(vmem_limit_bytes=VMEM_LIMIT))(y, g1, ge, gw, gv)
        flat = (3, 4, 8, 9, 10, 12, 14)
        return tuple(rows_first(x) if i < 3 else x.reshape(-1) if i in flat else x for i, x in enumerate(res))

    token = P("seq", "dp", None)
    return jax.shard_map(
        shards, mesh=mesh, in_specs=(token, token, P("dp"), token) + (P(),) * 12, out_specs=(token,) * 3 + (P(),) * 12,
        check_vma=False)
```

```python
import functools
import types

import jax
import jax.numpy as jnp
from jax import lax
from jax.experimental import pallas as pl
from jax.experimental.pallas import tpu as pltpu
from jax.sharding import PartitionSpec as P

EPS = 1e-05
MASKED = -1e30
HEADS = 4
HD = 64
BF = jnp.bfloat16
F32 = jnp.float32
MESH = pl.DeviceIdType.MESH
VMEM_LIMIT = 60 * 1024 * 1024


def nn(a, b):
    return lax.dot_general(a, b, (((1,), (0,)), ((), ())), preferred_element_type=F32)


def nt(a, b):
    return lax.dot_general(a, b, (((1,), (1,)), ((), ())), preferred_element_type=F32)


def normalise(x):
    mean = jnp.mean(x, axis=-1, keepdims=True)
    centred = x - mean
    rstd = lax.rsqrt(jnp.mean(centred * centred, axis=-1, keepdims=True) + EPS)
    return centred * rstd, rstd


def norm_back(grad, gain, xhat, rstd):
    gl = grad * gain
    m1 = jnp.mean(gl, axis=-1, keepdims=True)
    m2 = jnp.mean(gl * xhat, axis=-1, keepdims=True)
    return rstd * (gl - m1 - xhat * m2)


def fold(x):
    return jnp.sum(x.reshape(x.shape[0] // 8, 8, x.shape[1]), axis=0)


def gelu_parts(x):
    c0 = 0.7978845608028654
    x2 = x * x
    t = jnp.tanh(c0 * (x + 0.044715 * (x2 * x)))
    half = 0.5 * (1.0 + t)
    slope = half + (0.5 * x) * (1.0 - t * t) * (c0 * (1.0 + (3 * 0.044715) * x2))
    return x * half, slope


def head_rows(x, h):
    own = x[h * HD:(h + 1) * HD]
    zero = jnp.zeros_like(own)
    return jnp.concatenate([own, zero] if h % 2 == 0 else [zero, own], axis=0)


def pair(h):
    return slice((h // 2) * 2 * HD, (h // 2 + 1) * 2 * HD)


def heads_apart(x):
    lane = lax.broadcasted_iota(jnp.int32, x.shape, 1)
    return jnp.concatenate(
        [jnp.where((lane >= h * HD) & (lane < (h + 1) * HD), x, jnp.zeros((), x.dtype)) for h in range(HEADS)], axis=0)


def wide(x, n):
    return jnp.concatenate([x] * (n // 128), axis=1)


class Share:
    def __init__(self, v, start, w, into):
        self.v, self.start_lane = v, start
        self.cols = slice(start, start + w)
        self.r1, self.r2, self.r3, self.send, self.recv = into
        self.n2, self.n3 = v.S, v.DP // 2
        self.h1 = v.D // 2
        self.h2 = self.h1 // self.n2
        self.groups = self.h2 // 16
        self.w3 = w * self.groups // self.n3
        self.b1 = v.core * self.h1
        self.b2 = self.b1 + v.spot2 * self.h2

    def rows(self, base, n):
        return pl.ds(pl.multiple_of(base, 16), n)

    def chunk(self, z):
        row, lane = lax.rem(z, self.groups), lax.div(z, self.groups)
        return self.rows(self.b2 + row * 16, 16), pl.ds(pl.multiple_of(self.start_lane + lane * self.w3, 128), self.w3)

    def copies(self, i):
        v = self.v
        if i == 1:
            return [(v.stage.at[self.rows((1 - v.core) * self.h1, self.h1), self.cols], self.r1, v.sibling)]
        if i == 6:
            ref = v.gath.at[self.rows(self.b1, self.h1), self.cols]
            return [(ref, ref, v.sibling)]
        out = []
        if i in (2, 5):
            for j in range(1, self.n2):
                other = lax.rem(v.spot2 + j, self.n2)
                if i == 2:
                    src = v.stage.at[self.rows(self.b1 + other * self.h2, self.h2), self.cols]
                    out.append((src, self.r2.at[j - 1], v.in_plane(other)))
                else:
                    ref = v.gath.at[self.rows(self.b2, self.h2), self.cols]
                    out.append((ref, ref, v.in_plane(other)))
            return out
        for j in range(1, self.n3):
            other = lax.rem(v.spot3 + j, self.n3)
            if i == 3:
                out.append((v.stage.at[self.chunk(other)], self.r3.at[j - 1], v.across(other)))
            else:
                ref = v.gath.at[self.chunk(v.spot3)]
                out.append((ref, ref, v.across(other)))
        return out

    def made(self, i):
        return [pltpu.make_async_remote_copy(src_ref=s, dst_ref=d, send_sem=self.send.at[i - 1, j], recv_sem=self.recv.at[i - 1, j],
                                             device_id=dev, device_id_type=MESH)
                for j, (s, d, dev) in enumerate(self.copies(i))]

    def start(self, i):
        v = self.v
        if i == 1:
            there = self.rows((1 - v.core) * self.h1, self.h1)
            v.stage[there, self.cols] = v.dW[there, self.cols].astype(BF)
        for c in self.made(i):
            c.start()

    def finish(self, i):
        v = self.v
        for c in self.made(i):
            c.wait()
        if i > 3:
            return
        if i == 1:
            at, got = (self.rows(self.b1, self.h1), self.cols), [self.r1]
        elif i == 2:
            at, got = (self.rows(self.b2, self.h2), self.cols), [self.r2.at[j] for j in range(self.n2 - 1)]
        else:
            at, got = self.chunk(v.spot3), [self.r3.at[j] for j in range(self.n3 - 1)]
        total = v.dW[at]
        for g in got:
            total = total + g[...].astype(F32)
        if i == 3:
            v.gath[at] = total.astype(BF)
        else:
            v.dW[at] = total
            v.stage[at] = total.astype(BF)

    def step(self, i):
        self.finish(i)
        if i < 6:
            self.start(i + 1)


class SmallSum:
    def __init__(self, v):
        self.v = v
        self.stages = [(v.vs1, v.core, 2, lambda other: v.sibling, v.vss1, v.vsr1),
                       (v.vs2, v.spot2, v.S, v.in_plane, v.vss2, v.vsr2), (v.vs3, v.spot3, v.DP // 2, v.across, v.vss3, v.vsr3)]

    def copies(self, i):
        buf, spot, n, device, send, recv = self.stages[i]
        return [pltpu.make_async_remote_copy(
            src_ref=buf.at[spot], dst_ref=buf.at[spot], send_sem=send.at[k - 1], recv_sem=recv.at[k - 1],
            device_id=device(lax.rem(spot + k, n)), device_id_type=MESH) for k in range(1, n)]

    def start(self, i, value):
        buf, spot = self.stages[i][:2]
        buf[spot] = value
        for c in self.copies(i):
            c.start()

    def finish(self, i):
        for c in self.copies(i):
            c.wait()
        buf, n = self.stages[i][0], self.stages[i][2]
        total = buf[0]
        for s in range(1, n):
            total = total + buf[s]
        return total


def out_copy(v, which, src, dst, r):
    return pltpu.make_async_copy(src.at[r], dst.at[r], v.out_sems.at[which, r])


LOADS = ("hid", "emb", "ln1g", "ln1b", "wqkv", "qvb", "wup", "wdn", "wout", "bout", "ln2g", "ln2b", "bup", "bdn", "cot")


def block_kernel(cfg, names, *refs):
    S, DP, R, L, D, FF, reduce_here = cfg
    W = 4 * D + 2 * FF
    v = types.SimpleNamespace(**dict(zip(names, refs, strict=True)))
    v.S, v.DP, v.R, v.L, v.D, v.FF, v.W, v.reduce_here = S, DP, R, L, D, FF, W, reduce_here
    v.me, v.dp = me, dp = lax.axis_index("seq"), lax.axis_index("dp")
    v.chip, v.core = chip, core = lax.div(me, 2), lax.rem(me, 2)
    X = v.X = S // 2
    v.mine = mine = pl.ds(pl.multiple_of(me * L, L), L)
    v.sibling = (dp, me + 1 - 2 * core)
    sizes = (S // 2, S)

    def with_size(body):
        low = 0
        for n in sizes:
            pl.when((me >= low) & (me < n))(functools.partial(body, n))
            low = n

    barrier = pltpu.get_barrier_semaphore()
    peers = [v.sibling] + [(dp, lax.rem(me + 2 * k, S)) for k in range(1, X)]
    if reduce_here:
        v.spot2, v.spot3 = chip * 2 + lax.rem(dp, 2), lax.div(dp, 2)
        v.in_plane = lambda n: (lax.div(dp, 2) * 2 + lax.rem(n, 2), lax.div(n, 2) * 2 + core)
        v.across = lambda n: (n * 2 + lax.rem(dp, 2), me)
        peers += [(dp + 1 - 2 * lax.rem(dp, 2), lax.rem(me + 2 * k, S)) for k in range(X)]
        peers += [v.across(lax.rem(v.spot3 + k, DP // 2)) for k in range(1, DP // 2)]
    for peer in peers:
        pl.semaphore_signal(barrier, inc=1, device_id=peer, device_id_type=MESH)

    brought = {}
    for k, name in enumerate(LOADS):
        brought[name] = pltpu.make_async_copy(getattr(v, name + "_in"), getattr(v, name), v.in_sem.at[k])
        brought[name].start()

    def need(*which):
        for name in which:
            brought.pop(name).wait()

    v.need = need

    def block_of(a, r, t):
        return v.nall.at[a, r, pl.ds(pl.multiple_of(t * L, L), L)]

    def normed_copy(a, r, t, send_sem, dst):
        ref = block_of(a, r, t)
        return pltpu.make_async_remote_copy(
            src_ref=ref, dst_ref=ref, send_sem=send_sem, recv_sem=v.nrecv.at[a, r, t], device_id=(dp, dst), device_id_type=MESH)

    def to_chip(a, r, c):
        return normed_copy(a, r, me, v.nsend.at[a, r, c], 2 * c + core)

    def to_sibling(a, r):
        return normed_copy(a, r, me, v.nsend.at[a, r, X], me + 1 - 2 * core)

    def handed_on(a, r, c):
        return normed_copy(a, r, 2 * c + core, v.fsend.at[a, r, c], me + 1 - 2 * core)

    def each_send(a, r, action):
        @pl.loop(chip + 1, X)
        def _(c):
            action(to_chip(a, r, c))

        @pl.when(core == 0)
        def _():
            action(to_sibling(a, r))

    def first_norm(a, r):
        u = v.stream[r] + v.emb[r].astype(F32)
        v.stream[r] = u
        xhat, rstd = normalise(u)
        v.xh1[a, r] = xhat
        v.rs1[a, r] = jnp.broadcast_to(rstd, (L, 128))
        v.nall[a, r, mine] = (xhat * ln1g + ln1b).astype(BF)

    def announce(a, r):
        each_send(a, r, lambda c: c.start())

    def hand_on(a, r):
        @pl.loop(0, chip)
        def _(c):
            handed_on(a, r, c).wait_recv()
            handed_on(a, r, c).start()

    def gathered(a, r):
        @pl.loop(0, chip)
        def _(c):
            normed_copy(a, r, 2 * c + 1 - core, v.fsend.at[a, r, c], me).wait_recv()

        @pl.when(core == 1)
        def _():
            normed_copy(a, r, me - 1, v.nsend.at[a, r, X], me).wait_recv()

    @pl.loop(me + 1, S)
    def _(t):
        for a in range(2):
            for r in range(R):
                v.nall[a, r, pl.ds(pl.multiple_of(t * L, L), L)] = jnp.zeros((L, D), BF)

    v.vec[...] = jnp.zeros_like(v.vec)
    need("hid", "emb", "ln1g", "ln1b")
    ln1g, ln1b = v.ln1g[...], v.ln1b[...]

    @pl.loop(0, R)
    def _(r):
        v.stream[r] = v.hid[r].astype(F32)
        first_norm(0, r)

    need("wqkv", "qvb")
    for k in range(3):
        v.wT[k * D:(k + 1) * D] = v.wqkv[:, k * D:(k + 1) * D].T
    for k in range(2):
        v.bcol[k] = jnp.broadcast_to(v.qvb[k:k + 1, :], (128, D)).T
    need("wup", "wdn")
    for k in range(FF // D):
        ks = slice(k * D, (k + 1) * D)
        v.wupT[ks] = v.wup[:, ks].T
        v.wdnT[:, ks] = v.wdn[ks].T

    pl.semaphore_wait(barrier, len(peers))
    for r in range(R):
        announce(0, r)

    need("wout", "bout", "ln2g", "ln2b", "bup", "bdn", "cot")
    ln2g, ln2b = v.ln2g[...], v.ln2b[...]

    def forward_attention(a, r, bias, s_scr, nb):
        KB = nb * L
        length = v.lengths[r]
        rows = v.nall[a, r, 0:KB, :]
        keys = nn(rows, v.wqkv[:, D:2 * D]).astype(BF)
        VT = (nt(v.wT[2 * D:], rows) + wide(v.bcol[1], KB)).astype(BF)
        qT = v.qT[...]
        for t in range(nb):
            key_pos = t * L + lax.broadcasted_iota(jnp.int32, (L, L), 0)
            query_pos = me * L + lax.broadcasted_iota(jnp.int32, (L, L), 1)
            bias[t * L:(t + 1) * L] = jnp.where((key_pos <= query_pos) & (key_pos < length), 0.0, MASKED)
        tops = []
        for h in range(HEADS):
            s = nn(keys[:, pair(h)], head_rows(qT, h)) + bias[0:KB]
            s_scr[0:KB, h * L:(h + 1) * L] = s
            tops.append(jnp.max(jnp.max(s.reshape(KB // 8, 8, L), axis=0), axis=0, keepdims=True))
        for h in range(HEADS):
            hs = slice(h * HD, (h + 1) * HD)
            e = jnp.exp(s_scr[0:KB, h * L:(h + 1) * L] - tops[h])
            inv = 1.0 / jnp.sum(fold(e), axis=0, keepdims=True)
            low = e.astype(BF)
            v.e_scr[a, r, 0:KB, h * L:(h + 1) * L] = low
            v.linv[a, r, h] = jnp.broadcast_to(inv, (8, L))
            v.oT[a, r, hs] = (nn(VT[hs], low) * inv).astype(BF)

    def forward_all(bias, s_scr):
        hand_on(0, 0)

        @pl.loop(0, 2 * R)
        def _(n):
            a, r = lax.div(n, R), lax.rem(n, R)
            normed = v.nall[a, r, mine]
            qT = ((nt(v.wT[:D], normed) + wide(v.bcol[0], L)) * (HD ** -0.5)).astype(BF)
            v.qn[a, r] = qT.T
            v.qT[...] = qT
            gathered(a, r)
            with_size(functools.partial(forward_attention, a, r, bias, s_scr))

            @pl.when(n < 2 * R - 1)
            def _():
                hand_on(lax.div(n + 1, R), lax.rem(n + 1, R))

            middle = v.stream[r] + (nn(v.oT[a, r].T, v.wout[...]) + v.bout[...])
            xhat, rstd = normalise(middle)
            v.xh2[a, r] = xhat
            v.rs2[a, r] = jnp.broadcast_to(rstd, (L, 128))
            normed2 = (xhat * ln2g + ln2b).astype(BF)
            v.n2T[a, r] = normed2.T
            hidden, slope = gelu_parts(nn(normed2, v.wup[...]) + v.bup[...])
            hidden = hidden.astype(BF)
            v.hidden[a, r] = hidden
            v.slope[a, r] = slope
            v.stream[r] = middle + (nn(hidden, v.wdn[...]) + v.bdn[...])

            @pl.when(a == 0)
            def _():
                first_norm(1, r)
                announce(1, r)

            @pl.when(a == 1)
            def _():
                v.hid[r] = v.stream[r].astype(BF)
                v.gstream[r] = v.cot[r].astype(F32)
                out_copy(v, 0, v.hid, v.y, r).start()

    VM = pltpu.VMEM
    pl.run_scoped(forward_all, VM((S * L, L), F32), VM((S * L, HEADS * L), F32))
    pl.run_scoped(functools.partial(backward, v, with_size), VM((R, D, L), BF), VM((R, L, FF), BF), VM((R, L, D), BF),
                  VM((R, L, 3 * D), BF), VM((D, W), F32), VM((L, D), F32))

    for a in range(2):
        for r in range(R):
            each_send(a, r, lambda c: c.wait_send())

            @pl.loop(0, chip)
            def _(c):
                handed_on(a, r, c).wait_send()


def backward(v, with_size, gbT, gpre, ga_s, gqkv, dW, gns):
    S, DP, R, L, D, FF, W = v.S, v.DP, v.R, v.L, v.D, v.FF, v.W
    me, dp, mine = v.me, v.dp, v.mine
    v.dW = dW
    ln1g, ln2g = v.ln1g[...], v.ln2g[...]
    UP, DN, OW, QW = 0, FF, 2 * FF, 2 * FF + D
    V_LN1G, V_LN1B, V_QB, V_VB, V_OB, V_LN2G, V_LN2B, V_DB, V_UB = [D * k for k in range(9)]

    X, chip, core = v.X, v.chip, v.core

    def pair_copy(a, r, c):
        return pltpu.make_async_remote_copy(
            src_ref=v.pair_out.at[a, r, c], dst_ref=v.pair_in.at[a, r, c], send_sem=v.psend.at[0, a, r, c],
            recv_sem=v.precv.at[0, a, r, c], device_id=v.sibling, device_id_type=MESH)

    def part_copy(a, r, src, dst):
        return pltpu.make_async_remote_copy(
            src_ref=v.part_out.at[a, r, dst], dst_ref=v.part_in.at[a, r, src - 1], send_sem=v.psend.at[1, a, r, dst],
            recv_sem=v.precv.at[1, a, r, src], device_id=(dp, 2 * dst + core), device_id_type=MESH)

    def near_copy(a, r):
        return pltpu.make_async_remote_copy(
            src_ref=v.near_out.at[a, r], dst_ref=v.near_in.at[a, r], send_sem=v.nearsem.at[0, a, r],
            recv_sem=v.nearsem.at[1, a, r], device_id=v.sibling, device_id_type=MESH)

    def pass_on(a, r):
        @pl.loop(0, chip)
        def _(c):
            pair_copy(a, r, c).wait_recv()
            v.part_out[a, r, c] = (v.keep[r, c] + v.pair_in[a, r, c].astype(F32)).astype(BF)
            part_copy(a, r, chip, c).start()

    def add_vec(start, terms):
        v.vec[:, start:start + terms.shape[1]] += fold(terms)

    def backward_mlp(a, r):
        g = v.gstream[r]
        gb = g.astype(BF)
        add_vec(V_DB, gb.astype(F32))
        gbT[r] = gb.T
        pre = (nn(gb, v.wdnT[...]) * v.slope[a, r]).astype(BF)
        gpre[r] = pre
        add_vec(V_UB, pre.astype(F32))
        gn2 = nn(pre, v.wupT[...])
        xhat = v.xh2[a, r]
        add_vec(V_LN2G, gn2 * xhat)
        add_vec(V_LN2B, gn2)
        gm = g + norm_back(gn2, ln2g, xhat, wide(v.rs2[a, r], D))
        v.gmid[r] = gm
        ga = gm.astype(BF)
        ga_s[r] = ga
        add_vec(V_OB, ga.astype(F32))

    def attention_core(a, r, tick, nb):
        KB = nb * L
        gaT = nt(v.wout[...], ga_s[r]).astype(BF).astype(F32)
        oT = v.oT[a, r].astype(F32)
        scaled, deltas = [], []
        for h in range(HEADS):
            hs = slice(h * HD, (h + 1) * HD)
            part = gaT[hs] * v.linv[a, r, h, 0:1]
            scaled.append(part.astype(BF))
            deltas.append(jnp.sum(part * oT[hs], axis=0, keepdims=True))
        gaT_n = jnp.concatenate(scaled, axis=0)
        rows = v.nall[a, r, 0:KB, :]
        values = (nn(rows, v.wqkv[:, 2 * D:]) + v.qvb[1:2, :]).astype(BF)
        KT = nt(v.wT[D:2 * D], rows).astype(BF)
        gv = nn(v.e_scr[a, r, 0:KB, :], heads_apart(gaT_n.T))
        for h in range(HEADS):
            hl = slice(h * L, (h + 1) * L)
            gp = nn(values[:, pair(h)], head_rows(gaT_n, h))
            v.e_scr[a, r, 0:KB, hl] = (v.e_scr[a, r, 0:KB, hl].astype(F32) * (gp - deltas[h])).astype(BF)
        tick()
        gk = nn(v.e_scr[a, r, 0:KB, :], heads_apart(v.qn[a, r]))
        gkv = jnp.concatenate([gk, gv], axis=1).astype(BF)
        gqT = jnp.concatenate([nn(KT[h * HD:(h + 1) * HD], v.e_scr[a, r, 0:KB, h * L:(h + 1) * L]) for h in range(HEADS)], axis=0)
        pg = nn(gkv, v.wT[D:])
        for t in range(nb):
            block = pg[t * L:(t + 1) * L]
            if t // 2 < nb // 2 - 1:
                @pl.when((t // 2 < chip) & (t % 2 == core))
                def _():
                    v.keep[r, t // 2] = block

                @pl.when((t // 2 < chip) & (t % 2 != core))
                def _():
                    v.pair_out[a, r, t // 2] = block.astype(BF)
                    pair_copy(a, r, t // 2).start()

            if t % 2 == 0:
                @pl.when(t == me - 1)
                def _():
                    v.near_out[a, r] = block.astype(BF)
                    near_copy(a, r).start()

            @pl.when(t == me)
            def _():
                gqkv[r, :, D:] = gkv[t * L:(t + 1) * L]

        add_vec(V_VB, gkv[:, D:].astype(F32))
        dW[:, QW + D:QW + 3 * D] += nn(rows.T, gkv)
        gq = (gqT * (HD ** -0.5)).T.astype(BF)
        gqkv[r, :, :D] = gq
        add_vec(V_QB, gq.astype(F32))

    def backward_norm(a, r):
        gns[...] = nn(gqkv[r], v.wT[...])

        @pl.when(core == 0)
        def _():
            near_copy(a, r).wait_recv()
            gns[...] += v.near_in[a, r].astype(F32)

        @pl.loop(chip + 1, X)
        def _(c):
            part_copy(a, r, c, chip).wait_recv()
            gns[...] += v.part_in[a, r, c - 1].astype(F32)

        gn = gns[...]
        xhat = v.xh1[a, r]
        add_vec(V_LN1G, gn * xhat)
        add_vec(V_LN1B, gn)
        v.gstream[r] = v.gmid[r] + norm_back(gn, ln1g, xhat, wide(v.rs1[a, r], D))

    def put(first, start, value):
        if first:
            dW[:, start:start + value.shape[1]] = value
        else:
            dW[:, start:start + value.shape[1]] += value

    def weight_terms(a, rows, which):
        first = a == 1 and rows[0] == 0
        if "up" in which:
            put(first, UP, sum(nn(v.n2T[a, r], gpre[r]) for r in rows))
        if "down" in which:
            put(first, DN, sum(nn(gbT[r], v.hidden[a, r]) for r in rows))
            put(first, OW, sum(nn(v.oT[a, r], ga_s[r]) for r in rows))

    def query_terms(a):
        put(a == 1, QW, sum(nn(v.nall[a, r, mine].T, gqkv[r, :, :D]) for r in range(R)))

    every, early, last = tuple(range(R)), tuple(range(R - 1)), (R - 1,)
    dW[:, QW + D:QW + 3 * D] = jnp.zeros((D, 2 * D), F32)
    reducing = v.reduce_here
    if reducing:
        into = lambda p: tuple(getattr(v, f"{n}_{p}") for n in ("r1", "r2", "r3", "ss", "sr"))
        up, down, qkv = (Share(v, start, w, into(p)) for p, (start, w) in enumerate(((UP, FF), (DN, FF + D), (QW, 3 * D))))
        small = SmallSum(v)

    def nothing():
        pass

    def attention(a, r, tick):
        with_size(functools.partial(attention_core, a, r, tick if reducing else nothing))

    @pl.loop(0, R)
    def _(r):
        backward_mlp(1, r)

    weight_terms(1, every, ("up", "down"))

    @pl.loop(0, R)
    def _(r):
        attention(1, r, nothing)

        @pl.when(r > 0)
        def _():
            pass_on(1, r - 1)

    query_terms(1)
    pass_on(1, R - 1)

    def between(r):
        backward_norm(1, r)
        v.stream[r] = v.gstream[r]
        backward_mlp(0, r)

    pl.loop(0, R - 1)(between)
    if early:
        weight_terms(0, early, ("up", "down"))
    between(R - 1)
    weight_terms(0, last, ("up",))
    if reducing:
        up.start(1)
    weight_terms(0, last, ("down",))
    if reducing:
        down.start(1)

    def tick_first():
        up.step(1)
        down.step(1)

    def tick_last():
        up.step(2)

    for r in range(R):
        attention(0, r, tick_first if r == 0 else tick_last if r == R - 1 else nothing)
        if r > 0:
            pass_on(0, r - 1)
    if reducing:
        down.step(2)
    query_terms(0)
    if reducing:
        qkv.start(1)
    pass_on(0, R - 1)

    def final(r):
        backward_norm(0, r)
        v.gmid[r] = v.gstream[r] + v.stream[r]
        out_copy(v, 1, v.gstream, v.g1, r).start()
        out_copy(v, 2, v.gmid, v.ge, r).start()

    def small_lines():
        sums = jnp.sum(v.vec[...], axis=0, keepdims=True)
        return jnp.concatenate([sums[:, k * 128:(k + 1) * 128] for k in range(W // 128)], axis=0)

    if reducing:
        qkv.step(1)
        pl.loop(0, R - 1)(final)
        up.step(3)
        down.step(3)
        final(R - 1)
        small.start(0, small_lines())
        qkv.step(2)
        up.step(4)
        small.start(1, small.finish(0))
        down.step(4)
        qkv.step(3)
        small.start(2, small.finish(1))
        up.step(5)
        down.step(5)
        v.gv[...] = small.finish(2)
        qkv.step(4)
        up.finish(6)
        down.finish(6)
        gath_copy = lambda k, cols: pltpu.make_async_copy(v.gath.at[:, cols], v.gw.at[:, cols], v.gw_sem.at[k])
        first_out, second_out = gath_copy(0, slice(0, QW)), gath_copy(1, slice(QW, W))
        first_out.start()
        qkv.step(5)
        qkv.finish(6)
        second_out.start()
        first_out.wait()
        second_out.wait()
    else:
        pl.loop(0, R)(final)
        out = pltpu.make_async_copy(v.gath if v.reduce_here else dW, v.gw, v.gw_sem.at[0])
        out.start()
        out.wait()
        v.gv[...] = small_lines()

    for r in range(R):
        out_copy(v, 0, v.hid, v.y, r).wait()
        out_copy(v, 1, v.gstream, v.g1, r).wait()
        out_copy(v, 2, v.gmid, v.ge, r).wait()
        for a in range(2):
            @pl.loop(0, chip)
            def _(c):
                pair_copy(a, r, c).wait_send()
                part_copy(a, r, chip, c).wait_send()

            @pl.when(core == 1)
            def _():
                near_copy(a, r).wait_send()


def finish_kernel(D, FF, names, *refs):
    v = types.SimpleNamespace(**dict(zip(names, refs, strict=True)))
    load = lambda i, src, dst: pltpu.make_async_copy(src, dst, v.sems.at[0, i])
    save = lambda i, src, dst: pltpu.make_async_copy(src, dst, v.sems.at[1, i])
    loads = [load(0, v.gw, v.gw_s), load(1, v.gv, v.gv_s), load(2, v.g1, v.g1_s), load(3, v.ge, v.ge_s), load(4, v.y, v.y_s)]
    for c in loads:
        c.start()
    saves = []

    def keep(src, dst):
        saves.append(save(len(saves), src, dst))
        saves[-1].start()

    loads[0].wait()
    v.wup_s[...] = v.gw_s[:, 0:FF].astype(F32)
    keep(v.wup_s, v.wup)
    v.wdn_s[...] = v.gw_s[:, FF:2 * FF].T.astype(F32)
    keep(v.wdn_s, v.wdn)
    v.wqkv_s[...] = v.gw_s[:, 2 * FF + D:].astype(F32)
    keep(v.wqkv_s, v.wqkv)
    v.wout_s[...] = v.gw_s[:, 2 * FF:2 * FF + D].astype(F32)
    keep(v.wout_s, v.wout)
    for c, src, dst in zip(loads[2:], (v.g1_s, v.ge_s, v.y_s), (v.g1_o, v.ge_o, v.y_o)):
        c.wait()
        keep(src, dst)
    loads[1].wait()
    n = D // 128
    at = 0
    for ref, size in ((v.ln1g, n), (v.ln1b, n), (v.qvb, 2 * n), (v.bout, n), (v.ln2g, n), (v.ln2b, n), (v.bdn, n),
                      (v.bup, FF // 128)):
        for k in range(size):
            row, col = divmod(k, ref.shape[1] // 128)
            ref[row:row + 1, col * 128:(col + 1) * 128] = v.gv_s[at + k:at + k + 1, :]
        at += size
    for c in saves:
        c.wait()


def solution(mesh):
    S, DP = mesh.shape["seq"], mesh.shape["dp"]

    def shards(hidden_in, embedding, lengths, cotangent, ln1_gain, ln1_bias, qkv_weight, qv_bias, out_weight, out_bias,
               ln2_gain, ln2_bias, up_weight, up_bias, down_weight, down_bias):
        L, R, D = hidden_in.shape
        FF = up_weight.shape[1]
        W = 4 * D + 2 * FF
        X, Z = S // 2, DP // 2
        parts = (FF, FF + D, 3 * D)
        h2 = D // 2 // S
        groups = max(h2 // 16, 1)
        reduce_here = (DP % 2 == 0 and Z > 1 and D % (2 * S * 16) == 0 and Z % groups == 0
                       and all(w * groups % (128 * Z) == 0 for w in parts))
        cfg = (S, DP, R, L, D, FF, reduce_here)
        VM = pltpu.VMEM
        DMA = pltpu.SemaphoreType.DMA
        scratch = dict(
            wT=VM((3 * D, D), BF), wupT=VM((FF, D), BF), wdnT=VM((D, FF), BF), bcol=VM((2, D, 128), F32),
            stream=VM((R, L, D), F32), gstream=VM((R, L, D), F32), gmid=VM((R, L, D), F32), nall=VM((2, R, S * L, D), BF), xh1=VM((2, R, L, D), F32), rs1=VM((2, R, L, 128), F32),
            xh2=VM((2, R, L, D), F32), rs2=VM((2, R, L, 128), F32), n2T=VM((2, R, D, L), BF), qT=VM((D, L), BF),
            qn=VM((2, R, L, D), BF), linv=VM((2, R, HEADS, 8, L), F32), oT=VM((2, R, D, L), BF),
            hidden=VM((2, R, L, FF), BF), slope=VM((2, R, L, FF), F32), e_scr=VM((2, R, S * L, HEADS * L), BF),
            pair_out=VM((2, R, X - 1, L, D), BF), pair_in=VM((2, R, X - 1, L, D), BF), part_out=VM((2, R, X - 1, L, D), BF),
            part_in=VM((2, R, X - 1, L, D), BF), near_out=VM((2, R, L, D), BF), near_in=VM((2, R, L, D), BF),
            keep=VM((R, X - 1, L, D), F32), vec=VM((8, W), F32),
            nsend=DMA((2, R, X + 1)), fsend=DMA((2, R, X)), nrecv=DMA((2, R, S)), psend=DMA((2, 2, R, X)), precv=DMA((2, 2, R, X)),
            nearsem=DMA((2, 2, R)), out_sems=DMA((3, R)), gw_sem=DMA((2,)), in_sem=DMA((len(LOADS),)))
        if reduce_here:
            lines = W // 128
            scratch.update(
                stage=VM((D, W), BF), gath=VM((D, W), BF), vs1=VM((2, lines, 128), F32), vs2=VM((S, lines, 128), F32),
                vs3=VM((Z, lines, 128), F32), vss1=DMA((1,)), vsr1=DMA((1,)), vss2=DMA((S - 1,)), vsr2=DMA((S - 1,)),
                vss3=DMA((Z - 1,)), vsr3=DMA((Z - 1,)))
            most = max(S, Z) - 1
            for p, w in enumerate(parts):
                scratch.update({
                    f"r1_{p}": VM((D // 2, w), BF), f"r2_{p}": VM((S - 1, h2, w), BF), f"r3_{p}": VM((Z - 1, 16, w * groups // Z), BF),
                    f"ss_{p}": DMA((6, most)), f"sr_{p}": DMA((6, most))})
        vm = pl.BlockSpec(memory_space=pltpu.VMEM)
        sm = pl.BlockSpec(memory_space=pltpu.SMEM)
        hbm = pl.BlockSpec(memory_space=pl.ANY)
        rows_first = lambda x: jnp.transpose(x, (1, 0, 2))
        line = lambda x: x.reshape(1, -1)
        ins = dict(
            hid=rows_first(hidden_in), emb=rows_first(embedding), cot=rows_first(cotangent), lengths=lengths, ln1g=line(ln1_gain),
            ln1b=line(ln1_bias), wqkv=qkv_weight, qvb=qv_bias, wout=out_weight, bout=line(out_bias), ln2g=line(ln2_gain),
            ln2b=line(ln2_bias), wup=up_weight, bup=line(up_bias), wdn=down_weight, bdn=line(down_bias))
        shape = jax.ShapeDtypeStruct
        outs = dict(
            y=shape((R, L, D), BF), g1=shape((R, L, D), F32), ge=shape((R, L, D), F32),
            gw=shape((D, W), BF if reduce_here else F32), gv=shape((W // 128, 128), F32))
        scratch.update({n: VM(ins[n].shape, ins[n].dtype) for n in LOADS})
        names = (*(n if n == "lengths" else n + "_in" for n in ins), *outs, *scratch)
        y, g1, ge, gw, gv = pl.pallas_call(
            functools.partial(block_kernel, cfg, names), out_shape=tuple(outs.values()),
            in_specs=[sm if n == "lengths" else hbm for n in ins], out_specs=tuple(vm if n == "gv" else hbm for n in outs),
            scratch_shapes=list(scratch.values()),
            compiler_params=pltpu.CompilerParams(collective_id=0, has_side_effects=True, vmem_limit_bytes=VMEM_LIMIT),
        )(*ins.values())
        if not reduce_here:
            gw, gv = lax.psum((gw, gv), ("dp", "seq"))
        full = [shape((R, L, D), BF), shape((R, L, D), F32), shape((R, L, D), F32), shape((1, D), F32), shape((1, D), F32),
                shape((D, 3 * D), F32), shape((2, D), F32), shape((D, D), F32), shape((1, D), F32), shape((1, D), F32),
                shape((1, D), F32), shape((D, FF), F32), shape((1, FF), F32), shape((FF, D), F32), shape((1, D), F32)]
        ends = ["y_o", "g1_o", "ge_o", "ln1g", "ln1b", "wqkv", "qvb", "wout", "bout", "ln2g", "ln2b", "wup", "bup", "wdn", "bdn"]
        large = ("y_o", "g1_o", "ge_o", "wqkv", "wout", "wup", "wdn")
        temps = dict(
            y_s=VM((R, L, D), BF), g1_s=VM((R, L, D), F32), ge_s=VM((R, L, D), F32), gw_s=VM((D, W), gw.dtype),
            gv_s=VM((W // 128, 128), F32), wup_s=VM((D, FF), F32), wdn_s=VM((FF, D), F32), wqkv_s=VM((D, 3 * D), F32),
            wout_s=VM((D, D), F32), sems=DMA((2, 7)))
        res = pl.pallas_call(
            functools.partial(finish_kernel, D, FF, (*outs, *ends, *temps)), out_shape=full, in_specs=[hbm] * 5,
            out_specs=[hbm if n in large else vm for n in ends], scratch_shapes=list(temps.values()),
            compiler_params=pltpu.CompilerParams(vmem_limit_bytes=VMEM_LIMIT))(y, g1, ge, gw, gv)
        flat = (3, 4, 8, 9, 10, 12, 14)
        return tuple(rows_first(x) if i < 3 else x.reshape(-1) if i in flat else x for i, x in enumerate(res))

    token = P("seq", "dp", None)
    return jax.shard_map(
        shards, mesh=mesh, in_specs=(token, token, P("dp"), token) + (P(),) * 12, out_specs=(token,) * 3 + (P(),) * 12,
        check_vma=False)
```

```python
import functools
import types

import jax
import jax.numpy as jnp
from jax import lax
from jax.experimental import pallas as pl
from jax.experimental.pallas import tpu as pltpu
from jax.sharding import PartitionSpec as P

EPS = 1e-05
MASKED = -1e30
HEADS = 4
HD = 64
BF = jnp.bfloat16
F32 = jnp.float32
MESH = pl.DeviceIdType.MESH
VMEM_LIMIT = 61 * 1024 * 1024


def nn(a, b):
    return lax.dot_general(a, b, (((1,), (0,)), ((), ())), preferred_element_type=F32)


def nt(a, b):
    return lax.dot_general(a, b, (((1,), (1,)), ((), ())), preferred_element_type=F32)


def normalise(x):
    mean = jnp.mean(x, axis=-1, keepdims=True)
    centred = x - mean
    rstd = lax.rsqrt(jnp.mean(centred * centred, axis=-1, keepdims=True) + EPS)
    return centred * rstd, rstd


def norm_back(grad, gain, xhat, rstd):
    gl = grad * gain
    m1 = jnp.mean(gl, axis=-1, keepdims=True)
    m2 = jnp.mean(gl * xhat, axis=-1, keepdims=True)
    return rstd * (gl - m1 - xhat * m2)


def fold(x):
    return jnp.sum(x.reshape(x.shape[0] // 8, 8, x.shape[1]), axis=0)


def gelu_parts(x):
    c0 = 0.7978845608028654
    c1 = c0 * 0.044715
    x2 = x * x
    half = 0.5 + 0.5 * jnp.tanh(x * (c0 + c1 * x2))
    slope = half + (half * (1.0 - half)) * (x * (2 * c0 + (6 * c1) * x2))
    return x * half, slope


def head_rows(x, h):
    own = x[h * HD:(h + 1) * HD]
    zero = jnp.zeros_like(own)
    return jnp.concatenate([own, zero] if h % 2 == 0 else [zero, own], axis=0)


def pair(h):
    return slice((h // 2) * 2 * HD, (h // 2 + 1) * 2 * HD)


def heads_apart(x):
    lane = lax.broadcasted_iota(jnp.int32, x.shape, 1)
    return jnp.concatenate(
        [jnp.where((lane >= h * HD) & (lane < (h + 1) * HD), x, jnp.zeros((), x.dtype)) for h in range(HEADS)], axis=0)


def wide(x, n):
    return jnp.concatenate([x] * (n // 128), axis=1)


class Share:
    def __init__(self, v, start, w, into, stages, whole_last):
        self.v, self.stages, self.whole = v, stages, whole_last
        self.bufs, self.send, self.recv = into
        self.down = len(stages)
        self.steps = 2 * self.down - (1 if whole_last else 0)
        self.plan = share_plan(v.D, w, [n for n, _, _ in stages], whole_last)
        base = (0, start)
        self.bases = [base]
        for k, (n, own, _) in enumerate(stages):
            base = self.part(k, own)[0]
            self.bases.append(base)

    def part(self, k, number):
        rows, lanes, row_parts, _ = self.plan[k]
        r, c = self.bases[k]
        if row_parts == 1:
            return (r, c + number * lanes), (rows, lanes)
        return (r + lax.rem(number, row_parts) * rows, c + lax.div(number, row_parts) * lanes), (rows, lanes)

    def window(self, base, size):
        r, c = base
        at = c if isinstance(c, int) else pl.multiple_of(c, 128)
        return pl.ds(pl.multiple_of(r, 16) if not isinstance(r, int) else r, size[0]), pl.ds(at, size[1])

    def region(self, k):
        rows, lanes, row_parts, lane_parts = self.plan[k]
        return self.window(self.bases[k], (rows * row_parts, lanes * lane_parts))

    def copies(self, i):
        v = self.v
        k = i if i < self.down else 2 * self.down - 1 - i - (1 if self.whole else 0)
        n, own, device = self.stages[k]
        out = []
        for j in range(1, n):
            other = lax.rem(own + j, n)
            if i == self.down - 1 and self.whole:
                out.append((v.stage.at[self.region(k)], self.bufs[k].at[own], device(other)))
            elif i < self.down:
                out.append((v.stage.at[self.window(*self.part(k, other))], self.bufs[k].at[j - 1], device(other)))
            else:
                ref = v.gath.at[self.window(*self.part(k, own))]
                out.append((ref, ref, device(other)))
        return out

    def made(self, i):
        return [pltpu.make_async_remote_copy(src_ref=s, dst_ref=d, send_sem=self.send.at[i, j], recv_sem=self.recv.at[i, j],
                                             device_id=dev, device_id_type=MESH)
                for j, (s, d, dev) in enumerate(self.copies(i))]

    def start(self, i):
        v = self.v
        if i == 0:
            n, own, _ = self.stages[0]
            for j in range(1, n):
                there = self.window(*self.part(0, lax.rem(own + j, n)))
                v.stage[there] = v.dW[there].astype(BF)
        for c in self.made(i):
            c.start()

    def finish(self, i):
        v = self.v
        for c in self.made(i):
            c.wait()
        if i >= self.down:
            return
        n, own, _ = self.stages[i]
        if i == self.down - 1 and self.whole:
            at = self.region(i)
            self.bufs[i][own] = v.stage[at]
            total = self.bufs[i][0].astype(F32)
            for j in range(1, n):
                total = total + self.bufs[i][j].astype(F32)
        else:
            at = self.window(*self.part(i, own))
            total = v.dW[at]
            for j in range(n - 1):
                total = total + self.bufs[i][j].astype(F32)
        if i == self.down - 1:
            v.gath[at] = total.astype(BF)
        else:
            v.dW[at] = total
            v.stage[at] = total.astype(BF)

    def step(self, i):
        self.finish(i)
        if i + 1 < self.steps:
            self.start(i + 1)


def share_plan(D, w, members, whole_last):
    rows, lanes, plan = D, w, []
    for k, n in enumerate(members):
        if whole_last and k == len(members) - 1:
            plan.append((rows, lanes, 1, 1))
            continue
        row_parts = max(p for p in range(1, n + 1) if n % p == 0 and rows % (16 * p) == 0)
        lane_parts = n // row_parts
        if lanes % (128 * lane_parts):
            return None
        rows, lanes = rows // row_parts, lanes // lane_parts
        plan.append((rows, lanes, row_parts, lane_parts))
    return plan


def part_shapes(D, w, members, whole_last):
    shapes = []
    for k, (n, (rows, lanes, rp, lp)) in enumerate(zip(members, share_plan(D, w, members, whole_last))):
        whole = whole_last and k == len(members) - 1
        shapes.append((n if whole else n - 1, rows, lanes))
    return shapes


class SmallSum:
    def __init__(self, v):
        self.v = v
        self.stages = [(v.vs1, v.core, 2, lambda other: v.sibling, v.vss1, v.vsr1),
                       (v.vs2, v.spot2, v.S, v.in_plane, v.vss2, v.vsr2), (v.vs3, v.spot3, v.DP // 2, v.across, v.vss3, v.vsr3)]

    def copies(self, i):
        buf, spot, n, device, send, recv = self.stages[i]
        return [pltpu.make_async_remote_copy(
            src_ref=buf.at[spot], dst_ref=buf.at[spot], send_sem=send.at[k - 1], recv_sem=recv.at[k - 1],
            device_id=device(lax.rem(spot + k, n)), device_id_type=MESH) for k in range(1, n)]

    def start(self, i, value):
        buf, spot = self.stages[i][:2]
        buf[spot] = value
        for c in self.copies(i):
            c.start()

    def finish(self, i):
        for c in self.copies(i):
            c.wait()
        buf, n = self.stages[i][0], self.stages[i][2]
        total = buf[0]
        for s in range(1, n):
            total = total + buf[s]
        return total


def out_copy(v, which, src, dst, r):
    return pltpu.make_async_copy(src.at[r], dst.at[r], v.out_sems.at[which, r])


LOADS = ("hid", "emb", "ln1g", "ln1b", "wqkv", "qvb", "wup", "wdn", "wout", "bout", "ln2g", "ln2b", "bup", "bdn", "cot")


def block_kernel(cfg, names, *refs):
    S, DP, R, L, D, FF, reduce_here = cfg
    W = 4 * D + 2 * FF
    v = types.SimpleNamespace(**dict(zip(names, refs, strict=True)))
    v.S, v.DP, v.R, v.L, v.D, v.FF, v.W, v.reduce_here = S, DP, R, L, D, FF, W, reduce_here
    v.me, v.dp = me, dp = lax.axis_index("seq"), lax.axis_index("dp")
    v.chip, v.core = chip, core = lax.div(me, 2), lax.rem(me, 2)
    X = v.X = S // 2
    v.mine = mine = pl.ds(pl.multiple_of(me * L, L), L)
    v.sibling = (dp, me + 1 - 2 * core)
    sizes = (S // 2, S)

    def with_size(body):
        low = 0
        for n in sizes:
            pl.when((me >= low) & (me < n))(functools.partial(body, n))
            low = n

    barrier = pltpu.get_barrier_semaphore()
    peers = [v.sibling] + [(dp, lax.rem(me + 2 * k, S)) for k in range(1, X)]
    if reduce_here:
        v.spot2, v.spot3 = chip * 2 + lax.rem(dp, 2), lax.div(dp, 2)
        v.in_plane = lambda n: (lax.div(dp, 2) * 2 + lax.rem(n, 2), lax.div(n, 2) * 2 + core)
        v.across = lambda n: (n * 2 + lax.rem(dp, 2), me)
        peers += [(dp + 1 - 2 * lax.rem(dp, 2), lax.rem(me + 2 * k, S)) for k in range(X)]
        peers += [v.across(lax.rem(v.spot3 + k, DP // 2)) for k in range(1, DP // 2)]
    for peer in peers:
        pl.semaphore_signal(barrier, inc=1, device_id=peer, device_id_type=MESH)

    brought = {}
    for k, name in enumerate(LOADS):
        brought[name] = pltpu.make_async_copy(getattr(v, name + "_in"), getattr(v, name), v.in_sem.at[k])
        brought[name].start()

    def need(*which):
        for name in which:
            brought.pop(name).wait()

    v.need = need

    def block_of(a, r, t):
        return v.nall.at[a, r, pl.ds(pl.multiple_of(t * L, L), L)]

    def normed_copy(a, r, t, send_sem, dst):
        ref = block_of(a, r, t)
        return pltpu.make_async_remote_copy(
            src_ref=ref, dst_ref=ref, send_sem=send_sem, recv_sem=v.nrecv.at[a, r, t], device_id=(dp, dst), device_id_type=MESH)

    def to_chip(a, r, c):
        return normed_copy(a, r, me, v.nsend.at[a, r, c], 2 * c + core)

    def to_sibling(a, r):
        return normed_copy(a, r, me, v.nsend.at[a, r, X], me + 1 - 2 * core)

    def handed_on(a, r, c):
        return normed_copy(a, r, 2 * c + core, v.fsend.at[a, r, c], me + 1 - 2 * core)

    def each_send(a, r, action):
        @pl.loop(chip + 1, X)
        def _(c):
            action(to_chip(a, r, c))

        @pl.when(core == 0)
        def _():
            action(to_sibling(a, r))

    def first_norm(a, r):
        u = v.stream[r] + v.emb[r].astype(F32)
        v.stream[r] = u
        xhat, rstd = normalise(u)
        v.xh1[a, r] = xhat
        v.rs1[a, r] = jnp.broadcast_to(rstd, (L, 128))
        v.nall[a, r, mine] = (xhat * ln1g + ln1b).astype(BF)

    def announce(a, r):
        each_send(a, r, lambda c: c.start())

    def hand_on(a, r):
        @pl.loop(0, chip)
        def _(c):
            handed_on(a, r, c).wait_recv()
            handed_on(a, r, c).start()

    def gathered(a, r):
        @pl.loop(0, chip)
        def _(c):
            normed_copy(a, r, 2 * c + 1 - core, v.fsend.at[a, r, c], me).wait_recv()

        @pl.when(core == 1)
        def _():
            normed_copy(a, r, me - 1, v.nsend.at[a, r, X], me).wait_recv()

    @pl.loop(me + 1, S)
    def _(t):
        for a in range(2):
            for r in range(R):
                v.nall[a, r, pl.ds(pl.multiple_of(t * L, L), L)] = jnp.zeros((L, D), BF)

    v.vec[...] = jnp.zeros_like(v.vec)
    need("hid", "emb", "ln1g", "ln1b")
    ln1g, ln1b = v.ln1g[...], v.ln1b[...]

    @pl.loop(0, R)
    def _(r):
        v.stream[r] = v.hid[r].astype(F32)
        first_norm(0, r)

    need("wqkv", "qvb")
    for k in range(3):
        v.wT[k * D:(k + 1) * D] = v.wqkv[:, k * D:(k + 1) * D].T
    for k in range(2):
        v.bcol[k] = jnp.broadcast_to(v.qvb[k:k + 1, :], (128, D)).T
    need("wup", "wdn")
    for k in range(FF // D):
        ks = slice(k * D, (k + 1) * D)
        v.wupT[ks] = v.wup[:, ks].T
        v.wdnT[:, ks] = v.wdn[ks].T

    pl.semaphore_wait(barrier, len(peers))
    for r in range(R):
        announce(0, r)

    need("wout", "bout", "ln2g", "ln2b", "bup", "bdn", "cot")
    ln2g, ln2b = v.ln2g[...], v.ln2b[...]

    def forward_attention(a, r, bias, s_scr, nb):
        KB = nb * L
        length = v.lengths[r]
        rows = v.nall[a, r, 0:KB, :]
        keys = nn(rows, v.wqkv[:, D:2 * D]).astype(BF)
        qT = v.qT[...]
        for t in range(nb):
            key_pos = t * L + lax.broadcasted_iota(jnp.int32, (L, L), 0)
            query_pos = me * L + lax.broadcasted_iota(jnp.int32, (L, L), 1)
            bias[t * L:(t + 1) * L] = jnp.where((key_pos <= query_pos) & (key_pos < length), 0.0, MASKED)
        tops = []
        for h in range(HEADS):
            s = nn(keys[:, pair(h)], head_rows(qT, h)) + bias[0:KB]
            s_scr[0:KB, h * L:(h + 1) * L] = s
            tops.append(jnp.max(jnp.max(s.reshape(KB // 8, 8, L), axis=0), axis=0, keepdims=True))
        VT = (nt(v.wT[2 * D:], rows) + wide(v.bcol[1], KB)).astype(BF)
        for h in range(HEADS):
            hs, hl = slice(h * HD, (h + 1) * HD), slice(h * L, (h + 1) * L)
            sums, out = [], []
            for t in range(nb):
                ts = slice(t * L, (t + 1) * L)
                e = jnp.exp(s_scr[ts, hl] - tops[h])
                sums.append(fold(e))
                low = e.astype(BF)
                v.e_scr[a, r, ts, hl] = low
                out.append(nn(VT[hs, ts], low))
            inv = 1.0 / jnp.sum(sum(sums), axis=0, keepdims=True)
            v.linv[a, r, h] = jnp.broadcast_to(inv, (8, L))
            v.oT[a, r, hs] = (sum(out) * inv).astype(BF)

    def forward_all(bias, s_scr):
        hand_on(0, 0)

        @pl.loop(0, 2 * R)
        def _(n):
            a, r = lax.div(n, R), lax.rem(n, R)
            normed = v.nall[a, r, mine]
            qT = ((nt(v.wT[:D], normed) + wide(v.bcol[0], L)) * (HD ** -0.5)).astype(BF)
            v.qn[a, r] = qT.T
            v.qT[...] = qT
            gathered(a, r)
            with_size(functools.partial(forward_attention, a, r, bias, s_scr))

            @pl.when(n < 2 * R - 1)
            def _():
                hand_on(lax.div(n + 1, R), lax.rem(n + 1, R))

            middle = v.stream[r] + (nn(v.oT[a, r].T, v.wout[...]) + v.bout[...])
            xhat, rstd = normalise(middle)
            v.xh2[a, r] = xhat
            v.rs2[a, r] = jnp.broadcast_to(rstd, (L, 128))
            normed2 = (xhat * ln2g + ln2b).astype(BF)
            v.n2T[a, r] = normed2.T
            hidden, slope = gelu_parts(nn(normed2, v.wup[...]) + v.bup[...])
            hidden = hidden.astype(BF)
            v.hidden[a, r] = hidden
            v.slope[a, r] = slope
            v.stream[r] = middle + (nn(hidden, v.wdn[...]) + v.bdn[...])

            @pl.when(a == 0)
            def _():
                first_norm(1, r)
                announce(1, r)

            @pl.when(a == 1)
            def _():
                v.hid[r] = v.stream[r].astype(BF)
                v.gstream[r] = v.cot[r].astype(F32)
                out_copy(v, 0, v.hid, v.y, r).start()

    VM = pltpu.VMEM
    pl.run_scoped(forward_all, VM((S * L, L), F32), VM((S * L, HEADS * L), F32))
    pl.run_scoped(functools.partial(backward, v, with_size), VM((R, D, L), BF), VM((R, L, FF), BF), VM((R, L, D), BF),
                  VM((R, L, 3 * D), BF), VM((D, W), F32), VM((L, D), F32),
                  VM((S * L, D), BF), VM((S * L, 2 * D), BF))

    for a in range(2):
        for r in range(R):
            each_send(a, r, lambda c: c.wait_send())

            @pl.loop(0, chip)
            def _(c):
                handed_on(a, r, c).wait_send()


def backward(v, with_size, gbT, gpre, ga_s, gqkv, dW, gns, pg_s, gkv_s):
    S, DP, R, L, D, FF, W = v.S, v.DP, v.R, v.L, v.D, v.FF, v.W
    me, dp, mine = v.me, v.dp, v.mine
    v.dW = dW
    ln1g, ln2g = v.ln1g[...], v.ln2g[...]
    UP, DN, OW, QW = 0, FF, 2 * FF, 2 * FF + D
    V_LN1G, V_LN1B, V_QB, V_VB, V_OB, V_LN2G, V_LN2B, V_DB, V_UB = [D * k for k in range(9)]

    X, chip, core = v.X, v.chip, v.core

    def pair_copy(a, r, c):
        return pltpu.make_async_remote_copy(
            src_ref=v.pair_out.at[r, c], dst_ref=v.pair_in.at[a, r, c], send_sem=v.psend.at[0, a, r, c],
            recv_sem=v.precv.at[0, a, r, c], device_id=v.sibling, device_id_type=MESH)

    def part_copy(a, r, src, dst):
        return pltpu.make_async_remote_copy(
            src_ref=v.part_out.at[r, dst], dst_ref=v.part_in.at[a, r, src - 1], send_sem=v.psend.at[1, a, r, dst],
            recv_sem=v.precv.at[1, a, r, src], device_id=(dp, 2 * dst + core), device_id_type=MESH)

    def near_copy(a, r):
        return pltpu.make_async_remote_copy(
            src_ref=v.near_out.at[r], dst_ref=v.near_in.at[a, r], send_sem=v.nearsem.at[0, a, r],
            recv_sem=v.nearsem.at[1, a, r], device_id=v.sibling, device_id_type=MESH)

    def pass_on(a, r):
        @pl.loop(0, chip)
        def _(c):
            pair_copy(a, r, c).wait_recv()
            v.part_out[r, c] = (v.keep[r, c].astype(F32) + v.pair_in[a, r, c].astype(F32)).astype(BF)
            part_copy(a, r, chip, c).start()

    def sent(a):
        for r in range(R):
            @pl.loop(0, chip)
            def _(c):
                pair_copy(a, r, c).wait_send()
                part_copy(a, r, chip, c).wait_send()

            @pl.when(core == 1)
            def _():
                near_copy(a, r).wait_send()

    def add_vec(start, terms):
        v.vec[:, start:start + terms.shape[1]] += fold(terms)

    def backward_mlp(a, r):
        g = v.gstream[r]
        gb = g.astype(BF)
        add_vec(V_DB, gb.astype(F32))
        gbT[r] = gb.T
        pre = (nn(gb, v.wdnT[...]) * v.slope[a, r]).astype(BF)
        gpre[r] = pre
        add_vec(V_UB, pre.astype(F32))
        gn2 = nn(pre, v.wupT[...])
        xhat = v.xh2[a, r]
        add_vec(V_LN2G, gn2 * xhat)
        add_vec(V_LN2B, gn2)
        gm = g + norm_back(gn2, ln2g, xhat, wide(v.rs2[a, r], D))
        v.gmid[r] = gm
        ga = gm.astype(BF)
        ga_s[r] = ga
        add_vec(V_OB, ga.astype(F32))

    def attention_core(a, r, tick, nb):
        KB = nb * L
        gaT = nt(v.wout[...], ga_s[r]).astype(BF).astype(F32)
        oT = v.oT[a, r].astype(F32)
        scaled, deltas = [], []
        for h in range(HEADS):
            hs = slice(h * HD, (h + 1) * HD)
            part = gaT[hs] * v.linv[a, r, h, 0:1]
            scaled.append(part.astype(BF))
            deltas.append(jnp.sum(part * oT[hs], axis=0, keepdims=True))
        gaT_n = jnp.concatenate(scaled, axis=0)
        rows = v.nall[a, r, 0:KB, :]
        values = (nn(rows, v.wqkv[:, 2 * D:]) + v.qvb[1:2, :]).astype(BF)
        KT = nt(v.wT[D:2 * D], rows).astype(BF)
        blocks = [slice(t * L, (t + 1) * L) for t in range(nb)]
        ga_apart, q_apart = heads_apart(gaT_n.T), heads_apart(v.qn[a, r])
        for ts in blocks:
            gkv_s[ts, D:] = nn(v.e_scr[a, r, ts, :], ga_apart).astype(BF)
        for h in range(HEADS):
            hl = slice(h * L, (h + 1) * L)
            gp = nn(values[:, pair(h)], head_rows(gaT_n, h))
            v.e_scr[a, r, 0:KB, hl] = (v.e_scr[a, r, 0:KB, hl].astype(F32) * (gp - deltas[h])).astype(BF)
        tick()
        for ts in blocks:
            gkv_s[ts, :D] = nn(v.e_scr[a, r, ts, :], q_apart).astype(BF)
        for ts in blocks:
            pg_s[ts] = nn(gkv_s[ts, :], v.wT[D:]).astype(BF)
        for t in range(nb):
            ts = blocks[t]
            if t // 2 < nb // 2 - 1:
                @pl.when((t // 2 < chip) & (t % 2 == core))
                def _():
                    v.keep[r, t // 2] = pg_s[ts]

                @pl.when((t // 2 < chip) & (t % 2 != core))
                def _():
                    v.pair_out[r, t // 2] = pg_s[ts]
                    pair_copy(a, r, t // 2).start()

            if t % 2 == 0:
                @pl.when(t == me - 1)
                def _():
                    v.near_out[r] = pg_s[ts]
                    near_copy(a, r).start()

            @pl.when(t == me)
            def _():
                gqkv[r, :, D:] = gkv_s[ts]

        add_vec(V_VB, gkv_s[0:KB, D:].astype(F32))
        gqT = jnp.concatenate([nn(KT[h * HD:(h + 1) * HD], v.e_scr[a, r, 0:KB, h * L:(h + 1) * L]) for h in range(HEADS)], axis=0)
        dW[:, QW + D:QW + 3 * D] += nn(rows.T, gkv_s[0:KB])
        gq = (gqT * (HD ** -0.5)).T.astype(BF)
        gqkv[r, :, :D] = gq
        add_vec(V_QB, gq.astype(F32))

    def backward_norm(a, r):
        gns[...] = nn(gqkv[r], v.wT[...])

        @pl.when(core == 0)
        def _():
            near_copy(a, r).wait_recv()
            gns[...] += v.near_in[a, r].astype(F32)

        @pl.loop(chip + 1, X)
        def _(c):
            part_copy(a, r, c, chip).wait_recv()
            gns[...] += v.part_in[a, r, c - 1].astype(F32)

        gn = gns[...]
        xhat = v.xh1[a, r]
        add_vec(V_LN1G, gn * xhat)
        add_vec(V_LN1B, gn)
        v.gstream[r] = v.gmid[r] + norm_back(gn, ln1g, xhat, wide(v.rs1[a, r], D))

    def put(first, start, value):
        if first:
            dW[:, start:start + value.shape[1]] = value
        else:
            dW[:, start:start + value.shape[1]] += value

    def weight_terms(a, rows, which):
        first = a == 1 and rows[0] == 0
        if "up" in which:
            put(first, UP, sum(nn(v.n2T[a, r], gpre[r]) for r in rows))
        if "down" in which:
            put(first, DN, sum(nn(gbT[r], v.hidden[a, r]) for r in rows))
            put(first, OW, sum(nn(v.oT[a, r], ga_s[r]) for r in rows))

    def query_terms(a):
        put(a == 1, QW, sum(nn(v.nall[a, r, mine].T, gqkv[r, :, :D]) for r in range(R)))

    every, early, last = tuple(range(R)), tuple(range(R - 1)), (R - 1,)
    dW[:, QW + D:QW + 3 * D] = jnp.zeros((D, 2 * D), F32)
    reducing = v.reduce_here
    if reducing:
        pair_stage = (2, core, lambda n: v.sibling)
        plane, across = (S, v.spot2, v.in_plane), (DP // 2, v.spot3, v.across)
        into = lambda p: ([getattr(v, f"b{k}_{p}") for k in range(3)], getattr(v, f"ss_{p}"), getattr(v, f"sr_{p}"))
        up, down, qkv = (Share(v, start, w, into(p), (pair_stage, plane, across), whole)
                         for p, (start, w, whole) in enumerate(((UP, FF, False), (DN, FF + D, False), (QW, 3 * D, True))))
        small = SmallSum(v)

    def nothing():
        pass

    def attention(a, r, tick):
        with_size(functools.partial(attention_core, a, r, tick if reducing else nothing))

    for r in range(R):
        backward_mlp(1, r)

    weight_terms(1, every, ("up", "down"))

    @pl.loop(0, R)
    def _(r):
        attention(1, r, nothing)

        @pl.when(r > 0)
        def _():
            pass_on(1, r - 1)

    query_terms(1)
    pass_on(1, R - 1)

    def between(r):
        backward_norm(1, r)
        v.stream[r] = v.gstream[r]
        backward_mlp(0, r)

    for r in range(R - 1):
        between(r)
    if early:
        weight_terms(0, early, ("up", "down"))
    between(R - 1)
    weight_terms(0, last, ("up",))
    if reducing:
        up.start(0)
    weight_terms(0, last, ("down",))
    if reducing:
        down.start(0)

    sent(1)

    def tick_first():
        up.step(0)
        down.step(0)

    def tick_last():
        up.step(1)

    for r in range(R):
        attention(0, r, tick_first if r == 0 else tick_last if r == R - 1 else nothing)
        if r > 0:
            pass_on(0, r - 1)
    query_terms(0)
    if reducing:
        qkv.start(0)
    pass_on(0, R - 1)
    if reducing:
        down.step(1)

    def final(r):
        backward_norm(0, r)
        v.gmid[r] = v.gstream[r] + v.stream[r]
        out_copy(v, 1, v.gstream, v.g1, r).start()
        out_copy(v, 2, v.gmid, v.ge, r).start()

    def small_lines():
        sums = jnp.sum(v.vec[...], axis=0, keepdims=True)
        return jnp.concatenate([sums[:, k * 128:(k + 1) * 128] for k in range(W // 128)], axis=0)

    if reducing:
        gath_copy = lambda k, cols: pltpu.make_async_copy(v.gath.at[:, cols], v.gw.at[:, cols], v.gw_sem.at[k])
        first_out, second_out = gath_copy(0, slice(0, QW)), gath_copy(1, slice(QW, W))
        qkv.step(0)
        for r in range(R - 1):
            final(r)
        up.step(2)
        qkv.step(1)
        down.step(2)
        final(R - 1)
        small.start(0, small_lines())
        up.step(3)
        small.start(1, small.finish(0))
        qkv.step(2)
        down.step(3)
        small.start(2, small.finish(1))
        up.step(4)
        qkv.step(3)
        down.step(4)
        v.gv[...] = small.finish(2)
        up.finish(5)
        down.finish(5)
        first_out.start()
        qkv.finish(4)
        second_out.start()
        first_out.wait()
        second_out.wait()
    else:
        pl.loop(0, R)(final)
        out = pltpu.make_async_copy(v.gath if v.reduce_here else dW, v.gw, v.gw_sem.at[0])
        out.start()
        out.wait()
        v.gv[...] = small_lines()

    for r in range(R):
        out_copy(v, 0, v.hid, v.y, r).wait()
        out_copy(v, 1, v.gstream, v.g1, r).wait()
        out_copy(v, 2, v.gmid, v.ge, r).wait()
    sent(0)


def finish_kernel(D, FF, names, *refs):
    v = types.SimpleNamespace(**dict(zip(names, refs, strict=True)))
    load = lambda i, src, dst: pltpu.make_async_copy(src, dst, v.sems.at[0, i])
    save = lambda i, src, dst: pltpu.make_async_copy(src, dst, v.sems.at[1, i])
    cols = (slice(FF, 2 * FF), slice(0, FF), slice(2 * FF + D, 2 * FF + 4 * D), slice(2 * FF, 2 * FF + D))
    loads = [load(i, v.gw.at[:, c], v.gw_s.at[:, c]) for i, c in enumerate(cols)]
    loads += [load(4, v.g1, v.g1_s), load(5, v.ge, v.ge_s), load(6, v.y, v.y_s), load(7, v.gv, v.gv_s)]
    for c in loads:
        c.start()
    saves = []

    def keep(src, dst):
        saves.append(save(len(saves), src, dst))
        saves[-1].start()

    for i, (c, src, dst) in enumerate(zip(cols, (v.wdn_s, v.wup_s, v.wqkv_s, v.wout_s), (v.wdn, v.wup, v.wqkv, v.wout))):
        loads[i].wait()
        part = v.gw_s[:, c]
        src[...] = (part.T if i == 0 else part).astype(F32)
        keep(src, dst)
    for c, src, dst in zip(loads[4:7], (v.g1_s, v.ge_s, v.y_s), (v.g1_o, v.ge_o, v.y_o)):
        c.wait()
        keep(src, dst)
    loads[7].wait()
    n = D // 128
    at = 0
    for ref, size in ((v.ln1g, n), (v.ln1b, n), (v.qvb, 2 * n), (v.bout, n), (v.ln2g, n), (v.ln2b, n), (v.bdn, n),
                      (v.bup, FF // 128)):
        for k in range(size):
            row, col = divmod(k, ref.shape[1] // 128)
            ref[row:row + 1, col * 128:(col + 1) * 128] = v.gv_s[at + k:at + k + 1, :]
        at += size
    for c in saves:
        c.wait()


def solution(mesh):
    S, DP = mesh.shape["seq"], mesh.shape["dp"]

    def shards(hidden_in, embedding, lengths, cotangent, ln1_gain, ln1_bias, qkv_weight, qv_bias, out_weight, out_bias,
               ln2_gain, ln2_bias, up_weight, up_bias, down_weight, down_bias):
        L, R, D = hidden_in.shape
        FF = up_weight.shape[1]
        W = 4 * D + 2 * FF
        X, Z = S // 2, DP // 2
        parts = (FF, FF + D, 3 * D)
        members, wholes = (2, S, Z), (False, False, True)
        reduce_here = DP % 2 == 0 and Z > 1 and all(share_plan(D, w, members, f) for w, f in zip(parts, wholes))
        cfg = (S, DP, R, L, D, FF, reduce_here)
        VM = pltpu.VMEM
        DMA = pltpu.SemaphoreType.DMA
        scratch = dict(
            wT=VM((3 * D, D), BF), wupT=VM((FF, D), BF), wdnT=VM((D, FF), BF), bcol=VM((2, D, 128), F32),
            stream=VM((R, L, D), F32), gstream=VM((R, L, D), F32), gmid=VM((R, L, D), F32), nall=VM((2, R, S * L, D), BF), xh1=VM((2, R, L, D), F32), rs1=VM((2, R, L, 128), F32),
            xh2=VM((2, R, L, D), F32), rs2=VM((2, R, L, 128), F32), n2T=VM((2, R, D, L), BF), qT=VM((D, L), BF),
            qn=VM((2, R, L, D), BF), linv=VM((2, R, HEADS, 8, L), F32), oT=VM((2, R, D, L), BF),
            hidden=VM((2, R, L, FF), BF), slope=VM((2, R, L, FF), F32), e_scr=VM((2, R, S * L, HEADS * L), BF),
            pair_out=VM((R, X - 1, L, D), BF), pair_in=VM((2, R, X - 1, L, D), BF), part_out=VM((R, X - 1, L, D), BF),
            part_in=VM((2, R, X - 1, L, D), BF), near_out=VM((R, L, D), BF), near_in=VM((2, R, L, D), BF),
            keep=VM((R, X - 1, L, D), BF), vec=VM((8, W), F32),
            nsend=DMA((2, R, X + 1)), fsend=DMA((2, R, X)), nrecv=DMA((2, R, S)), psend=DMA((2, 2, R, X)), precv=DMA((2, 2, R, X)),
            nearsem=DMA((2, 2, R)), out_sems=DMA((3, R)), gw_sem=DMA((2,)), in_sem=DMA((len(LOADS),)))
        if reduce_here:
            lines = W // 128
            scratch.update(
                stage=VM((D, W), BF), gath=VM((D, W), BF), vs1=VM((2, lines, 128), F32), vs2=VM((S, lines, 128), F32),
                vs3=VM((Z, lines, 128), F32), vss1=DMA((1,)), vsr1=DMA((1,)), vss2=DMA((S - 1,)), vsr2=DMA((S - 1,)),
                vss3=DMA((Z - 1,)), vsr3=DMA((Z - 1,)))
            most = max(S, Z) - 1
            for p, (w, f) in enumerate(zip(parts, wholes)):
                for k, dims in enumerate(part_shapes(D, w, members, f)):
                    scratch[f"b{k}_{p}"] = VM(dims, BF)
                scratch.update({f"ss_{p}": DMA((6, most)), f"sr_{p}": DMA((6, most))})
        vm = pl.BlockSpec(memory_space=pltpu.VMEM)
        sm = pl.BlockSpec(memory_space=pltpu.SMEM)
        hbm = pl.BlockSpec(memory_space=pl.ANY)
        rows_first = lambda x: jnp.transpose(x, (1, 0, 2))
        line = lambda x: x.reshape(1, -1)
        ins = dict(
            hid=rows_first(hidden_in), emb=rows_first(embedding), cot=rows_first(cotangent), lengths=lengths, ln1g=line(ln1_gain),
            ln1b=line(ln1_bias), wqkv=qkv_weight, qvb=qv_bias, wout=out_weight, bout=line(out_bias), ln2g=line(ln2_gain),
            ln2b=line(ln2_bias), wup=up_weight, bup=line(up_bias), wdn=down_weight, bdn=line(down_bias))
        shape = jax.ShapeDtypeStruct
        outs = dict(
            y=shape((R, L, D), BF), g1=shape((R, L, D), F32), ge=shape((R, L, D), F32),
            gw=shape((D, W), BF if reduce_here else F32), gv=shape((W // 128, 128), F32))
        scratch.update({n: VM(ins[n].shape, ins[n].dtype) for n in LOADS})
        names = (*(n if n == "lengths" else n + "_in" for n in ins), *outs, *scratch)
        y, g1, ge, gw, gv = pl.pallas_call(
            functools.partial(block_kernel, cfg, names), out_shape=tuple(outs.values()),
            in_specs=[sm if n == "lengths" else hbm for n in ins], out_specs=tuple(vm if n == "gv" else hbm for n in outs),
            scratch_shapes=list(scratch.values()),
            compiler_params=pltpu.CompilerParams(collective_id=0, has_side_effects=True, vmem_limit_bytes=VMEM_LIMIT),
        )(*ins.values())
        if not reduce_here:
            gw, gv = lax.psum((gw, gv), ("dp", "seq"))
        full = [shape((R, L, D), BF), shape((R, L, D), F32), shape((R, L, D), F32), shape((1, D), F32), shape((1, D), F32),
                shape((D, 3 * D), F32), shape((2, D), F32), shape((D, D), F32), shape((1, D), F32), shape((1, D), F32),
                shape((1, D), F32), shape((D, FF), F32), shape((1, FF), F32), shape((FF, D), F32), shape((1, D), F32)]
        ends = ["y_o", "g1_o", "ge_o", "ln1g", "ln1b", "wqkv", "qvb", "wout", "bout", "ln2g", "ln2b", "wup", "bup", "wdn", "bdn"]
        large = ("y_o", "g1_o", "ge_o", "wqkv", "wout", "wup", "wdn")
        temps = dict(
            y_s=VM((R, L, D), BF), g1_s=VM((R, L, D), F32), ge_s=VM((R, L, D), F32), gw_s=VM((D, W), gw.dtype),
            gv_s=VM((W // 128, 128), F32), wup_s=VM((D, FF), F32), wdn_s=VM((FF, D), F32), wqkv_s=VM((D, 3 * D), F32),
            wout_s=VM((D, D), F32), sems=DMA((2, 8)))
        res = pl.pallas_call(
            functools.partial(finish_kernel, D, FF, (*outs, *ends, *temps)), out_shape=full, in_specs=[hbm] * 5,
            out_specs=[hbm if n in large else vm for n in ends], scratch_shapes=list(temps.values()),
            compiler_params=pltpu.CompilerParams(vmem_limit_bytes=VMEM_LIMIT))(y, g1, ge, gw, gv)
        flat = (3, 4, 8, 9, 10, 12, 14)
        return tuple(rows_first(x) if i < 3 else x.reshape(-1) if i in flat else x for i, x in enumerate(res))

    token = P("seq", "dp", None)
    return jax.shard_map(
        shards, mesh=mesh, in_specs=(token, token, P("dp"), token) + (P(),) * 12, out_specs=(token,) * 3 + (P(),) * 12,
        check_vma=False)
```

```python
import functools
import types

import jax
import jax.numpy as jnp
from jax import lax
from jax.experimental import pallas as pl
from jax.experimental.pallas import tpu as pltpu
from jax.sharding import PartitionSpec as P

EPS = 1e-05
MASKED = -1e30
HEADS = 4
HD = 64
BF = jnp.bfloat16
F32 = jnp.float32
MESH = pl.DeviceIdType.MESH
VMEM_LIMIT = 61 * 1024 * 1024


def nn(a, b):
    return lax.dot_general(a, b, (((1,), (0,)), ((), ())), preferred_element_type=F32)


def nt(a, b):
    return lax.dot_general(a, b, (((1,), (1,)), ((), ())), preferred_element_type=F32)


def normalise(x):
    mean = jnp.mean(x, axis=-1, keepdims=True)
    centred = x - mean
    rstd = lax.rsqrt(jnp.mean(centred * centred, axis=-1, keepdims=True) + EPS)
    return centred * rstd, rstd


def norm_back(grad, gain, xhat, rstd):
    gl = grad * gain
    m1 = jnp.mean(gl, axis=-1, keepdims=True)
    m2 = jnp.mean(gl * xhat, axis=-1, keepdims=True)
    return rstd * (gl - m1 - xhat * m2)


def fold(x):
    return jnp.sum(x.reshape(x.shape[0] // 8, 8, x.shape[1]), axis=0)


def gelu_parts(x):
    c0 = 0.7978845608028654
    c1 = c0 * 0.044715
    x2 = x * x
    half = 0.5 + 0.5 * jnp.tanh(x * (c0 + c1 * x2))
    slope = half + (half * (1.0 - half)) * (x * (2 * c0 + (6 * c1) * x2))
    return x * half, slope


def head_rows(x, h):
    own = x[h * HD:(h + 1) * HD]
    zero = jnp.zeros_like(own)
    return jnp.concatenate([own, zero] if h % 2 == 0 else [zero, own], axis=0)


def pair(h):
    return slice((h // 2) * 2 * HD, (h // 2 + 1) * 2 * HD)


def heads_apart(x):
    lane = lax.broadcasted_iota(jnp.int32, x.shape, 1)
    return jnp.concatenate(
        [jnp.where((lane >= h * HD) & (lane < (h + 1) * HD), x, jnp.zeros((), x.dtype)) for h in range(HEADS)], axis=0)


def wide(x, n):
    return jnp.concatenate([x] * (n // 128), axis=1)


class Share:
    def __init__(self, v, start, w, into, stages, whole_last):
        self.v, self.stages, self.whole = v, stages, whole_last
        self.bufs, self.send, self.recv = into
        self.down = len(stages)
        self.steps = 2 * self.down - (1 if whole_last else 0)
        self.plan = share_plan(v.D, w, [n for n, _, _ in stages], whole_last)
        base = (0, start)
        self.bases = [base]
        for k, (n, own, _) in enumerate(stages):
            base = self.part(k, own)[0]
            self.bases.append(base)

    def part(self, k, number):
        rows, lanes, row_parts, _ = self.plan[k]
        r, c = self.bases[k]
        if row_parts == 1:
            return (r, c + number * lanes), (rows, lanes)
        return (r + lax.rem(number, row_parts) * rows, c + lax.div(number, row_parts) * lanes), (rows, lanes)

    def window(self, base, size):
        r, c = base
        at = c if isinstance(c, int) else pl.multiple_of(c, 128)
        return pl.ds(pl.multiple_of(r, 16) if not isinstance(r, int) else r, size[0]), pl.ds(at, size[1])

    def region(self, k):
        rows, lanes, row_parts, lane_parts = self.plan[k]
        return self.window(self.bases[k], (rows * row_parts, lanes * lane_parts))

    def copies(self, i):
        v = self.v
        k = i if i < self.down else 2 * self.down - 1 - i - (1 if self.whole else 0)
        n, own, device = self.stages[k]
        out = []
        for j in range(1, n):
            other = lax.rem(own + j, n)
            if i == self.down - 1 and self.whole:
                out.append((v.stage.at[self.region(k)], self.bufs[k].at[own], device(other)))
            elif i < self.down:
                out.append((v.stage.at[self.window(*self.part(k, other))], self.bufs[k].at[j - 1], device(other)))
            else:
                ref = v.gath.at[self.window(*self.part(k, own))]
                out.append((ref, ref, device(other)))
        return out

    def made(self, i):
        return [pltpu.make_async_remote_copy(src_ref=s, dst_ref=d, send_sem=self.send.at[i, j], recv_sem=self.recv.at[i, j],
                                             device_id=dev, device_id_type=MESH)
                for j, (s, d, dev) in enumerate(self.copies(i))]

    def start(self, i):
        v = self.v
        if i == 0:
            n, own, _ = self.stages[0]
            for j in range(1, n):
                there = self.window(*self.part(0, lax.rem(own + j, n)))
                v.stage[there] = v.dW[there].astype(BF)
        for c in self.made(i):
            c.start()

    def finish(self, i):
        v = self.v
        for c in self.made(i):
            c.wait()
        if i >= self.down:
            return
        n, own, _ = self.stages[i]
        if i == self.down - 1 and self.whole:
            at = self.region(i)
            self.bufs[i][own] = v.stage[at]
            total = self.bufs[i][0].astype(F32)
            for j in range(1, n):
                total = total + self.bufs[i][j].astype(F32)
        else:
            at = self.window(*self.part(i, own))
            total = v.dW[at]
            for j in range(n - 1):
                total = total + self.bufs[i][j].astype(F32)
        if i == self.down - 1:
            v.gath[at] = total.astype(BF)
        else:
            v.dW[at] = total
            v.stage[at] = total.astype(BF)

    def step(self, i):
        self.finish(i)
        if i + 1 < self.steps:
            self.start(i + 1)


def share_plan(D, w, members, whole_last):
    rows, lanes, plan = D, w, []
    for k, n in enumerate(members):
        if whole_last and k == len(members) - 1:
            plan.append((rows, lanes, 1, 1))
            continue
        row_parts = max(p for p in range(1, n + 1) if n % p == 0 and rows % (16 * p) == 0)
        lane_parts = n // row_parts
        if lanes % (128 * lane_parts):
            return None
        rows, lanes = rows // row_parts, lanes // lane_parts
        plan.append((rows, lanes, row_parts, lane_parts))
    return plan


def part_shapes(D, w, members, whole_last):
    shapes = []
    for k, (n, (rows, lanes, rp, lp)) in enumerate(zip(members, share_plan(D, w, members, whole_last))):
        whole = whole_last and k == len(members) - 1
        shapes.append((n if whole else n - 1, rows, lanes))
    return shapes


class SmallSum:
    def __init__(self, v):
        self.v = v
        self.stages = [(v.vs1, v.core, 2, lambda other: v.sibling, v.vss1, v.vsr1),
                       (v.vs2, v.spot2, v.S, v.in_plane, v.vss2, v.vsr2), (v.vs3, v.spot3, v.DP // 2, v.across, v.vss3, v.vsr3)]

    def copies(self, i):
        buf, spot, n, device, send, recv = self.stages[i]
        return [pltpu.make_async_remote_copy(
            src_ref=buf.at[spot], dst_ref=buf.at[spot], send_sem=send.at[k - 1], recv_sem=recv.at[k - 1],
            device_id=device(lax.rem(spot + k, n)), device_id_type=MESH) for k in range(1, n)]

    def start(self, i, value):
        buf, spot = self.stages[i][:2]
        buf[spot] = value
        for c in self.copies(i):
            c.start()

    def finish(self, i):
        for c in self.copies(i):
            c.wait()
        buf, n = self.stages[i][0], self.stages[i][2]
        total = buf[0]
        for s in range(1, n):
            total = total + buf[s]
        return total


def out_copy(v, which, src, dst, r):
    return pltpu.make_async_copy(src.at[r], dst.at[r], v.out_sems.at[which, r])


LOADS = ("hid", "emb", "ln1g", "ln1b", "wqkv", "qvb", "wup", "wdn", "wout", "bout", "ln2g", "ln2b", "bup", "bdn", "cot")


def block_kernel(cfg, names, *refs):
    S, DP, R, L, D, FF, reduce_here = cfg
    W = 4 * D + 2 * FF
    v = types.SimpleNamespace(**dict(zip(names, refs, strict=True)))
    v.S, v.DP, v.R, v.L, v.D, v.FF, v.W, v.reduce_here = S, DP, R, L, D, FF, W, reduce_here
    v.me, v.dp = me, dp = lax.axis_index("seq"), lax.axis_index("dp")
    v.chip, v.core = chip, core = lax.div(me, 2), lax.rem(me, 2)
    X = v.X = S // 2
    v.mine = mine = pl.ds(pl.multiple_of(me * L, L), L)
    v.sibling = (dp, me + 1 - 2 * core)
    sizes = (S // 2, S)

    def with_size(body):
        low = 0
        for n in sizes:
            pl.when((me >= low) & (me < n))(functools.partial(body, n))
            low = n

    barrier = pltpu.get_barrier_semaphore()
    Z = DP // 2
    x_peers = [(dp, lax.rem(me + 2 * k, S)) for k in range(1, X)]
    peers, count = [v.sibling] + x_peers, X
    if reduce_here:
        v.spot2, v.spot3 = chip * 2 + lax.rem(dp, 2), lax.div(dp, 2)
        v.in_plane = lambda n: (lax.div(dp, 2) * 2 + lax.rem(n, 2), lax.div(n, 2) * 2 + core)
        v.across = lambda n: (n * 2 + lax.rem(dp, 2), me)
        z = v.spot3
        peers.append((dp + 1 - 2 * lax.rem(dp, 2), me))
        count = count + 1 + jnp.where(z > 0, 1, 0) + jnp.where(z < Z - 1, 1, 0)
    for peer in peers:
        pl.semaphore_signal(barrier, inc=1, device_id=peer, device_id_type=MESH)
    if reduce_here:
        for there, step in ((z < Z - 1, 1), (z > 0, -1)):
            @pl.when(there)
            def _():
                pl.semaphore_signal(barrier, inc=1, device_id=v.across(z + step), device_id_type=MESH)

    def tell(which, peer):
        pl.semaphore_signal(v.relay.at[which], inc=1, device_id=peer, device_id_type=MESH)

    def first_word():
        for peer in x_peers:
            tell(0, peer)

        @pl.when((z > 0) & (z < Z - 1))
        def _():
            tell(1, v.across(z + 1))
            tell(2, v.across(z - 1))

    def passed_on():
        pl.semaphore_wait(v.relay.at[0], X - 1)
        pl.when(z >= 2)(lambda: pl.semaphore_wait(v.relay.at[1], 1))
        pl.when(z <= Z - 3)(lambda: pl.semaphore_wait(v.relay.at[2], 1))
        pl.when((z >= 2) & (z < Z - 1))(lambda: tell(3, v.across(z + 1)))
        pl.when((z <= Z - 3) & (z > 0))(lambda: tell(4, v.across(z - 1)))
        pl.when(z >= 3)(lambda: pl.semaphore_wait(v.relay.at[3], 1))
        pl.when(z <= Z - 4)(lambda: pl.semaphore_wait(v.relay.at[4], 1))

    brought = {}
    for k, name in enumerate(LOADS):
        brought[name] = pltpu.make_async_copy(getattr(v, name + "_in"), getattr(v, name), v.in_sem.at[k])
        brought[name].start()

    def need(*which):
        for name in which:
            brought.pop(name).wait()

    v.need = need

    def block_of(a, r, t):
        return v.nall.at[a, r, pl.ds(pl.multiple_of(t * L, L), L)]

    def normed_copy(a, r, t, send_sem, dst):
        ref = block_of(a, r, t)
        return pltpu.make_async_remote_copy(
            src_ref=ref, dst_ref=ref, send_sem=send_sem, recv_sem=v.nrecv.at[a, r, t], device_id=(dp, dst), device_id_type=MESH)

    def to_chip(a, r, c):
        return normed_copy(a, r, me, v.nsend.at[a, r, c], 2 * c + core)

    def to_sibling(a, r):
        return normed_copy(a, r, me, v.nsend.at[a, r, X], me + 1 - 2 * core)

    def handed_on(a, r, c):
        return normed_copy(a, r, 2 * c + core, v.fsend.at[a, r, c], me + 1 - 2 * core)

    def each_send(a, r, action):
        @pl.loop(chip + 1, X)
        def _(c):
            action(to_chip(a, r, c))

        @pl.when(core == 0)
        def _():
            action(to_sibling(a, r))

    def first_norm(a, r):
        u = v.stream[r] + v.emb[r].astype(F32)
        v.stream[r] = u
        xhat, rstd = normalise(u)
        v.xh1[a, r] = xhat
        v.rs1[a, r] = jnp.broadcast_to(rstd, (L, 128))
        v.nall[a, r, mine] = (xhat * ln1g + ln1b).astype(BF)

    def announce(a, r):
        each_send(a, r, lambda c: c.start())

    def hand_on(a, r):
        @pl.loop(0, chip)
        def _(c):
            handed_on(a, r, c).wait_recv()
            handed_on(a, r, c).start()

    def gathered(a, r):
        @pl.loop(0, chip)
        def _(c):
            normed_copy(a, r, 2 * c + 1 - core, v.fsend.at[a, r, c], me).wait_recv()

        @pl.when(core == 1)
        def _():
            normed_copy(a, r, me - 1, v.nsend.at[a, r, X], me).wait_recv()

    need("hid", "emb", "ln1g", "ln1b")
    ln1g, ln1b = v.ln1g[...], v.ln1b[...]

    def first_input(r):
        v.stream[r] = v.hid[r].astype(F32)
        first_norm(0, r)

    first_input(0)
    @pl.loop(me + 1, S)
    def _(t):
        for a in range(2):
            for r in range(R):
                v.nall[a, r, pl.ds(pl.multiple_of(t * L, L), L)] = jnp.zeros((L, D), BF)

    v.vec[...] = jnp.zeros_like(v.vec)
    pl.semaphore_wait(barrier, count)
    announce(0, 0)

    @pl.loop(1, R)
    def _(r):
        first_input(r)
        announce(0, r)

    if reduce_here:
        first_word()
    need("wqkv", "qvb")
    for k in range(3):
        v.wT[k * D:(k + 1) * D] = v.wqkv[:, k * D:(k + 1) * D].T
    for k in range(2):
        v.bcol[k] = jnp.broadcast_to(v.qvb[k:k + 1, :], (128, D)).T
    need("wup", "wdn")
    for k in range(FF // D):
        ks = slice(k * D, (k + 1) * D)
        v.wupT[ks] = v.wup[:, ks].T
        v.wdnT[:, ks] = v.wdn[ks].T

    need("wout", "bout", "ln2g", "ln2b", "bup", "bdn", "cot")
    ln2g, ln2b = v.ln2g[...], v.ln2b[...]

    def forward_attention(a, r, bias, s_scr, qT_s, nb):
        KB = nb * L
        rows = v.nall[a, r, 0:KB, :]
        keys = nn(rows, v.wqkv[:, D:2 * D]).astype(BF)
        qT = qT_s[r]
        tops = []
        for h in range(HEADS):
            s = nn(keys[:, pair(h)], head_rows(qT, h)) + bias[r, 0:KB]
            s_scr[0:KB, h * L:(h + 1) * L] = s
            tops.append(jnp.max(jnp.max(s.reshape(KB // 8, 8, L), axis=0), axis=0, keepdims=True))
        VT = (nt(v.wT[2 * D:], rows) + wide(v.bcol[1], KB)).astype(BF)
        for h in range(HEADS):
            hs, hl = slice(h * HD, (h + 1) * HD), slice(h * L, (h + 1) * L)
            sums, out = [], []
            for t in range(nb):
                ts = slice(t * L, (t + 1) * L)
                e = jnp.exp(s_scr[ts, hl] - tops[h])
                sums.append(fold(e))
                low = e.astype(BF)
                v.e_scr[a, r, ts, hl] = low
                out.append(nn(VT[hs, ts], low))
            inv = 1.0 / jnp.sum(sum(sums), axis=0, keepdims=True)
            v.linv[a, r, h] = jnp.broadcast_to(inv, (8, L))
            v.oT[a, r, hs] = (sum(out) * inv).astype(BF)

    def forward_all(bias, s_scr, qT_s):
        def queries(a, r):
            normed = v.nall[a, r, mine]
            qT = ((nt(v.wT[:D], normed) + wide(v.bcol[0], L)) * (HD ** -0.5)).astype(BF)
            v.qn[a, r] = qT.T
            qT_s[r] = qT

        @pl.loop(0, R)
        def _(r):
            queries(0, r)
            length = v.lengths[r]
            for t in range(S):
                key_pos = t * L + lax.broadcasted_iota(jnp.int32, (L, L), 0)
                query_pos = me * L + lax.broadcasted_iota(jnp.int32, (L, L), 1)
                bias[r, t * L:(t + 1) * L] = jnp.where((key_pos <= query_pos) & (key_pos < length), 0.0, MASKED)

        hand_on(0, 0)

        @pl.loop(0, 2 * R)
        def _(n):
            a, r = lax.div(n, R), lax.rem(n, R)
            gathered(a, r)
            with_size(functools.partial(forward_attention, a, r, bias, s_scr, qT_s))

            @pl.when(n < 2 * R - 1)
            def _():
                hand_on(lax.div(n + 1, R), lax.rem(n + 1, R))

            middle = v.stream[r] + (nn(v.oT[a, r].T, v.wout[...]) + v.bout[...])
            xhat, rstd = normalise(middle)
            v.xh2[a, r] = xhat
            v.rs2[a, r] = jnp.broadcast_to(rstd, (L, 128))
            normed2 = (xhat * ln2g + ln2b).astype(BF)
            v.n2T[a, r] = normed2.T
            hidden, slope = gelu_parts(nn(normed2, v.wup[...]) + v.bup[...])
            hidden = hidden.astype(BF)
            v.hidden[a, r] = hidden
            v.slope[a, r] = slope
            v.stream[r] = middle + (nn(hidden, v.wdn[...]) + v.bdn[...])

            @pl.when(a == 0)
            def _():
                first_norm(1, r)
                announce(1, r)
                queries(1, r)

            @pl.when(a == 1)
            def _():
                v.hid[r] = v.stream[r].astype(BF)
                v.gstream[r] = v.cot[r].astype(F32)
                out_copy(v, 0, v.hid, v.y, r).start()

    VM = pltpu.VMEM
    if reduce_here:
        v.passed_on = passed_on
    pl.run_scoped(forward_all, VM((R, S * L, L), F32), VM((S * L, HEADS * L), F32), VM((R, D, L), BF))
    pl.run_scoped(functools.partial(backward, v, with_size), VM((R, D, L), BF), VM((R, L, FF), BF), VM((R, L, D), BF),
                  VM((R, L, 3 * D), BF), VM((D, W), F32), VM((L, D), F32),
                  VM((S * L, D), BF), VM((S * L, 2 * D), BF))

    for a in range(2):
        for r in range(R):
            each_send(a, r, lambda c: c.wait_send())

            @pl.loop(0, chip)
            def _(c):
                handed_on(a, r, c).wait_send()


def backward(v, with_size, gbT, gpre, ga_s, gqkv, dW, gns, pg_s, gkv_s):
    S, DP, R, L, D, FF, W = v.S, v.DP, v.R, v.L, v.D, v.FF, v.W
    me, dp, mine = v.me, v.dp, v.mine
    v.dW = dW
    ln1g, ln2g = v.ln1g[...], v.ln2g[...]
    UP, DN, OW, QW = 0, FF, 2 * FF, 2 * FF + D
    V_LN1G, V_LN1B, V_QB, V_VB, V_OB, V_LN2G, V_LN2B, V_DB, V_UB = [D * k for k in range(9)]

    X, chip, core = v.X, v.chip, v.core

    def pair_copy(a, r, c):
        return pltpu.make_async_remote_copy(
            src_ref=v.pair_out.at[r, c], dst_ref=v.pair_in.at[a, r, c], send_sem=v.psend.at[0, a, r, c],
            recv_sem=v.precv.at[0, a, r, c], device_id=v.sibling, device_id_type=MESH)

    def part_copy(a, r, src, dst):
        return pltpu.make_async_remote_copy(
            src_ref=v.part_out.at[r, dst], dst_ref=v.part_in.at[a, r, src - 1], send_sem=v.psend.at[1, a, r, dst],
            recv_sem=v.precv.at[1, a, r, src], device_id=(dp, 2 * dst + core), device_id_type=MESH)

    def near_copy(a, r):
        return pltpu.make_async_remote_copy(
            src_ref=v.near_out.at[r], dst_ref=v.near_in.at[a, r], send_sem=v.nearsem.at[0, a, r],
            recv_sem=v.nearsem.at[1, a, r], device_id=v.sibling, device_id_type=MESH)

    def pass_on(a, r):
        @pl.loop(0, chip)
        def _(c):
            pair_copy(a, r, c).wait_recv()
            v.part_out[r, c] = (v.keep[r, c].astype(F32) + v.pair_in[a, r, c].astype(F32)).astype(BF)
            part_copy(a, r, chip, c).start()

    def sent(a):
        for r in range(R):
            @pl.loop(0, chip)
            def _(c):
                pair_copy(a, r, c).wait_send()
                part_copy(a, r, chip, c).wait_send()

            @pl.when(core == 1)
            def _():
                near_copy(a, r).wait_send()

    def add_vec(start, terms):
        v.vec[:, start:start + terms.shape[1]] += fold(terms)

    def backward_mlp(a, r):
        g = v.gstream[r]
        gb = g.astype(BF)
        add_vec(V_DB, gb.astype(F32))
        gbT[r] = gb.T
        pre = (nn(gb, v.wdnT[...]) * v.slope[a, r]).astype(BF)
        gpre[r] = pre
        add_vec(V_UB, pre.astype(F32))
        gn2 = nn(pre, v.wupT[...])
        xhat = v.xh2[a, r]
        add_vec(V_LN2G, gn2 * xhat)
        add_vec(V_LN2B, gn2)
        gm = g + norm_back(gn2, ln2g, xhat, wide(v.rs2[a, r], D))
        v.gmid[r] = gm
        ga = gm.astype(BF)
        ga_s[r] = ga
        add_vec(V_OB, ga.astype(F32))

    def attention_core(a, r, tick, nb):
        KB = nb * L
        gaT = nt(v.wout[...], ga_s[r]).astype(BF).astype(F32)
        oT = v.oT[a, r].astype(F32)
        scaled, deltas = [], []
        for h in range(HEADS):
            hs = slice(h * HD, (h + 1) * HD)
            part = gaT[hs] * v.linv[a, r, h, 0:1]
            scaled.append(part.astype(BF))
            deltas.append(jnp.sum(part * oT[hs], axis=0, keepdims=True))
        gaT_n = jnp.concatenate(scaled, axis=0)
        rows = v.nall[a, r, 0:KB, :]
        values = (nn(rows, v.wqkv[:, 2 * D:]) + v.qvb[1:2, :]).astype(BF)
        KT = nt(v.wT[D:2 * D], rows).astype(BF)
        blocks = [slice(t * L, (t + 1) * L) for t in range(nb)]
        ga_apart, q_apart = heads_apart(gaT_n.T), heads_apart(v.qn[a, r])
        for ts in blocks:
            gkv_s[ts, D:] = nn(v.e_scr[a, r, ts, :], ga_apart).astype(BF)
        for h in range(HEADS):
            hl = slice(h * L, (h + 1) * L)
            gp = nn(values[:, pair(h)], head_rows(gaT_n, h))
            v.e_scr[a, r, 0:KB, hl] = (v.e_scr[a, r, 0:KB, hl].astype(F32) * (gp - deltas[h])).astype(BF)
        tick()
        for ts in blocks:
            gkv_s[ts, :D] = nn(v.e_scr[a, r, ts, :], q_apart).astype(BF)
        for ts in blocks:
            pg_s[ts] = nn(gkv_s[ts, :], v.wT[D:]).astype(BF)
        for t in range(nb):
            ts = blocks[t]
            if t // 2 < nb // 2 - 1:
                @pl.when((t // 2 < chip) & (t % 2 == core))
                def _():
                    v.keep[r, t // 2] = pg_s[ts]

                @pl.when((t // 2 < chip) & (t % 2 != core))
                def _():
                    v.pair_out[r, t // 2] = pg_s[ts]
                    pair_copy(a, r, t // 2).start()

            if t % 2 == 0:
                @pl.when(t == me - 1)
                def _():
                    v.near_out[r] = pg_s[ts]
                    near_copy(a, r).start()

            @pl.when(t == me)
            def _():
                gqkv[r, :, D:] = gkv_s[ts]

        add_vec(V_VB, gkv_s[0:KB, D:].astype(F32))
        gqT = jnp.concatenate([nn(KT[h * HD:(h + 1) * HD], v.e_scr[a, r, 0:KB, h * L:(h + 1) * L]) for h in range(HEADS)], axis=0)
        dW[:, QW + D:QW + 3 * D] += nn(rows.T, gkv_s[0:KB])
        gq = (gqT * (HD ** -0.5)).T.astype(BF)
        gqkv[r, :, :D] = gq
        add_vec(V_QB, gq.astype(F32))

    def backward_norm(a, r):
        gns[...] = nn(gqkv[r], v.wT[...])

        @pl.when(core == 0)
        def _():
            near_copy(a, r).wait_recv()
            gns[...] += v.near_in[a, r].astype(F32)

        @pl.loop(chip + 1, X)
        def _(c):
            part_copy(a, r, c, chip).wait_recv()
            gns[...] += v.part_in[a, r, c - 1].astype(F32)

        gn = gns[...]
        xhat = v.xh1[a, r]
        add_vec(V_LN1G, gn * xhat)
        add_vec(V_LN1B, gn)
        v.gstream[r] = v.gmid[r] + norm_back(gn, ln1g, xhat, wide(v.rs1[a, r], D))

    def put(first, start, value):
        if first:
            dW[:, start:start + value.shape[1]] = value
        else:
            dW[:, start:start + value.shape[1]] += value

    def weight_terms(a, rows, which):
        first = a == 1 and rows[0] == 0
        if "up" in which:
            put(first, UP, sum(nn(v.n2T[a, r], gpre[r]) for r in rows))
        if "down" in which:
            put(first, DN, sum(nn(gbT[r], v.hidden[a, r]) for r in rows))
            put(first, OW, sum(nn(v.oT[a, r], ga_s[r]) for r in rows))

    def query_terms(a):
        put(a == 1, QW, sum(nn(v.nall[a, r, mine].T, gqkv[r, :, :D]) for r in range(R)))

    every, early, last = tuple(range(R)), tuple(range(R - 1)), (R - 1,)
    dW[:, QW + D:QW + 3 * D] = jnp.zeros((D, 2 * D), F32)
    reducing = v.reduce_here
    if reducing:
        pair_stage = (2, core, lambda n: v.sibling)
        plane, across = (S, v.spot2, v.in_plane), (DP // 2, v.spot3, v.across)
        into = lambda p: ([getattr(v, f"b{k}_{p}") for k in range(3)], getattr(v, f"ss_{p}"), getattr(v, f"sr_{p}"))
        up, down, qkv = (Share(v, start, w, into(p), (pair_stage, plane, across), whole)
                         for p, (start, w, whole) in enumerate(((UP, FF, False), (DN, FF + D, False), (QW, 3 * D, True))))
        small = SmallSum(v)
        v.passed_on()

    def nothing():
        pass

    def attention(a, r, tick):
        with_size(functools.partial(attention_core, a, r, tick))

    for r in range(R):
        backward_mlp(1, r)

    weight_terms(1, every, ("up", "down"))

    @pl.loop(0, R)
    def _(r):
        attention(1, r, lambda: pl.when(r > 0)(lambda: pass_on(1, r - 1)))

    pass_on(1, R - 1)
    query_terms(1)

    def between(r):
        backward_norm(1, r)
        v.stream[r] = v.gstream[r]
        backward_mlp(0, r)

    for r in range(R - 1):
        between(r)
    if early:
        weight_terms(0, early, ("up", "down"))
    between(R - 1)
    weight_terms(0, last, ("up",))
    if reducing:
        up.start(0)
    weight_terms(0, last, ("down",))
    if reducing:
        down.start(0)

    sent(1)

    def tick_first():
        if reducing:
            up.step(0)
            down.step(0)

    def tick_last():
        if reducing:
            up.step(1)

    for r in range(R):
        attention(0, r, tick_first if r == 0 else tick_last if r == R - 1 else nothing)
        if r > 0:
            pass_on(0, r - 1)
    query_terms(0)
    if reducing:
        qkv.start(0)
    pass_on(0, R - 1)
    if reducing:
        down.step(1)

    def final(r):
        backward_norm(0, r)
        v.gmid[r] = v.gstream[r] + v.stream[r]
        out_copy(v, 1, v.gstream, v.g1, r).start()
        out_copy(v, 2, v.gmid, v.ge, r).start()

    def small_lines():
        sums = jnp.sum(v.vec[...], axis=0, keepdims=True)
        return jnp.concatenate([sums[:, k * 128:(k + 1) * 128] for k in range(W // 128)], axis=0)

    if reducing:
        gath_copy = lambda k, cols: pltpu.make_async_copy(v.gath.at[:, cols], v.gw.at[:, cols], v.gw_sem.at[k])
        first_out, second_out = gath_copy(0, slice(0, QW)), gath_copy(1, slice(QW, W))
        qkv.step(0)
        for r in range(R - 1):
            final(r)
        up.step(2)
        qkv.step(1)
        down.step(2)
        final(R - 1)
        small.start(0, small_lines())
        up.step(3)
        small.start(1, small.finish(0))
        qkv.step(2)
        down.step(3)
        small.start(2, small.finish(1))
        up.step(4)
        qkv.step(3)
        down.step(4)
        v.gv[...] = small.finish(2)
        up.finish(5)
        down.finish(5)
        first_out.start()
        qkv.finish(4)
        second_out.start()
        first_out.wait()
        second_out.wait()
    else:
        pl.loop(0, R)(final)
        out = pltpu.make_async_copy(v.gath if v.reduce_here else dW, v.gw, v.gw_sem.at[0])
        out.start()
        out.wait()
        v.gv[...] = small_lines()

    for r in range(R):
        out_copy(v, 0, v.hid, v.y, r).wait()
        out_copy(v, 1, v.gstream, v.g1, r).wait()
        out_copy(v, 2, v.gmid, v.ge, r).wait()
    sent(0)


def finish_kernel(D, FF, names, *refs):
    v = types.SimpleNamespace(**dict(zip(names, refs, strict=True)))
    load = lambda i, src, dst: pltpu.make_async_copy(src, dst, v.sems.at[0, i])
    save = lambda i, src, dst: pltpu.make_async_copy(src, dst, v.sems.at[1, i])
    cols = (slice(FF, 2 * FF), slice(0, FF), slice(2 * FF + D, 2 * FF + 4 * D), slice(2 * FF, 2 * FF + D))
    loads = [load(i, v.gw.at[:, c], v.gw_s.at[:, c]) for i, c in enumerate(cols)]
    loads += [load(4, v.g1, v.g1_s), load(5, v.ge, v.ge_s), load(6, v.y, v.y_s), load(7, v.gv, v.gv_s)]
    for c in loads:
        c.start()
    saves = []

    def keep(src, dst):
        saves.append(save(len(saves), src, dst))
        saves[-1].start()

    for i, (c, src, dst) in enumerate(zip(cols, (v.wdn_s, v.wup_s, v.wqkv_s, v.wout_s), (v.wdn, v.wup, v.wqkv, v.wout))):
        loads[i].wait()
        part = v.gw_s[:, c]
        src[...] = (part.T if i == 0 else part).astype(F32)
        keep(src, dst)
    for c, src, dst in zip(loads[4:7], (v.g1_s, v.ge_s, v.y_s), (v.g1_o, v.ge_o, v.y_o)):
        c.wait()
        keep(src, dst)
    loads[7].wait()
    n = D // 128
    at = 0
    for ref, size in ((v.ln1g, n), (v.ln1b, n), (v.qvb, 2 * n), (v.bout, n), (v.ln2g, n), (v.ln2b, n), (v.bdn, n),
                      (v.bup, FF // 128)):
        for k in range(size):
            row, col = divmod(k, ref.shape[1] // 128)
            ref[row:row + 1, col * 128:(col + 1) * 128] = v.gv_s[at + k:at + k + 1, :]
        at += size
    for c in saves:
        c.wait()


def solution(mesh):
    S, DP = mesh.shape["seq"], mesh.shape["dp"]

    def shards(hidden_in, embedding, lengths, cotangent, ln1_gain, ln1_bias, qkv_weight, qv_bias, out_weight, out_bias,
               ln2_gain, ln2_bias, up_weight, up_bias, down_weight, down_bias):
        L, R, D = hidden_in.shape
        FF = up_weight.shape[1]
        W = 4 * D + 2 * FF
        X, Z = S // 2, DP // 2
        parts = (FF, FF + D, 3 * D)
        members, wholes = (2, S, Z), (False, False, True)
        reduce_here = DP % 2 == 0 and 1 < Z <= 4 and all(share_plan(D, w, members, f) for w, f in zip(parts, wholes))
        cfg = (S, DP, R, L, D, FF, reduce_here)
        VM = pltpu.VMEM
        DMA = pltpu.SemaphoreType.DMA
        scratch = dict(
            wT=VM((3 * D, D), BF), wupT=VM((FF, D), BF), wdnT=VM((D, FF), BF), bcol=VM((2, D, 128), F32),
            stream=VM((R, L, D), F32), gstream=VM((R, L, D), F32), gmid=VM((R, L, D), F32), nall=VM((2, R, S * L, D), BF), xh1=VM((2, R, L, D), F32), rs1=VM((2, R, L, 128), F32),
            xh2=VM((2, R, L, D), F32), rs2=VM((2, R, L, 128), F32), n2T=VM((2, R, D, L), BF),
            qn=VM((2, R, L, D), BF), linv=VM((2, R, HEADS, 8, L), F32), oT=VM((2, R, D, L), BF),
            hidden=VM((2, R, L, FF), BF), slope=VM((2, R, L, FF), F32), e_scr=VM((2, R, S * L, HEADS * L), BF),
            pair_out=VM((R, X - 1, L, D), BF), pair_in=VM((2, R, X - 1, L, D), BF), part_out=VM((R, X - 1, L, D), BF),
            part_in=VM((2, R, X - 1, L, D), BF), near_out=VM((R, L, D), BF), near_in=VM((2, R, L, D), BF),
            keep=VM((R, X - 1, L, D), BF), vec=VM((8, W), F32),
            nsend=DMA((2, R, X + 1)), fsend=DMA((2, R, X)), nrecv=DMA((2, R, S)), psend=DMA((2, 2, R, X)), precv=DMA((2, 2, R, X)),
            nearsem=DMA((2, 2, R)), out_sems=DMA((3, R)), gw_sem=DMA((2,)), in_sem=DMA((len(LOADS),)))
        if reduce_here:
            lines = W // 128
            scratch.update(
                stage=VM((D, W), BF), gath=VM((D, W), BF), vs1=VM((2, lines, 128), F32), vs2=VM((S, lines, 128), F32),
                vs3=VM((Z, lines, 128), F32), vss1=DMA((1,)), vsr1=DMA((1,)), vss2=DMA((S - 1,)), vsr2=DMA((S - 1,)),
                vss3=DMA((Z - 1,)), vsr3=DMA((Z - 1,)), relay=pltpu.SemaphoreType.REGULAR((5,)))
            most = max(S, Z) - 1
            for p, (w, f) in enumerate(zip(parts, wholes)):
                for k, dims in enumerate(part_shapes(D, w, members, f)):
                    scratch[f"b{k}_{p}"] = VM(dims, BF)
                scratch.update({f"ss_{p}": DMA((6, most)), f"sr_{p}": DMA((6, most))})
        vm = pl.BlockSpec(memory_space=pltpu.VMEM)
        sm = pl.BlockSpec(memory_space=pltpu.SMEM)
        hbm = pl.BlockSpec(memory_space=pl.ANY)
        rows_first = lambda x: jnp.transpose(x, (1, 0, 2))
        line = lambda x: x.reshape(1, -1)
        ins = dict(
            hid=rows_first(hidden_in), emb=rows_first(embedding), cot=rows_first(cotangent), lengths=lengths, ln1g=line(ln1_gain),
            ln1b=line(ln1_bias), wqkv=qkv_weight, qvb=qv_bias, wout=out_weight, bout=line(out_bias), ln2g=line(ln2_gain),
            ln2b=line(ln2_bias), wup=up_weight, bup=line(up_bias), wdn=down_weight, bdn=line(down_bias))
        shape = jax.ShapeDtypeStruct
        outs = dict(
            y=shape((R, L, D), BF), g1=shape((R, L, D), F32), ge=shape((R, L, D), F32),
            gw=shape((D, W), BF if reduce_here else F32), gv=shape((W // 128, 128), F32))
        scratch.update({n: VM(ins[n].shape, ins[n].dtype) for n in LOADS})
        names = (*(n if n == "lengths" else n + "_in" for n in ins), *outs, *scratch)
        y, g1, ge, gw, gv = pl.pallas_call(
            functools.partial(block_kernel, cfg, names), out_shape=tuple(outs.values()),
            in_specs=[sm if n == "lengths" else hbm for n in ins], out_specs=tuple(vm if n == "gv" else hbm for n in outs),
            scratch_shapes=list(scratch.values()),
            compiler_params=pltpu.CompilerParams(collective_id=0, has_side_effects=True, vmem_limit_bytes=VMEM_LIMIT),
        )(*ins.values())
        if not reduce_here:
            gw, gv = lax.psum((gw, gv), ("dp", "seq"))
        full = [shape((R, L, D), BF), shape((R, L, D), F32), shape((R, L, D), F32), shape((1, D), F32), shape((1, D), F32),
                shape((D, 3 * D), F32), shape((2, D), F32), shape((D, D), F32), shape((1, D), F32), shape((1, D), F32),
                shape((1, D), F32), shape((D, FF), F32), shape((1, FF), F32), shape((FF, D), F32), shape((1, D), F32)]
        ends = ["y_o", "g1_o", "ge_o", "ln1g", "ln1b", "wqkv", "qvb", "wout", "bout", "ln2g", "ln2b", "wup", "bup", "wdn", "bdn"]
        large = ("y_o", "g1_o", "ge_o", "wqkv", "wout", "wup", "wdn")
        temps = dict(
            y_s=VM((R, L, D), BF), g1_s=VM((R, L, D), F32), ge_s=VM((R, L, D), F32), gw_s=VM((D, W), gw.dtype),
            gv_s=VM((W // 128, 128), F32), wup_s=VM((D, FF), F32), wdn_s=VM((FF, D), F32), wqkv_s=VM((D, 3 * D), F32),
            wout_s=VM((D, D), F32), sems=DMA((2, 8)))
        res = pl.pallas_call(
            functools.partial(finish_kernel, D, FF, (*outs, *ends, *temps)), out_shape=full, in_specs=[hbm] * 5,
            out_specs=[hbm if n in large else vm for n in ends], scratch_shapes=list(temps.values()),
            compiler_params=pltpu.CompilerParams(vmem_limit_bytes=VMEM_LIMIT))(y, g1, ge, gw, gv)
        flat = (3, 4, 8, 9, 10, 12, 14)
        return tuple(rows_first(x) if i < 3 else x.reshape(-1) if i in flat else x for i, x in enumerate(res))

    token = P("seq", "dp", None)
    return jax.shard_map(
        shards, mesh=mesh, in_specs=(token, token, P("dp"), token) + (P(),) * 12, out_specs=(token,) * 3 + (P(),) * 12,
        check_vma=False)
```

```python
import functools
import types

import jax
import jax.numpy as jnp
from jax import lax
from jax.experimental import pallas as pl
from jax.experimental.pallas import tpu as pltpu
from jax.sharding import PartitionSpec as P

EPS = 1e-05
MASKED = -1e30
HEADS = 4
HD = 64
BF = jnp.bfloat16
F32 = jnp.float32
MESH = pl.DeviceIdType.MESH
VMEM_LIMIT = 61 * 1024 * 1024


def nn(a, b):
    return lax.dot_general(a, b, (((1,), (0,)), ((), ())), preferred_element_type=F32)


def nt(a, b):
    return lax.dot_general(a, b, (((1,), (1,)), ((), ())), preferred_element_type=F32)


def normalise(x):
    mean = jnp.mean(x, axis=-1, keepdims=True)
    centred = x - mean
    rstd = lax.rsqrt(jnp.mean(centred * centred, axis=-1, keepdims=True) + EPS)
    return centred * rstd, rstd


def norm_back(grad, gain, xhat, rstd):
    gl = grad * gain
    m1 = jnp.mean(gl, axis=-1, keepdims=True)
    m2 = jnp.mean(gl * xhat, axis=-1, keepdims=True)
    return rstd * (gl - m1 - xhat * m2)


def fold(x):
    return jnp.sum(x.reshape(x.shape[0] // 8, 8, x.shape[1]), axis=0)


def gelu_parts(x):
    c0 = 0.7978845608028654
    c1 = c0 * 0.044715
    x2 = x * x
    half = 0.5 + 0.5 * jnp.tanh(x * (c0 + c1 * x2))
    slope = half + (half * (1.0 - half)) * (x * (2 * c0 + (6 * c1) * x2))
    return x * half, slope


def head_rows(x, h):
    own = x[h * HD:(h + 1) * HD]
    zero = jnp.zeros_like(own)
    return jnp.concatenate([own, zero] if h % 2 == 0 else [zero, own], axis=0)


def pair(h):
    return slice((h // 2) * 2 * HD, (h // 2 + 1) * 2 * HD)


def heads_apart(x):
    lane = lax.broadcasted_iota(jnp.int32, x.shape, 1)
    return jnp.concatenate(
        [jnp.where((lane >= h * HD) & (lane < (h + 1) * HD), x, jnp.zeros((), x.dtype)) for h in range(HEADS)], axis=0)


def wide(x, n):
    return jnp.concatenate([x] * (n // 128), axis=1)


class Share:
    def __init__(self, v, start, w, into, stages, whole_last):
        self.v, self.stages, self.whole = v, stages, whole_last
        self.bufs, self.send, self.recv = into
        self.down = len(stages)
        self.steps = 2 * self.down - (1 if whole_last else 0)
        self.plan = share_plan(v.D, w, [n for n, _, _ in stages], whole_last)
        base = (0, start)
        self.bases = [base]
        for k, (n, own, _) in enumerate(stages):
            base = self.part(k, own)[0]
            self.bases.append(base)

    def part(self, k, number):
        rows, lanes, row_parts, _ = self.plan[k]
        r, c = self.bases[k]
        if row_parts == 1:
            return (r, c + number * lanes), (rows, lanes)
        return (r + lax.rem(number, row_parts) * rows, c + lax.div(number, row_parts) * lanes), (rows, lanes)

    def window(self, base, size):
        r, c = base
        at = c if isinstance(c, int) else pl.multiple_of(c, 128)
        return pl.ds(pl.multiple_of(r, 16) if not isinstance(r, int) else r, size[0]), pl.ds(at, size[1])

    def region(self, k):
        rows, lanes, row_parts, lane_parts = self.plan[k]
        return self.window(self.bases[k], (rows * row_parts, lanes * lane_parts))

    def copies(self, i):
        v = self.v
        k = i if i < self.down else 2 * self.down - 1 - i - (1 if self.whole else 0)
        n, own, device = self.stages[k]
        out = []
        for j in range(1, n):
            other = lax.rem(own + j, n)
            if i == self.down - 1 and self.whole:
                out.append((v.stage.at[self.region(k)], self.bufs[k].at[own], device(other)))
            elif i < self.down:
                out.append((v.stage.at[self.window(*self.part(k, other))], self.bufs[k].at[j - 1], device(other)))
            else:
                ref = v.gath.at[self.window(*self.part(k, own))]
                out.append((ref, ref, device(other)))
        return out

    def made(self, i):
        return [pltpu.make_async_remote_copy(src_ref=s, dst_ref=d, send_sem=self.send.at[i, j], recv_sem=self.recv.at[i, j],
                                             device_id=dev, device_id_type=MESH)
                for j, (s, d, dev) in enumerate(self.copies(i))]

    def start(self, i):
        v = self.v
        if i == 0:
            n, own, _ = self.stages[0]
            for j in range(1, n):
                there = self.window(*self.part(0, lax.rem(own + j, n)))
                v.stage[there] = v.dW[there].astype(BF)
        for c in self.made(i):
            c.start()

    def finish(self, i):
        v = self.v
        for c in self.made(i):
            c.wait()
        if i >= self.down:
            return
        n, own, _ = self.stages[i]
        if i == self.down - 1 and self.whole:
            at = self.region(i)
            self.bufs[i][own] = v.stage[at]
            total = self.bufs[i][0].astype(F32)
            for j in range(1, n):
                total = total + self.bufs[i][j].astype(F32)
        else:
            at = self.window(*self.part(i, own))
            total = v.dW[at]
            for j in range(n - 1):
                total = total + self.bufs[i][j].astype(F32)
        if i == self.down - 1:
            v.gath[at] = total.astype(BF)
        else:
            v.dW[at] = total
            v.stage[at] = total.astype(BF)

    def step(self, i):
        self.finish(i)
        if i + 1 < self.steps:
            self.start(i + 1)


def share_plan(D, w, members, whole_last):
    rows, lanes, plan = D, w, []
    for k, n in enumerate(members):
        if whole_last and k == len(members) - 1:
            plan.append((rows, lanes, 1, 1))
            continue
        row_parts = max(p for p in range(1, n + 1) if n % p == 0 and rows % (16 * p) == 0)
        lane_parts = n // row_parts
        if lanes % (128 * lane_parts):
            return None
        rows, lanes = rows // row_parts, lanes // lane_parts
        plan.append((rows, lanes, row_parts, lane_parts))
    return plan


def part_shapes(D, w, members, whole_last):
    shapes = []
    for k, (n, (rows, lanes, rp, lp)) in enumerate(zip(members, share_plan(D, w, members, whole_last))):
        whole = whole_last and k == len(members) - 1
        shapes.append((n if whole else n - 1, rows, lanes))
    return shapes


class SmallSum:
    def __init__(self, v):
        self.v = v
        self.stages = [(v.vs1, v.core, 2, lambda other: v.sibling, v.vss1, v.vsr1),
                       (v.vs2, v.spot2, v.S, v.in_plane, v.vss2, v.vsr2), (v.vs3, v.spot3, v.DP // 2, v.across, v.vss3, v.vsr3)]

    def copies(self, i):
        buf, spot, n, device, send, recv = self.stages[i]
        return [pltpu.make_async_remote_copy(
            src_ref=buf.at[spot], dst_ref=buf.at[spot], send_sem=send.at[k - 1], recv_sem=recv.at[k - 1],
            device_id=device(lax.rem(spot + k, n)), device_id_type=MESH) for k in range(1, n)]

    def start(self, i, value):
        buf, spot = self.stages[i][:2]
        buf[spot] = value
        for c in self.copies(i):
            c.start()

    def finish(self, i):
        for c in self.copies(i):
            c.wait()
        buf, n = self.stages[i][0], self.stages[i][2]
        total = buf[0]
        for s in range(1, n):
            total = total + buf[s]
        return total


def out_copy(v, which, src, dst, r):
    return pltpu.make_async_copy(src.at[r], dst.at[r], v.out_sems.at[which, r])


LOADS = ("hid", "emb", "ln1g", "ln1b", "wqkv", "qvb", "wup", "wdn", "wout", "bout", "ln2g", "ln2b", "bup", "bdn", "cot")


def block_kernel(cfg, names, *refs):
    S, DP, R, L, D, FF, reduce_here = cfg
    W = 4 * D + 2 * FF
    v = types.SimpleNamespace(**dict(zip(names, refs, strict=True)))
    v.S, v.DP, v.R, v.L, v.D, v.FF, v.W, v.reduce_here = S, DP, R, L, D, FF, W, reduce_here
    v.me, v.dp = me, dp = lax.axis_index("seq"), lax.axis_index("dp")
    v.chip, v.core = chip, core = lax.div(me, 2), lax.rem(me, 2)
    X = v.X = S // 2
    v.mine = mine = pl.ds(pl.multiple_of(me * L, L), L)
    v.sibling = (dp, me + 1 - 2 * core)
    sizes = (S // 2, S)

    def with_size(body):
        low = 0
        for n in sizes:
            pl.when((me >= low) & (me < n))(functools.partial(body, n))
            low = n

    barrier = pltpu.get_barrier_semaphore()
    Z = DP // 2
    x_peers = [(dp, lax.rem(me + 2 * k, S)) for k in range(1, X)]
    peers, count = [v.sibling] + x_peers, X
    if reduce_here:
        v.spot2, v.spot3 = chip * 2 + lax.rem(dp, 2), lax.div(dp, 2)
        v.in_plane = lambda n: (lax.div(dp, 2) * 2 + lax.rem(n, 2), lax.div(n, 2) * 2 + core)
        v.across = lambda n: (n * 2 + lax.rem(dp, 2), me)
        z = v.spot3
        peers.append((dp + 1 - 2 * lax.rem(dp, 2), me))
        count = count + 1 + jnp.where(z > 0, 1, 0) + jnp.where(z < Z - 1, 1, 0)
    for peer in peers:
        pl.semaphore_signal(barrier, inc=1, device_id=peer, device_id_type=MESH)
    if reduce_here:
        for there, step in ((z < Z - 1, 1), (z > 0, -1)):
            @pl.when(there)
            def _():
                pl.semaphore_signal(barrier, inc=1, device_id=v.across(z + step), device_id_type=MESH)

    def tell(which, peer):
        pl.semaphore_signal(v.relay.at[which], inc=1, device_id=peer, device_id_type=MESH)

    def first_word():
        for peer in x_peers:
            tell(0, peer)

        @pl.when((z > 0) & (z < Z - 1))
        def _():
            tell(1, v.across(z + 1))
            tell(2, v.across(z - 1))

    def passed_on():
        pl.semaphore_wait(v.relay.at[0], X - 1)
        pl.when(z >= 2)(lambda: pl.semaphore_wait(v.relay.at[1], 1))
        pl.when(z <= Z - 3)(lambda: pl.semaphore_wait(v.relay.at[2], 1))
        pl.when((z >= 2) & (z < Z - 1))(lambda: tell(3, v.across(z + 1)))
        pl.when((z <= Z - 3) & (z > 0))(lambda: tell(4, v.across(z - 1)))
        pl.when(z >= 3)(lambda: pl.semaphore_wait(v.relay.at[3], 1))
        pl.when(z <= Z - 4)(lambda: pl.semaphore_wait(v.relay.at[4], 1))

    brought = {}
    for k, name in enumerate(LOADS):
        brought[name] = pltpu.make_async_copy(getattr(v, name + "_in"), getattr(v, name), v.in_sem.at[k])
        brought[name].start()

    def need(*which):
        for name in which:
            brought.pop(name).wait()

    v.need = need

    def block_of(a, r, t):
        return v.nall.at[a, r, pl.ds(pl.multiple_of(t * L, L), L)]

    def normed_copy(a, r, t, send_sem, dst):
        ref = block_of(a, r, t)
        return pltpu.make_async_remote_copy(
            src_ref=ref, dst_ref=ref, send_sem=send_sem, recv_sem=v.nrecv.at[a, r, t], device_id=(dp, dst), device_id_type=MESH)

    def to_chip(a, r, c):
        return normed_copy(a, r, me, v.nsend.at[a, r, c], 2 * c + core)

    def to_sibling(a, r):
        return normed_copy(a, r, me, v.nsend.at[a, r, X], me + 1 - 2 * core)

    def handed_on(a, r, c):
        return normed_copy(a, r, 2 * c + core, v.fsend.at[a, r, c], me + 1 - 2 * core)

    def each_send(a, r, action):
        @pl.loop(chip + 1, X)
        def _(c):
            action(to_chip(a, r, c))

        @pl.when(core == 0)
        def _():
            action(to_sibling(a, r))

    def first_norm(a, r):
        u = v.stream[r] + v.emb[r].astype(F32)
        v.stream[r] = u
        xhat, rstd = normalise(u)
        v.xh1[a, r] = xhat
        v.rs1[a, r] = jnp.broadcast_to(rstd, (L, 128))
        v.nall[a, r, mine] = (xhat * ln1g + ln1b).astype(BF)

    def announce(a, r):
        each_send(a, r, lambda c: c.start())

    def hand_on(a, r):
        @pl.loop(0, chip)
        def _(c):
            handed_on(a, r, c).wait_recv()
            handed_on(a, r, c).start()

    def gathered(a, r):
        @pl.loop(0, chip)
        def _(c):
            normed_copy(a, r, 2 * c + 1 - core, v.fsend.at[a, r, c], me).wait_recv()

        @pl.when(core == 1)
        def _():
            normed_copy(a, r, me - 1, v.nsend.at[a, r, X], me).wait_recv()

    need("hid", "emb", "ln1g", "ln1b")
    ln1g, ln1b = v.ln1g[...], v.ln1b[...]

    def first_input(r):
        v.stream[r] = v.hid[r].astype(F32)
        first_norm(0, r)

    first_input(0)
    @pl.loop(me + 1, S)
    def _(t):
        for a in range(2):
            for r in range(R):
                v.nall[a, r, pl.ds(pl.multiple_of(t * L, L), L)] = jnp.zeros((L, D), BF)

    v.vec[...] = jnp.zeros_like(v.vec)
    pl.semaphore_wait(barrier, count)
    announce(0, 0)

    @pl.loop(1, R)
    def _(r):
        first_input(r)
        announce(0, r)

    if reduce_here:
        first_word()
    need("wqkv", "qvb")
    for k in range(3):
        v.wT[k * D:(k + 1) * D] = v.wqkv[:, k * D:(k + 1) * D].T
    for k in range(2):
        v.bcol[k] = jnp.broadcast_to(v.qvb[k:k + 1, :], (128, D)).T
    need("wup", "wdn")
    for k in range(FF // D):
        ks = slice(k * D, (k + 1) * D)
        v.wupT[ks] = v.wup[:, ks].T
        v.wdnT[:, ks] = v.wdn[ks].T

    need("wout", "bout", "ln2g", "ln2b", "bup", "bdn", "cot")
    ln2g, ln2b = v.ln2g[...], v.ln2b[...]

    def forward_attention(a, r, bias, s_scr, qT_s, nb):
        KB = nb * L
        rows = v.nall[a, r, 0:KB, :]
        keys = nn(rows, v.wqkv[:, D:2 * D]).astype(BF)
        qT = qT_s[r]
        tops = []
        for h in range(HEADS):
            s = nn(keys[:, pair(h)], head_rows(qT, h)) + bias[r, 0:KB]
            s_scr[0:KB, h * L:(h + 1) * L] = s
            tops.append(jnp.max(jnp.max(s.reshape(KB // 8, 8, L), axis=0), axis=0, keepdims=True))
        VT = (nt(v.wT[2 * D:], rows) + wide(v.bcol[1], KB)).astype(BF)
        for h in range(HEADS):
            hs, hl = slice(h * HD, (h + 1) * HD), slice(h * L, (h + 1) * L)
            sums, out = [], []
            for t in range(nb):
                ts = slice(t * L, (t + 1) * L)
                e = jnp.exp(s_scr[ts, hl] - tops[h])
                sums.append(fold(e))
                low = e.astype(BF)
                v.e_scr[a, r, ts, hl] = low
                out.append(nn(VT[hs, ts], low))
            inv = 1.0 / jnp.sum(sum(sums), axis=0, keepdims=True)
            v.linv[a, r, h] = jnp.broadcast_to(inv, (8, L))
            v.oT[a, r, hs] = (sum(out) * inv).astype(BF)

    def forward_all(bias, s_scr, qT_s):
        def queries(a, r):
            normed = v.nall[a, r, mine]
            qT = ((nt(v.wT[:D], normed) + wide(v.bcol[0], L)) * (HD ** -0.5)).astype(BF)
            v.qn[a, r] = qT.T
            qT_s[r] = qT

        @pl.loop(0, R)
        def _(r):
            queries(0, r)
            length = v.lengths[r]
            for t in range(S):
                key_pos = t * L + lax.broadcasted_iota(jnp.int32, (L, L), 0)
                query_pos = me * L + lax.broadcasted_iota(jnp.int32, (L, L), 1)
                bias[r, t * L:(t + 1) * L] = jnp.where((key_pos <= query_pos) & (key_pos < length), 0.0, MASKED)

        hand_on(0, 0)

        @pl.loop(0, 2 * R)
        def _(n):
            a, r = lax.div(n, R), lax.rem(n, R)
            gathered(a, r)
            with_size(functools.partial(forward_attention, a, r, bias, s_scr, qT_s))

            @pl.when(n < 2 * R - 1)
            def _():
                hand_on(lax.div(n + 1, R), lax.rem(n + 1, R))

            middle = v.stream[r] + (nn(v.oT[a, r].T, v.wout[...]) + v.bout[...])
            xhat, rstd = normalise(middle)
            v.xh2[a, r] = xhat
            v.rs2[a, r] = jnp.broadcast_to(rstd, (L, 128))
            normed2 = (xhat * ln2g + ln2b).astype(BF)
            v.n2T[a, r] = normed2.T
            hidden, slope = gelu_parts(nn(normed2, v.wup[...]) + v.bup[...])
            hidden = hidden.astype(BF)
            v.hidden[a, r] = hidden
            v.slope[a, r] = slope
            v.stream[r] = middle + (nn(hidden, v.wdn[...]) + v.bdn[...])

            @pl.when(a == 0)
            def _():
                first_norm(1, r)
                announce(1, r)
                queries(1, r)

            @pl.when(a == 1)
            def _():
                v.hid[r] = v.stream[r].astype(BF)
                v.gstream[r] = v.cot[r].astype(F32)
                out_copy(v, 0, v.hid, v.y, r).start()

    VM = pltpu.VMEM
    if reduce_here:
        v.passed_on = passed_on
    pl.run_scoped(forward_all, VM((R, S * L, L), F32), VM((S * L, HEADS * L), F32), VM((R, D, L), BF))
    pl.run_scoped(functools.partial(backward, v, with_size), VM((R, D, L), BF), VM((R, L, FF), BF), VM((R, L, D), BF),
                  VM((R, L, 3 * D), BF), VM((D, W), F32), VM((L, D), F32),
                  VM((S * L, D), BF), VM((S * L, 2 * D), BF))

    for a in range(2):
        for r in range(R):
            each_send(a, r, lambda c: c.wait_send())

            @pl.loop(0, chip)
            def _(c):
                handed_on(a, r, c).wait_send()


def backward(v, with_size, gbT, gpre, ga_s, gqkv, dW, gns, pg_s, gkv_s):
    S, DP, R, L, D, FF, W = v.S, v.DP, v.R, v.L, v.D, v.FF, v.W
    me, dp, mine = v.me, v.dp, v.mine
    v.dW = dW
    ln1g, ln2g = v.ln1g[...], v.ln2g[...]
    UP, DN, OW, QW = 0, FF, 2 * FF, 2 * FF + D
    V_LN1G, V_LN1B, V_QB, V_VB, V_OB, V_LN2G, V_LN2B, V_DB, V_UB = [D * k for k in range(9)]

    X, chip, core = v.X, v.chip, v.core

    def pair_copy(a, r, c):
        return pltpu.make_async_remote_copy(
            src_ref=v.pair_out.at[r, c], dst_ref=v.pair_in.at[a, r, c], send_sem=v.psend.at[0, a, r, c],
            recv_sem=v.precv.at[0, a, r, c], device_id=v.sibling, device_id_type=MESH)

    def part_copy(a, r, src, dst):
        return pltpu.make_async_remote_copy(
            src_ref=v.part_out.at[r, dst], dst_ref=v.part_in.at[a, r, src - 1], send_sem=v.psend.at[1, a, r, dst],
            recv_sem=v.precv.at[1, a, r, src], device_id=(dp, 2 * dst + core), device_id_type=MESH)

    def near_copy(a, r):
        return pltpu.make_async_remote_copy(
            src_ref=v.near_out.at[r], dst_ref=v.near_in.at[a, r], send_sem=v.nearsem.at[0, a, r],
            recv_sem=v.nearsem.at[1, a, r], device_id=v.sibling, device_id_type=MESH)

    def pass_on(a, r):
        @pl.loop(0, chip)
        def _(c):
            pair_copy(a, r, c).wait_recv()
            v.part_out[r, c] = (v.keep[r, c].astype(F32) + v.pair_in[a, r, c].astype(F32)).astype(BF)
            part_copy(a, r, chip, c).start()

    def sent(a):
        for r in range(R):
            @pl.loop(0, chip)
            def _(c):
                pair_copy(a, r, c).wait_send()
                part_copy(a, r, chip, c).wait_send()

            @pl.when(core == 1)
            def _():
                near_copy(a, r).wait_send()

    def add_vec(start, terms):
        v.vec[:, start:start + terms.shape[1]] += fold(terms)

    def backward_mlp(a, r):
        g = v.gstream[r]
        gb = g.astype(BF)
        add_vec(V_DB, gb.astype(F32))
        gbT[r] = gb.T
        pre = (nn(gb, v.wdnT[...]) * v.slope[a, r]).astype(BF)
        gpre[r] = pre
        add_vec(V_UB, pre.astype(F32))
        gn2 = nn(pre, v.wupT[...])
        xhat = v.xh2[a, r]
        add_vec(V_LN2G, gn2 * xhat)
        add_vec(V_LN2B, gn2)
        gm = g + norm_back(gn2, ln2g, xhat, wide(v.rs2[a, r], D))
        v.gmid[r] = gm
        ga = gm.astype(BF)
        ga_s[r] = ga
        add_vec(V_OB, ga.astype(F32))

    def attention_core(a, r, tick, nb):
        KB = nb * L
        gaT = nt(v.wout[...], ga_s[r]).astype(BF).astype(F32)
        oT = v.oT[a, r].astype(F32)
        scaled, deltas = [], []
        for h in range(HEADS):
            hs = slice(h * HD, (h + 1) * HD)
            part = gaT[hs] * v.linv[a, r, h, 0:1]
            scaled.append(part.astype(BF))
            deltas.append(jnp.sum(part * oT[hs], axis=0, keepdims=True))
        gaT_n = jnp.concatenate(scaled, axis=0)
        rows = v.nall[a, r, 0:KB, :]
        values = (nn(rows, v.wqkv[:, 2 * D:]) + v.qvb[1:2, :]).astype(BF)
        KT = nt(v.wT[D:2 * D], rows).astype(BF)
        blocks = [slice(t * L, (t + 1) * L) for t in range(nb)]
        ga_apart, q_apart = heads_apart(gaT_n.T), heads_apart(v.qn[a, r])
        for ts in blocks:
            gkv_s[ts, D:] = nn(v.e_scr[a, r, ts, :], ga_apart).astype(BF)
        for h in range(HEADS):
            hl = slice(h * L, (h + 1) * L)
            gp = nn(values[:, pair(h)], head_rows(gaT_n, h))
            v.e_scr[a, r, 0:KB, hl] = (v.e_scr[a, r, 0:KB, hl].astype(F32) * (gp - deltas[h])).astype(BF)
        tick()
        for ts in blocks:
            gkv_s[ts, :D] = nn(v.e_scr[a, r, ts, :], q_apart).astype(BF)
        for ts in blocks:
            pg_s[ts] = nn(gkv_s[ts, :], v.wT[D:]).astype(BF)
        for t in range(nb):
            ts = blocks[t]
            if t // 2 < nb // 2 - 1:
                @pl.when((t // 2 < chip) & (t % 2 == core))
                def _():
                    v.keep[r, t // 2] = pg_s[ts]

                @pl.when((t // 2 < chip) & (t % 2 != core))
                def _():
                    v.pair_out[r, t // 2] = pg_s[ts]
                    pair_copy(a, r, t // 2).start()

            if t % 2 == 0:
                @pl.when(t == me - 1)
                def _():
                    v.near_out[r] = pg_s[ts]
                    near_copy(a, r).start()

            @pl.when(t == me)
            def _():
                gqkv[r, :, D:] = gkv_s[ts]

        add_vec(V_VB, gkv_s[0:KB, D:].astype(F32))
        gqT = jnp.concatenate([nn(KT[h * HD:(h + 1) * HD], v.e_scr[a, r, 0:KB, h * L:(h + 1) * L]) for h in range(HEADS)], axis=0)
        dW[:, QW + D:QW + 3 * D] += nn(rows.T, gkv_s[0:KB])
        gq = (gqT * (HD ** -0.5)).T.astype(BF)
        gqkv[r, :, :D] = gq
        add_vec(V_QB, gq.astype(F32))

    def backward_norm(a, r):
        gns[...] = nn(gqkv[r], v.wT[...])

        @pl.when(core == 0)
        def _():
            near_copy(a, r).wait_recv()
            gns[...] += v.near_in[a, r].astype(F32)

        @pl.loop(chip + 1, X)
        def _(c):
            part_copy(a, r, c, chip).wait_recv()
            gns[...] += v.part_in[a, r, c - 1].astype(F32)

        gn = gns[...]
        xhat = v.xh1[a, r]
        add_vec(V_LN1G, gn * xhat)
        add_vec(V_LN1B, gn)
        v.gstream[r] = v.gmid[r] + norm_back(gn, ln1g, xhat, wide(v.rs1[a, r], D))

    def put(first, start, value):
        if first:
            dW[:, start:start + value.shape[1]] = value
        else:
            dW[:, start:start + value.shape[1]] += value

    def weight_terms(a, rows, which):
        first = a == 1 and rows[0] == 0
        if "up" in which:
            put(first, UP, sum(nn(v.n2T[a, r], gpre[r]) for r in rows))
        if "down" in which:
            put(first, DN, sum(nn(gbT[r], v.hidden[a, r]) for r in rows))
            put(first, OW, sum(nn(v.oT[a, r], ga_s[r]) for r in rows))

    def query_terms(a):
        put(a == 1, QW, sum(nn(v.nall[a, r, mine].T, gqkv[r, :, :D]) for r in range(R)))

    every, early, last = tuple(range(R)), tuple(range(R - 1)), (R - 1,)
    dW[:, QW + D:QW + 3 * D] = jnp.zeros((D, 2 * D), F32)
    reducing = v.reduce_here
    if reducing:
        pair_stage = (2, core, lambda n: v.sibling)
        plane, across = (S, v.spot2, v.in_plane), (DP // 2, v.spot3, v.across)
        into = lambda p: ([getattr(v, f"b{k}_{p}") for k in range(3)], getattr(v, f"ss_{p}"), getattr(v, f"sr_{p}"))
        up, down, qkv = (Share(v, start, w, into(p), (pair_stage, plane, across), whole)
                         for p, (start, w, whole) in enumerate(((UP, FF, False), (DN, FF + D, False), (QW, 3 * D, True))))
        small = SmallSum(v)
        v.passed_on()

    def nothing():
        pass

    def attention(a, r, tick):
        with_size(functools.partial(attention_core, a, r, tick))

    for r in range(R):
        backward_mlp(1, r)

    weight_terms(1, every, ("up", "down"))

    @pl.loop(0, R)
    def _(r):
        attention(1, r, lambda: pl.when(r > 0)(lambda: pass_on(1, r - 1)))

    pass_on(1, R - 1)
    query_terms(1)

    def between(r):
        backward_norm(1, r)
        v.stream[r] = v.gstream[r]
        backward_mlp(0, r)

    for r in range(R - 1):
        between(r)
    if early:
        weight_terms(0, early, ("up", "down"))
    between(R - 1)
    weight_terms(0, last, ("up",))
    if reducing:
        up.start(0)
    weight_terms(0, last, ("down",))
    if reducing:
        down.start(0)

    sent(1)

    def tick_first():
        if reducing:
            up.step(0)
            down.step(0)

    def tick_last():
        if reducing:
            up.step(1)

    for r in range(R):
        attention(0, r, tick_first if r == 0 else tick_last if r == R - 1 else nothing)
        if r > 0:
            pass_on(0, r - 1)
    query_terms(0)
    if reducing:
        qkv.start(0)
    pass_on(0, R - 1)
    if reducing:
        down.step(1)

    def final(r):
        backward_norm(0, r)
        v.gmid[r] = v.gstream[r] + v.stream[r]
        out_copy(v, 1, v.gstream, v.g1, r).start()
        out_copy(v, 2, v.gmid, v.ge, r).start()

    def small_lines():
        sums = jnp.sum(v.vec[...], axis=0, keepdims=True)
        return jnp.concatenate([sums[:, k * 128:(k + 1) * 128] for k in range(W // 128)], axis=0)

    if reducing:
        gath_copy = lambda k, cols: pltpu.make_async_copy(v.gath.at[:, cols], v.gw.at[:, cols], v.gw_sem.at[k])
        first_out, second_out = gath_copy(0, slice(0, QW)), gath_copy(1, slice(QW, W))
        qkv.step(0)
        for r in range(R - 1):
            final(r)
        up.step(2)
        qkv.step(1)
        down.step(2)
        up.step(3)
        final(R - 1)
        small.start(0, small_lines())
        small.start(1, small.finish(0))
        qkv.step(2)
        down.step(3)
        small.start(2, small.finish(1))
        up.step(4)
        qkv.step(3)
        down.step(4)
        v.gv[...] = small.finish(2)
        up.finish(5)
        down.finish(5)
        first_out.start()
        qkv.finish(4)
        second_out.start()
        first_out.wait()
        second_out.wait()
    else:
        pl.loop(0, R)(final)
        out = pltpu.make_async_copy(v.gath if v.reduce_here else dW, v.gw, v.gw_sem.at[0])
        out.start()
        out.wait()
        v.gv[...] = small_lines()

    for r in range(R):
        out_copy(v, 0, v.hid, v.y, r).wait()
        out_copy(v, 1, v.gstream, v.g1, r).wait()
        out_copy(v, 2, v.gmid, v.ge, r).wait()
    sent(0)


def finish_kernel(D, FF, names, *refs):
    v = types.SimpleNamespace(**dict(zip(names, refs, strict=True)))
    load = lambda i, src, dst: pltpu.make_async_copy(src, dst, v.sems.at[0, i])
    save = lambda i, src, dst: pltpu.make_async_copy(src, dst, v.sems.at[1, i])
    cols = (slice(FF, 2 * FF), slice(0, FF), slice(2 * FF + D, 2 * FF + 4 * D), slice(2 * FF, 2 * FF + D))
    loads = [load(i, v.gw.at[:, c], v.gw_s.at[:, c]) for i, c in enumerate(cols)]
    loads += [load(4, v.g1, v.g1_s), load(5, v.ge, v.ge_s), load(6, v.y, v.y_s), load(7, v.gv, v.gv_s)]
    for c in loads:
        c.start()
    saves = []

    def keep(src, dst):
        saves.append(save(len(saves), src, dst))
        saves[-1].start()

    for i, (c, src, dst) in enumerate(zip(cols, (v.wdn_s, v.wup_s, v.wqkv_s, v.wout_s), (v.wdn, v.wup, v.wqkv, v.wout))):
        loads[i].wait()
        part = v.gw_s[:, c]
        src[...] = (part.T if i == 0 else part).astype(F32)
        keep(src, dst)
    for c, src, dst in zip(loads[4:7], (v.g1_s, v.ge_s, v.y_s), (v.g1_o, v.ge_o, v.y_o)):
        c.wait()
        keep(src, dst)
    loads[7].wait()
    n = D // 128
    at = 0
    for ref, size in ((v.ln1g, n), (v.ln1b, n), (v.qvb, 2 * n), (v.bout, n), (v.ln2g, n), (v.ln2b, n), (v.bdn, n),
                      (v.bup, FF // 128)):
        for k in range(size):
            row, col = divmod(k, ref.shape[1] // 128)
            ref[row:row + 1, col * 128:(col + 1) * 128] = v.gv_s[at + k:at + k + 1, :]
        at += size
    for c in saves:
        c.wait()


def solution(mesh):
    S, DP = mesh.shape["seq"], mesh.shape["dp"]

    def shards(hidden_in, embedding, lengths, cotangent, ln1_gain, ln1_bias, qkv_weight, qv_bias, out_weight, out_bias,
               ln2_gain, ln2_bias, up_weight, up_bias, down_weight, down_bias):
        L, R, D = hidden_in.shape
        FF = up_weight.shape[1]
        W = 4 * D + 2 * FF
        X, Z = S // 2, DP // 2
        parts = (FF, FF + D, 3 * D)
        members, wholes = (2, S, Z), (False, False, True)
        reduce_here = DP % 2 == 0 and 1 < Z <= 4 and all(share_plan(D, w, members, f) for w, f in zip(parts, wholes))
        cfg = (S, DP, R, L, D, FF, reduce_here)
        VM = pltpu.VMEM
        DMA = pltpu.SemaphoreType.DMA
        scratch = dict(
            wT=VM((3 * D, D), BF), wupT=VM((FF, D), BF), wdnT=VM((D, FF), BF), bcol=VM((2, D, 128), F32),
            stream=VM((R, L, D), F32), gstream=VM((R, L, D), F32), gmid=VM((R, L, D), F32), nall=VM((2, R, S * L, D), BF), xh1=VM((2, R, L, D), F32), rs1=VM((2, R, L, 128), F32),
            xh2=VM((2, R, L, D), F32), rs2=VM((2, R, L, 128), F32), n2T=VM((2, R, D, L), BF),
            qn=VM((2, R, L, D), BF), linv=VM((2, R, HEADS, 8, L), F32), oT=VM((2, R, D, L), BF),
            hidden=VM((2, R, L, FF), BF), slope=VM((2, R, L, FF), F32), e_scr=VM((2, R, S * L, HEADS * L), BF),
            pair_out=VM((R, X - 1, L, D), BF), pair_in=VM((2, R, X - 1, L, D), BF), part_out=VM((R, X - 1, L, D), BF),
            part_in=VM((2, R, X - 1, L, D), BF), near_out=VM((R, L, D), BF), near_in=VM((2, R, L, D), BF),
            keep=VM((R, X - 1, L, D), BF), vec=VM((8, W), F32),
            nsend=DMA((2, R, X + 1)), fsend=DMA((2, R, X)), nrecv=DMA((2, R, S)), psend=DMA((2, 2, R, X)), precv=DMA((2, 2, R, X)),
            nearsem=DMA((2, 2, R)), out_sems=DMA((3, R)), gw_sem=DMA((2,)), in_sem=DMA((len(LOADS),)))
        if reduce_here:
            lines = W // 128
            scratch.update(
                stage=VM((D, W), BF), gath=VM((D, W), BF), vs1=VM((2, lines, 128), F32), vs2=VM((S, lines, 128), F32),
                vs3=VM((Z, lines, 128), F32), vss1=DMA((1,)), vsr1=DMA((1,)), vss2=DMA((S - 1,)), vsr2=DMA((S - 1,)),
                vss3=DMA((Z - 1,)), vsr3=DMA((Z - 1,)), relay=pltpu.SemaphoreType.REGULAR((5,)))
            most = max(S, Z) - 1
            for p, (w, f) in enumerate(zip(parts, wholes)):
                for k, dims in enumerate(part_shapes(D, w, members, f)):
                    scratch[f"b{k}_{p}"] = VM(dims, BF)
                scratch.update({f"ss_{p}": DMA((6, most)), f"sr_{p}": DMA((6, most))})
        vm = pl.BlockSpec(memory_space=pltpu.VMEM)
        sm = pl.BlockSpec(memory_space=pltpu.SMEM)
        hbm = pl.BlockSpec(memory_space=pl.ANY)
        rows_first = lambda x: jnp.transpose(x, (1, 0, 2))
        line = lambda x: x.reshape(1, -1)
        ins = dict(
            hid=rows_first(hidden_in), emb=rows_first(embedding), cot=rows_first(cotangent), lengths=lengths, ln1g=line(ln1_gain),
            ln1b=line(ln1_bias), wqkv=qkv_weight, qvb=qv_bias, wout=out_weight, bout=line(out_bias), ln2g=line(ln2_gain),
            ln2b=line(ln2_bias), wup=up_weight, bup=line(up_bias), wdn=down_weight, bdn=line(down_bias))
        shape = jax.ShapeDtypeStruct
        outs = dict(
            y=shape((R, L, D), BF), g1=shape((R, L, D), F32), ge=shape((R, L, D), F32),
            gw=shape((D, W), BF if reduce_here else F32), gv=shape((W // 128, 128), F32))
        scratch.update({n: VM(ins[n].shape, ins[n].dtype) for n in LOADS})
        names = (*(n if n == "lengths" else n + "_in" for n in ins), *outs, *scratch)
        y, g1, ge, gw, gv = pl.pallas_call(
            functools.partial(block_kernel, cfg, names), out_shape=tuple(outs.values()),
            in_specs=[sm if n == "lengths" else hbm for n in ins], out_specs=tuple(vm if n == "gv" else hbm for n in outs),
            scratch_shapes=list(scratch.values()),
            compiler_params=pltpu.CompilerParams(collective_id=0, has_side_effects=True, vmem_limit_bytes=VMEM_LIMIT),
        )(*ins.values())
        if not reduce_here:
            gw, gv = lax.psum((gw, gv), ("dp", "seq"))
        full = [shape((R, L, D), BF), shape((R, L, D), F32), shape((R, L, D), F32), shape((1, D), F32), shape((1, D), F32),
                shape((D, 3 * D), F32), shape((2, D), F32), shape((D, D), F32), shape((1, D), F32), shape((1, D), F32),
                shape((1, D), F32), shape((D, FF), F32), shape((1, FF), F32), shape((FF, D), F32), shape((1, D), F32)]
        ends = ["y_o", "g1_o", "ge_o", "ln1g", "ln1b", "wqkv", "qvb", "wout", "bout", "ln2g", "ln2b", "wup", "bup", "wdn", "bdn"]
        large = ("y_o", "g1_o", "ge_o", "wqkv", "wout", "wup", "wdn")
        temps = dict(
            y_s=VM((R, L, D), BF), g1_s=VM((R, L, D), F32), ge_s=VM((R, L, D), F32), gw_s=VM((D, W), gw.dtype),
            gv_s=VM((W // 128, 128), F32), wup_s=VM((D, FF), F32), wdn_s=VM((FF, D), F32), wqkv_s=VM((D, 3 * D), F32),
            wout_s=VM((D, D), F32), sems=DMA((2, 8)))
        res = pl.pallas_call(
            functools.partial(finish_kernel, D, FF, (*outs, *ends, *temps)), out_shape=full, in_specs=[hbm] * 5,
            out_specs=[hbm if n in large else vm for n in ends], scratch_shapes=list(temps.values()),
            compiler_params=pltpu.CompilerParams(vmem_limit_bytes=VMEM_LIMIT))(y, g1, ge, gw, gv)
        flat = (3, 4, 8, 9, 10, 12, 14)
        return tuple(rows_first(x) if i < 3 else x.reshape(-1) if i in flat else x for i, x in enumerate(res))

    token = P("seq", "dp", None)
    return jax.shard_map(
        shards, mesh=mesh, in_specs=(token, token, P("dp"), token) + (P(),) * 12, out_specs=(token,) * 3 + (P(),) * 12,
        check_vma=False)
```
